256 devices in a mesh: gauss: 64 (over z, x, core), view: 4 (over y).
Axes of the slice: x: 4, y: 4, z: 8, core: 2. Of those that a mesh axis runs over, the one named last changes fastest.
Arguments:
- params: float32 [59, 65536], P(None, 'gauss'), as said below
- first_moment: float32 [59, 65536], P(None, 'gauss'), may hold values from -6 to 6
- second_moment: float32 [59, 65536], P(None, 'gauss'), may hold values from 0.0001 to 1
- cameras: float32 [4, 16], P('view'), as said below
- target: float32 [4, 256, 3, 256], P('view', 'gauss'), may hold values from 0 to 1
- tile_index: int32 [4, 256], P('view', 'gauss'), may hold values from 0 to 255, as said below
- tile_lists: int32 [4, 256, 256], P('view', 'gauss'), may hold values from -1 to 1023, as said below
- send_slots: int32 [4, 64, 1024], P('view', 'gauss'), may hold values from 0 to 1023, as said below
- reloc_send: int32 [64, 128], P('gauss'), may hold values from -1 to 1023, as said below
- reloc_recv: int32 [64, 128], P('gauss'), may hold values from -1 to 1023, as said below
Outputs:
- new_params: float32 [59, 65536], P(None, 'gauss')
- new_first: float32 [59, 65536], P(None, 'gauss')
- new_second: float32 [59, 65536], P(None, 'gauss')
- gradient: float32 [59, 65536], P(None, 'gauss')
The draws below stay inside these ranges and needn't reach their ends.
Inputs may be any that keep to these rules, and one draw needn't show every extreme that they name: `params`: positions lie in front of every camera at depth 2.5 or more; quaternions have norm 0.5 or more; rows are position, log scale, quaternion, opacity logit, then colour coefficients 3 k + channel. `cameras`: entries 0 to 8 a rotation matrix, 9 to 11 a translation, 12 and 13 focal lengths, 14 and 15 the principal point, in pixels of the crop. `tile_index`: each row is a permutation of the 256 screen tiles. `send_slots`: entry (v, s, d * 16 + k) names a Gaussian of device s; device d keeps it as its received row s * 16 + k. `tile_lists`: each entry is a column s * 16 + k of the tile's device's received rows, in compositing order; a tile's used entries are distinct, hold equally many rows from every device s, and the entries -1 come after all of them; in every view some tile has 256 used entries. `reloc_send`: entry (s, d * 2 + k) is a slot on device s copied to device d, or -1; the used entries of a pair (s, d) come first, and some pair uses all 2; a slot may appear several times; no slot of device s is both here and in row s of reloc_recv. `reloc_recv`: entry (d, s * 2 + k) is the slot on device d that receives the copy named by reloc_send[s, d * 2 + k], -1 exactly where that is -1; the used slots of a row are distinct.
All inputs are finite; a program needn't handle non-finite values.
Results may differ from the reference program's by a relative error of at most 0.0003.
Values sent between devices are 32-bit elements; how exact they have to be, the bound alone decides.
No kernel may reach another device: no remote copies, remote signals or barrier semaphores. Data moves between devices by JAX's collectives and lax.ppermute only.
A program may use at most 128 MiB of HBM per device.

```python
import math
import jax
import jax.numpy as jnp
from jax import lax

DEVICE_TILES = 4
RCAP = 2
PARAMS = 59
PIX = 256
LIST = 256
G_DEV = 1024
CAP = 16
TILES_ACROSS = 16
VIEWS = 4
TILES = 256
G_TOTAL = 65536
N_GAUSS = 64
N_VIEW = 4


def screen_layout(key):
    seeded = jax.random.fold_in(key, 53)
    streams = jax.random.split(seeded, 8)
    per_source = LIST // N_GAUSS
    tile_count = DEVICE_TILES * N_GAUSS
    pair_width = DEVICE_TILES * per_source
    gauss_count = G_DEV * N_GAUSS
    tile_scores = jax.random.randint(streams[0], (N_VIEW, tile_count), 0, 4096) * tile_count + jnp.arange(tile_count, dtype=jnp.int32)[None, :]
    tile_map = jnp.argsort(tile_scores, axis=1).astype(jnp.int32)
    crowded = jax.random.randint(streams[1], (tile_count,), 0, 4)
    levels = jax.random.randint(streams[2], (tile_count,), 1, per_source + 1)
    forced = jax.random.randint(streams[3], (1,), 0, tile_count)
    tile_ids = jnp.arange(tile_count, dtype=jnp.int32)
    density = jnp.where((crowded == 0) | (tile_ids == forced[0]), per_source, levels).astype(jnp.int32)
    tile_ends = jnp.cumsum(density).astype(jnp.int32)
    tile_starts = tile_ends - density
    slot_scores = jax.random.randint(streams[4], (N_GAUSS, G_DEV), 0, 4096) * G_DEV + jnp.arange(G_DEV, dtype=jnp.int32)[None, :]
    slot_order = jnp.argsort(slot_scores, axis=1).astype(jnp.int32)
    depth_high = jax.random.randint(streams[5], (gauss_count,), 0, 2048)
    place_scores = jax.random.randint(streams[6], (N_VIEW, N_GAUSS, N_GAUSS, pair_width), 0, 4096) * pair_width + jnp.arange(pair_width, dtype=jnp.int32)
    holders = jnp.argsort(place_scores, axis=-1).astype(jnp.int32)
    fillers = jax.random.randint(streams[7], (N_VIEW, N_GAUSS, N_GAUSS, pair_width), 0, G_DEV)
    positions = jnp.arange(pair_width, dtype=jnp.int32)
    within_tile = positions % per_source
    tile_of = positions // per_source
    screen = tile_map.reshape(N_VIEW, N_GAUSS, DEVICE_TILES)[:, :, tile_of]
    active = within_tile[None, None, :] < density[screen]
    ranking = jnp.where(active, tile_starts[screen] + within_tile[None, None, :], 0)
    chosen = jnp.transpose(slot_order[:, ranking], (1, 0, 2, 3)).astype(jnp.int32)
    return (tile_map, tile_ends, slot_order, depth_high, holders, fillers, active, chosen)


def draw_params(key, part):
    tile_map, tile_ends, slot_order, depth_high, holders, fillers, active, chosen = screen_layout(key)
    key = jax.random.fold_in(key, 11)
    streams = jax.random.split(key, 8)
    gauss_count = G_DEV * N_GAUSS
    ranking = jnp.argsort(slot_order, axis=1).astype(jnp.int32)
    visible_total = tile_ends[-1]
    seen = (ranking < visible_total).reshape(-1)
    home = jnp.searchsorted(tile_ends, ranking, side='right').astype(jnp.int32).reshape(-1)
    home = jnp.where(seen, home, 0)
    column = (home % TILES_ACROSS).astype(jnp.float32)
    tile_row = (home // TILES_ACROSS).astype(jnp.float32)
    serial = jnp.arange(gauss_count, dtype=jnp.int32).astype(jnp.float32)
    depth_place = (depth_high.astype(jnp.float32) + serial / gauss_count) / 2048.0
    depth = 3.5 + 5.0 * depth_place
    inside_u = jax.random.uniform(streams[0], (gauss_count,), minval=0.5, maxval=15.5)
    inside_w = jax.random.uniform(streams[1], (gauss_count,), minval=0.5, maxval=15.5)
    log_scale = jax.random.uniform(streams[2], (3, gauss_count), minval=-6.0, maxval=-3.8)
    quat_w = jax.random.uniform(streams[3], (1, gauss_count), minval=0.6, maxval=1.4)
    quat_rest = jnp.clip(jax.random.normal(streams[4], (3, gauss_count)) * 0.4, -1.2, 1.2)
    logit = jax.random.uniform(streams[5], (1, gauss_count), minval=-4.5, maxval=-1.5)
    base_colour = jnp.clip(jax.random.normal(streams[6], (3, gauss_count)), -4.0, 4.0)
    rest_colour = jnp.clip(jax.random.normal(streams[7], (45, gauss_count)) * 0.3, -1.5, 1.5)
    pixel_u = jnp.where(seen, 16.0 * column + inside_u, -40.0 - 3.75 * inside_u)
    pixel_w = 16.0 * tile_row + inside_w
    pos_x = (pixel_u - DEVICE_TILES * 32.0) * depth / 2000.0
    pos_y = (pixel_w - N_GAUSS * 2.0) * depth / 2000.0
    return jnp.concatenate([pos_x[None], pos_y[None], depth[None], log_scale, quat_w, quat_rest, logit, base_colour, rest_colour], axis=0).astype(jnp.float32)


def draw_cameras(key, part):
    key = jax.random.fold_in(key, 23)
    streams = jax.random.split(key, 5)
    angles = jax.random.uniform(streams[0], (3, N_VIEW), minval=-0.0005, maxval=0.0005)
    offset = jax.random.uniform(streams[1], (3, N_VIEW), minval=-0.002, maxval=0.002)
    focal = jax.random.uniform(streams[2], (2, N_VIEW), minval=1998.0, maxval=2002.0)
    centre_x = DEVICE_TILES * 32.0 + jax.random.uniform(streams[3], (N_VIEW,), minval=-1.0, maxval=1.0)
    centre_y = N_GAUSS * 2.0 + jax.random.uniform(streams[4], (N_VIEW,), minval=-1.0, maxval=1.0)
    cos_a, sin_a = (jnp.cos(angles[0]), jnp.sin(angles[0]))
    cos_b, sin_b = (jnp.cos(angles[1]), jnp.sin(angles[1]))
    cos_c, sin_c = (jnp.cos(angles[2]), jnp.sin(angles[2]))
    entries = [cos_c * cos_b, cos_c * sin_b * sin_a - sin_c * cos_a, cos_c * sin_b * cos_a + sin_c * sin_a, sin_c * cos_b, sin_c * sin_b * sin_a + cos_c * cos_a, sin_c * sin_b * cos_a - cos_c * sin_a, -sin_b, cos_b * sin_a, cos_b * cos_a, offset[0], offset[1], offset[2], focal[0], focal[1], centre_x, centre_y]
    return jnp.stack(entries, axis=1).astype(jnp.float32)


def draw_tile_index(key, part):
    tile_map, tile_ends, slot_order, depth_high, holders, fillers, active, chosen = screen_layout(key)
    return tile_map.astype(jnp.int32)


def draw_send_slots(key, part):
    tile_map, tile_ends, slot_order, depth_high, holders, fillers, active, chosen = screen_layout(key)
    pair_width = DEVICE_TILES * (LIST // N_GAUSS)
    active_full = jnp.broadcast_to(active[:, None, :, :], chosen.shape)
    marked = jnp.where(active_full, chosen, -1)
    picked = jnp.take_along_axis(marked, holders, axis=-1)
    result = jnp.where(picked >= 0, picked, fillers)
    return result.reshape(N_VIEW, N_GAUSS, N_GAUSS * pair_width).astype(jnp.int32)


def draw_tile_lists(key, part):
    tile_map, tile_ends, slot_order, depth_high, holders, fillers, active, chosen = screen_layout(key)
    per_source = LIST // N_GAUSS
    pair_width = DEVICE_TILES * per_source
    gauss_count = G_DEV * N_GAUSS
    placing = jnp.argsort(holders, axis=-1).astype(jnp.int32)
    source_ids = jnp.arange(N_GAUSS, dtype=jnp.int32)[None, :, None, None]
    row_ids = source_ids * pair_width + placing
    gauss_ids = source_ids * G_DEV + chosen
    depth_key = depth_high[gauss_ids] * gauss_count + gauss_ids
    active_full = jnp.broadcast_to(active[:, None, :, :], chosen.shape)

    def arrange(values):
        shaped = values.reshape(N_VIEW, N_GAUSS, N_GAUSS, DEVICE_TILES, per_source)
        return jnp.transpose(shaped, (0, 2, 3, 1, 4)).reshape(N_VIEW, N_GAUSS, DEVICE_TILES, LIST)
    rows_listed = arrange(row_ids)
    keys_listed = arrange(depth_key)
    live_listed = arrange(active_full)
    spare_score = 2 ** 30 + jnp.arange(LIST, dtype=jnp.int32)
    score = jnp.where(live_listed, keys_listed, spare_score)
    ordering = jnp.argsort(score, axis=-1)
    rows_sorted = jnp.take_along_axis(rows_listed, ordering, axis=-1)
    live_sorted = jnp.take_along_axis(live_listed, ordering, axis=-1)
    result = jnp.where(live_sorted, rows_sorted, -1)
    return result.reshape(N_VIEW, DEVICE_TILES * N_GAUSS, LIST).astype(jnp.int32)


def relocation_tables(key):
    seeded = jax.random.fold_in(key, 71)
    streams = jax.random.split(seeded, 3)
    slots_total = N_GAUSS * RCAP
    scores = jax.random.randint(streams[0], (N_GAUSS, G_DEV), 0, 2 ** 12) * G_DEV + jnp.arange(G_DEV, dtype=jnp.int32)[None, :]
    ordering = jnp.argsort(scores, axis=1).astype(jnp.int32)
    counts = jax.random.randint(streams[1], (N_GAUSS, N_GAUSS), 0, RCAP + 1)
    rows_id = jnp.arange(N_GAUSS, dtype=jnp.int32)[:, None]
    cols_id = jnp.arange(N_GAUSS, dtype=jnp.int32)[None, :]
    counts = jnp.where(cols_id == (rows_id + 1) % N_GAUSS, RCAP, counts)
    picks = jax.random.randint(streams[2], (N_GAUSS, slots_total), slots_total, G_DEV)
    chosen = jnp.take_along_axis(ordering, picks, axis=1)
    placing = jnp.arange(slots_total, dtype=jnp.int32)
    within = placing % RCAP
    peer_of = placing // RCAP
    sending = jnp.where(within[None, :] < counts[:, peer_of], chosen, -1)
    receiving = jnp.where(within[None, :] < jnp.transpose(counts)[:, peer_of], ordering[:, :slots_total], -1)
    return (sending.astype(jnp.int32), receiving.astype(jnp.int32))


def draw_reloc_send(key, part):
    sending, receiving = relocation_tables(key)
    return sending


def draw_reloc_recv(key, part):
    sending, receiving = relocation_tables(key)
    return receiving


def block_scale(rng, extent, cuts, low, largest):
    loudness = 1.0
    for dim, parts in cuts:
        draws = jax.random.uniform(jax.random.fold_in(jax.random.fold_in(rng, 6), dim), (parts,), jnp.float32, low / len(cuts), largest / len(cuts))
        loudness = loudness * jnp.repeat(jnp.exp(draws), extent[dim] // parts).reshape((-1,) + (1,) * (len(extent) - 1 - dim))
    return loudness


def scatter_about(stream_key, shape, spread, most, pieces=(), kind=jnp.bfloat16):
    gain = block_scale(stream_key, shape, pieces, -0.22, 0.18) if pieces else 1.0
    values = jax.random.normal(stream_key, shape, jnp.float32) * spread * gain
    return jnp.minimum(jnp.maximum(values, -most), most).astype(kind)


def setup_inputs(seed: int = 0) -> dict:
    arg_keys = jax.random.split(jax.random.key(seed), 11)
    return {
        "params": draw_params(jax.random.fold_in(arg_keys[10], 71), 0),
        "first_moment": scatter_about(arg_keys[1], (PARAMS, G_TOTAL), 1.0, 6.0, ((1, 64),), jnp.float32),
        "second_moment": jnp.clip(jnp.exp(math.log(1.0) - 9.2103404 * jax.random.uniform(arg_keys[2], (PARAMS, G_TOTAL), jnp.float32) ** block_scale(arg_keys[2], (PARAMS, G_TOTAL), ((1, 64),), -0.2, 0.2)), 0.0001, 1.0),
        "cameras": draw_cameras(jax.random.fold_in(arg_keys[10], 71), 0),
        "target": jnp.clip(1.0 * jax.random.uniform(arg_keys[4], (VIEWS, TILES, 3, PIX), jnp.float32) ** block_scale(arg_keys[4], (VIEWS, TILES, 3, PIX), ((0, 4), (1, 64)), -0.2, 0.2), 0.0, 1.0),
        "tile_index": draw_tile_index(jax.random.fold_in(arg_keys[10], 71), 0),
        "tile_lists": draw_tile_lists(jax.random.fold_in(arg_keys[10], 71), 0),
        "send_slots": draw_send_slots(jax.random.fold_in(arg_keys[10], 71), 0),
        "reloc_send": draw_reloc_send(jax.random.fold_in(arg_keys[10], 71), 0),
        "reloc_recv": draw_reloc_recv(jax.random.fold_in(arg_keys[10], 71), 0),
    }


TOP_PRECISION = lax.Precision.HIGHEST
SH_ZERO = 0.28209479177387814
SH_ONE = 0.4886025119029199
SH_TWO = (1.0925484305920792, -1.0925484305920792, 0.31539156525252005, -1.0925484305920792, 0.5462742152960396)
SH_THREE = (-0.5900435899266435, 2.890611442640554, -0.4570457994644658, 0.3731763325901154, -0.4570457994644658, 1.445305721320277, -0.5900435899266435)
BIAS_ONE = 1.0 - math.exp(1000.0 * math.log(0.9))
BIAS_TWO = 1.0 - math.exp(1000.0 * math.log(0.999))

def harmonic(coeffs, direction):
    dir_x, dir_y, dir_z = (direction[0], direction[1], direction[2])
    sq_x, sq_y, sq_z = (dir_x * dir_x, dir_y * dir_y, dir_z * dir_z)
    factors = [SH_ZERO * jnp.ones_like(dir_x), -SH_ONE * dir_y, SH_ONE * dir_z, -SH_ONE * dir_x, SH_TWO[0] * dir_x * dir_y, SH_TWO[1] * dir_y * dir_z, SH_TWO[2] * (2.0 * sq_z - sq_x - sq_y), SH_TWO[3] * dir_x * dir_z, SH_TWO[4] * (sq_x - sq_y), SH_THREE[0] * dir_y * (3.0 * sq_x - sq_y), SH_THREE[1] * dir_x * dir_y * dir_z, SH_THREE[2] * dir_y * (4.0 * sq_z - sq_x - sq_y), SH_THREE[3] * dir_z * (2.0 * sq_z - 3.0 * sq_x - 3.0 * sq_y), SH_THREE[4] * dir_x * (4.0 * sq_z - sq_x - sq_y), SH_THREE[5] * dir_z * (sq_x - sq_y), SH_THREE[6] * dir_x * (sq_x - 3.0 * sq_y)]
    result = jnp.zeros(coeffs.shape[1:], coeffs.dtype)
    for index_k in range(16):
        result = result + factors[index_k][None, :] * coeffs[index_k]
    return result

def project(params, camera):
    position = params[0:3]
    rotation = camera[0:9].reshape(3, 3)
    offset = camera[9:12]
    focal_x, focal_y, centre_x, centre_y = (camera[12], camera[13], camera[14], camera[15])
    in_camera = jnp.dot(rotation, position, precision=TOP_PRECISION) + offset[:, None]
    cam_x, cam_y, cam_z = (in_camera[0], in_camera[1], in_camera[2])
    inverse_z = 1.0 / cam_z
    mean_u = focal_x * cam_x * inverse_z + centre_x
    mean_w = focal_y * cam_y * inverse_z + centre_y
    quaternion = params[6:10]
    quaternion = quaternion / jnp.sqrt(lax.optimization_barrier(jnp.sum(quaternion * quaternion, axis=0)))
    quat_w, quat_x, quat_y, quat_z = (quaternion[0], quaternion[1], quaternion[2], quaternion[3])
    orient = [[1.0 - 2.0 * (quat_y * quat_y + quat_z * quat_z), 2.0 * (quat_x * quat_y - quat_w * quat_z), 2.0 * (quat_x * quat_z + quat_w * quat_y)], [2.0 * (quat_x * quat_y + quat_w * quat_z), 1.0 - 2.0 * (quat_x * quat_x + quat_z * quat_z), 2.0 * (quat_y * quat_z - quat_w * quat_x)], [2.0 * (quat_x * quat_z - quat_w * quat_y), 2.0 * (quat_y * quat_z + quat_w * quat_x), 1.0 - 2.0 * (quat_x * quat_x + quat_y * quat_y)]]
    scales = jnp.exp(params[3:6])
    factor_m = [[orient[row_i][col_j] * scales[col_j] for col_j in range(3)] for row_i in range(3)]
    sigma = [[factor_m[row_i][0] * factor_m[col_j][0] + factor_m[row_i][1] * factor_m[col_j][1] + factor_m[row_i][2] * factor_m[col_j][2] for col_j in range(3)] for row_i in range(3)]
    jac_a0 = focal_x * inverse_z
    jac_a2 = -focal_x * cam_x * inverse_z * inverse_z
    jac_b1 = focal_y * inverse_z
    jac_b2 = -focal_y * cam_y * inverse_z * inverse_z
    row_a = [jac_a0 * rotation[0, col_i] + jac_a2 * rotation[2, col_i] for col_i in range(3)]
    row_b = [jac_b1 * rotation[1, col_i] + jac_b2 * rotation[2, col_i] for col_i in range(3)]

    def quadratic(leftmost_row, right_row):
        total = jnp.zeros_like(cam_x)
        for row_i in range(3):
            for col_j in range(3):
                total = total + leftmost_row[row_i] * sigma[row_i][col_j] * right_row[col_j]
        return total
    cov_aa = quadratic(row_a, row_a) + 0.3
    cov_ab = quadratic(row_a, row_b)
    cov_bb = quadratic(row_b, row_b) + 0.3
    determinant = cov_aa * cov_bb - cov_ab * cov_ab
    opacity = jax.nn.sigmoid(params[10])
    centre = jnp.stack([-(rotation[0, col_i] * offset[0] + rotation[1, col_i] * offset[1] + rotation[2, col_i] * offset[2]) for col_i in range(3)])
    direction = position - centre[:, None]
    direction = direction / jnp.sqrt(lax.optimization_barrier(jnp.sum(direction * direction, axis=0)))
    colour_values = jnp.maximum(harmonic(params[11:59].reshape(16, 3, -1), direction) + 0.5, 0.0)
    head = jnp.stack([mean_u, mean_w, cov_bb / determinant, -cov_ab / determinant, cov_aa / determinant, opacity])
    return jnp.concatenate([head, colour_values], axis=0)

def render_group(received, tile_rows, tile_ids, target_tile):
    live_entry = tile_rows >= 0
    safe_index = jnp.where(live_entry, tile_rows, 0)
    listed = received[:, safe_index]
    live_mask = live_entry.astype(received.dtype)
    pixels = jnp.arange(256, dtype=jnp.int32)
    left_edge = (tile_ids % TILES_ACROSS * 16).astype(received.dtype)
    top_edge = (tile_ids // TILES_ACROSS * 16).astype(received.dtype)
    pixel_u = left_edge[:, None] + (pixels % 16).astype(received.dtype)[None, :] + 0.5
    pixel_w = top_edge[:, None] + (pixels // 16).astype(received.dtype)[None, :] + 0.5
    block_extent = 128
    index_row = jnp.arange(block_extent)
    strict_upper = (index_row[:, None] < index_row[None, :]).astype(received.dtype)
    carried = jnp.zeros(pixel_u.shape, received.dtype)
    colour_values = jnp.zeros((tile_ids.shape[0], 3, 256), received.dtype)
    for block_index in range(tile_rows.shape[1] // block_extent):
        lower = block_index * block_extent
        rows_per_block = listed[:, :, lower:lower + block_extent]
        block_live = live_mask[:, lower:lower + block_extent]
        off_u = pixel_u[:, :, None] - rows_per_block[0][:, None, :]
        off_w = pixel_w[:, :, None] - rows_per_block[1][:, None, :]
        exponent = -0.5 * (rows_per_block[2][:, None, :] * off_u * off_u + rows_per_block[4][:, None, :] * off_w * off_w) - rows_per_block[3][:, None, :] * off_u * off_w
        alphas = rows_per_block[5][:, None, :] * jnp.exp(exponent) * block_live[:, None, :]
        log_keep = jnp.log1p(-alphas)
        before = jnp.einsum('gpj,ji->gpi', log_keep, strict_upper, precision=TOP_PRECISION)
        blend_weights = jnp.exp(carried[:, :, None] + before) * alphas
        colour_values = colour_values + jnp.einsum('xuo,sxo->xsu', blend_weights, rows_per_block[6:9], precision=TOP_PRECISION)
        carried = carried + lax.optimization_barrier(jnp.sum(log_keep, axis=2))
    residual = colour_values - target_tile
    return 0.5 * jnp.sum(residual * residual)

def adam_update(params, gradient, first, second):
    rates = jnp.concatenate([jnp.full((3, 1), 0.00016), jnp.full((3, 1), 0.005), jnp.full((4, 1), 0.001), jnp.full((1, 1), 0.05), jnp.full((3, 1), 0.0025), jnp.full((45, 1), 0.000125)]).astype(params.dtype)
    first_new = 0.9 * first + 0.1 * gradient
    second_new = 0.999 * second + 0.001 * gradient * gradient
    stepped = params - rates * (first_new / BIAS_ONE) / (jnp.sqrt(second_new / BIAS_TWO) + 1e-15)
    return (stepped, first_new, second_new)

def total_loss(params, cameras, target, tile_index, tile_lists, send_slots):
    accumulated = jnp.zeros((), params.dtype)
    source_base = (jnp.arange(N_GAUSS, dtype=jnp.int32) * G_DEV)[None, :, None]
    for view_number in range(N_VIEW):
        projected = project(params, cameras[view_number])
        slot_table = send_slots[view_number].reshape(N_GAUSS, N_GAUSS, CAP)
        source_index = (jnp.transpose(slot_table, (1, 0, 2)) + source_base).reshape(N_GAUSS, N_GAUSS * CAP)
        arrived = jnp.moveaxis(projected[:, source_index], 1, 0)
        render_step = jax.checkpoint(lambda item: render_group(item[0], item[1], item[2], item[3]))
        group_losses = lax.map(render_step, (arrived, tile_lists[view_number].reshape(N_GAUSS, DEVICE_TILES, LIST), tile_index[view_number].reshape(N_GAUSS, DEVICE_TILES), target[view_number].reshape(N_GAUSS, DEVICE_TILES, 3, PIX)))
        accumulated = accumulated + jnp.sum(group_losses)
    return accumulated

def reference(params, first_moment, second_moment, cameras, target, tile_index, tile_lists, send_slots, reloc_send, reloc_recv):
    gradient = jax.grad(total_loss)(params, cameras, target, tile_index, tile_lists, send_slots)
    stepped, first_new, second_new = adam_update(params, gradient, first_moment, second_moment)
    slot_numbers = jnp.arange(G_DEV, dtype=jnp.int32)
    counts = lax.optimization_barrier(jnp.sum((reloc_send[:, None, :] == slot_numbers[None, :, None]).astype(jnp.int32), axis=2)).reshape(-1)
    sampled = counts > 0
    logit = stepped[10]
    share_log = -jax.nn.softplus(logit) / (counts.astype(stepped.dtype) + 1.0)
    spread_logit = jnp.log(-jnp.expm1(share_log)) - share_log
    stepped = stepped.at[10].set(jnp.where(sampled, spread_logit, logit))
    first_new = jnp.where(sampled[None, :], 0.0, first_new)
    second_new = jnp.where(sampled[None, :], 0.0, second_new)
    table = jnp.transpose(reloc_send.reshape(N_GAUSS, N_GAUSS, RCAP), (1, 0, 2))
    valid = table >= 0
    base_source = (jnp.arange(N_GAUSS, dtype=jnp.int32) * G_DEV)[None, :, None]
    global_source = jnp.where(valid, table + base_source, 0).reshape(-1)
    moved = jnp.where(valid.reshape(-1)[None, :], stepped[:, global_source], 0.0)
    base_target = (jnp.arange(N_GAUSS, dtype=jnp.int32) * G_DEV)[:, None]
    targets = jnp.where(reloc_recv >= 0, reloc_recv + base_target, N_GAUSS * G_DEV).reshape(-1)
    new_params = stepped.at[:, targets].set(moved, mode='drop')
    new_first = first_new.at[:, targets].set(0.0, mode='drop')
    new_second = second_new.at[:, targets].set(0.0, mode='drop')
    return (new_params, new_first, new_second, gradient)
```

```python
import math

import jax
import jax.numpy as jnp
from jax import lax
from jax.experimental import pallas as pl
from jax.experimental.pallas import tpu as pltpu
from jax.sharding import PartitionSpec as P

F32 = jnp.float32
BF16 = jnp.bfloat16
I32 = jnp.int32
PEERS = 64
LOCAL = 1024
CAP = 16
VIEWS = 4
TILES = 4
ACROSS = 16
ROWS = 16

SH_ZERO = 0.28209479177387814
SH_ONE = 0.4886025119029199
SH_TWO = (
    1.0925484305920792,
    -1.0925484305920792,
    0.31539156525252005,
    -1.0925484305920792,
    0.5462742152960396,
)
SH_THREE = (
    -0.5900435899266435,
    2.890611442640554,
    -0.4570457994644658,
    0.3731763325901154,
    -0.4570457994644658,
    1.445305721320277,
    -0.5900435899266435,
)
BIAS_ONE = 1.0 - math.exp(1000.0 * math.log(0.9))
BIAS_TWO = 1.0 - math.exp(1000.0 * math.log(0.999))
VMEM_LIMIT = 16 * 1024 * 1024


def split(x, parts):
    out = []
    for index in range(parts):
        piece = x.astype(BF16)
        out.append(piece)
        if index + 1 < parts:
            x = x - piece.astype(F32)
    return out


def low_onehot(idx):
    lane = lax.broadcasted_iota(I32, (128, idx.shape[1]), 0)
    return jnp.where(lane == (idx & 127), 1.0, 0.0).astype(BF16)


def take_columns(table, idx, hot):
    rows = table.shape[0]
    high = idx >> 7
    parts = split(table, 3)
    lhs = jnp.concatenate(
        [
            jnp.concatenate([p[:, c * 128 : (c + 1) * 128] for p in parts], axis=1)
            for c in range(8)
        ],
        axis=0,
    )
    rhs = jnp.concatenate([hot, hot, hot], axis=0)
    wide = jnp.dot(lhs, rhs, preferred_element_type=F32)
    total = None
    for c in range(8):
        term = jnp.where(high == c, wide[c * rows : (c + 1) * rows], 0.0)
        total = term if total is None else total + term
    return total


def add_columns(values, idx, hot):
    rows = values.shape[0]
    high = idx >> 7
    masked = jnp.concatenate([jnp.where(high == c, values, 0.0) for c in range(8)], axis=0)
    lhs = jnp.concatenate(split(masked, 3), axis=1)
    rhs = jnp.concatenate([hot, hot, hot], axis=1)
    wide = lax.dot_general(lhs, rhs, (((1,), (1,)), ((), ())), preferred_element_type=F32)
    return jnp.concatenate([wide[c * rows : (c + 1) * rows] for c in range(8)], axis=1)


def pack_peers(table):
    pieces = [table[:, k * PEERS : (k + 1) * PEERS] for k in range(CAP)]
    return jnp.concatenate(pieces, axis=0).T


def unpack_peers(block):
    flat = block.T
    return jnp.concatenate([flat[k * ROWS : (k + 1) * ROWS] for k in range(CAP)], axis=1)


def slots_by_rank(slots):
    source = lax.broadcasted_iota(I32, (128, LOCAL), 0)
    col = lax.broadcasted_iota(I32, (128, LOCAL), 1)
    pick = jnp.where(source == (col & 7) * 16 + (col >> 6), 1.0, 0.0).astype(BF16)
    upper = jnp.dot((slots >> 5).astype(F32).astype(BF16), pick, preferred_element_type=F32)
    lower = jnp.dot((slots & 31).astype(F32).astype(BF16), pick, preferred_element_type=F32)
    wide = upper * 32.0 + lower
    row = lax.broadcasted_iota(I32, (8, LOCAL), 0)
    column = lax.broadcasted_iota(I32, (8, LOCAL), 1)
    kept = jnp.where(row == ((column >> 3) & 7), wide, 0.0)
    return jnp.sum(kept, axis=0, keepdims=True).astype(I32)


def covariance(log_scale, quat):
    norm = jnp.sqrt(quat[0] * quat[0] + quat[1] * quat[1] + quat[2] * quat[2] + quat[3] * quat[3])
    quat_w, quat_x, quat_y, quat_z = [q / norm for q in quat]
    orient = [
        [
            1.0 - 2.0 * (quat_y * quat_y + quat_z * quat_z),
            2.0 * (quat_x * quat_y - quat_w * quat_z),
            2.0 * (quat_x * quat_z + quat_w * quat_y),
        ],
        [
            2.0 * (quat_x * quat_y + quat_w * quat_z),
            1.0 - 2.0 * (quat_x * quat_x + quat_z * quat_z),
            2.0 * (quat_y * quat_z - quat_w * quat_x),
        ],
        [
            2.0 * (quat_x * quat_z - quat_w * quat_y),
            2.0 * (quat_y * quat_z + quat_w * quat_x),
            1.0 - 2.0 * (quat_x * quat_x + quat_y * quat_y),
        ],
    ]
    scales = [jnp.exp(s) for s in log_scale]
    factor = [[orient[i][j] * scales[j] for j in range(3)] for i in range(3)]

    def entry(i, j):
        return (
            factor[i][0] * factor[j][0] + factor[i][1] * factor[j][1] + factor[i][2] * factor[j][2]
        )

    return [entry(0, 0), entry(0, 1), entry(0, 2), entry(1, 1), entry(1, 2), entry(2, 2)]


def harmonics(dir_x, dir_y, dir_z):
    sq_x, sq_y, sq_z = (dir_x * dir_x, dir_y * dir_y, dir_z * dir_z)
    return [
        -SH_ONE * dir_y,
        SH_ONE * dir_z,
        -SH_ONE * dir_x,
        SH_TWO[0] * dir_x * dir_y,
        SH_TWO[1] * dir_y * dir_z,
        SH_TWO[2] * (2.0 * sq_z - sq_x - sq_y),
        SH_TWO[3] * dir_x * dir_z,
        SH_TWO[4] * (sq_x - sq_y),
        SH_THREE[0] * dir_y * (3.0 * sq_x - sq_y),
        SH_THREE[1] * dir_x * dir_y * dir_z,
        SH_THREE[2] * dir_y * (4.0 * sq_z - sq_x - sq_y),
        SH_THREE[3] * dir_z * (2.0 * sq_z - 3.0 * sq_x - 3.0 * sq_y),
        SH_THREE[4] * dir_x * (4.0 * sq_z - sq_x - sq_y),
        SH_THREE[5] * dir_z * (sq_x - sq_y),
        SH_THREE[6] * dir_x * (sq_x - 3.0 * sq_y),
    ]


def view_rows(position, sigma, coeffs, cam):
    rot = [cam[0:3], cam[3:6], cam[6:9]]
    offset = cam[9:12]
    focal_x, focal_y, centre_x, centre_y = cam[12:16]
    cam_x, cam_y, cam_z = [
        rot[i][0] * position[0] + rot[i][1] * position[1] + rot[i][2] * position[2] + offset[i]
        for i in range(3)
    ]
    inverse_z = 1.0 / cam_z
    mean_u = focal_x * cam_x * inverse_z + centre_x
    mean_w = focal_y * cam_y * inverse_z + centre_y
    jac_a0 = focal_x * inverse_z
    jac_a2 = -focal_x * cam_x * inverse_z * inverse_z
    jac_b1 = focal_y * inverse_z
    jac_b2 = -focal_y * cam_y * inverse_z * inverse_z
    row_a = [jac_a0 * rot[0][i] + jac_a2 * rot[2][i] for i in range(3)]
    row_b = [jac_b1 * rot[1][i] + jac_b2 * rot[2][i] for i in range(3)]
    full = [
        [sigma[0], sigma[1], sigma[2]],
        [sigma[1], sigma[3], sigma[4]],
        [sigma[2], sigma[4], sigma[5]],
    ]

    def through(row):
        return [full[i][0] * row[0] + full[i][1] * row[1] + full[i][2] * row[2] for i in range(3)]

    def dot3(left, right):
        return left[0] * right[0] + left[1] * right[1] + left[2] * right[2]

    sigma_a = through(row_a)
    sigma_b = through(row_b)
    cov_aa = dot3(row_a, sigma_a) + 0.3
    cov_ab = dot3(row_a, sigma_b)
    cov_bb = dot3(row_b, sigma_b) + 0.3
    determinant = cov_aa * cov_bb - cov_ab * cov_ab
    inverse_det = 1.0 / determinant
    ray = [
        position[i] + (rot[0][i] * offset[0] + rot[1][i] * offset[1] + rot[2][i] * offset[2])
        for i in range(3)
    ]
    inverse_norm = 1.0 / jnp.sqrt(dot3(ray, ray))
    basis = harmonics(*[r * inverse_norm for r in ray])
    colours = []
    for channel in range(3):
        total = SH_ZERO * coeffs[channel]
        for index in range(15):
            total = total + basis[index] * coeffs[3 + 3 * index + channel]
        colours.append(jnp.maximum(total + 0.5, 0.0))
    return [
        mean_u,
        mean_w,
        cov_bb * inverse_det,
        -cov_ab * inverse_det,
        cov_aa * inverse_det,
    ] + colours


def send_kernel(params_ref, slots_ref, camera_ref, out_ref, order_ref):
    dense = params_ref[...].reshape(59, 8, 128)
    rows = [dense[i] for i in range(59)]
    cam = [camera_ref[0, i] for i in range(16)]
    sigma = covariance(rows[3:6], rows[6:10])
    seen = view_rows(rows[0:3], sigma, rows[11:59], cam)
    opacity = 1.0 / (1.0 + jnp.exp(-rows[10]))
    listed = seen[0:5] + [opacity] + seen[5:8]
    blank = jnp.zeros((8, 128), F32)
    table = jnp.stack(listed + [blank] * (ROWS - 9)).reshape(ROWS, LOCAL)
    order = slots_by_rank(slots_ref[...])
    order_ref[...] = order
    out_ref[...] = pack_peers(take_columns(table, order, low_onehot(order)))


def render_kernel(recv_ref, lists_ref, tiles_ref, target_ref, out_ref, alpha_ref, grad_ref):
    table = unpack_peers(recv_ref[...])
    entries = lists_ref[...]
    idx = jnp.where(entries < 0, -1, (entries & 15) * PEERS + (entries >> 4))
    hot = low_onehot(idx)
    listed = take_columns(table, idx, hot)
    iota_r = lax.broadcasted_iota(I32, (256, 256), 0)
    iota_c = lax.broadcasted_iota(I32, (256, 256), 1)
    before_mask = jnp.where(iota_r < iota_c, 1.0, 0.0).astype(BF16)
    after_mask = jnp.where(iota_r > iota_c, 1.0, 0.0).astype(BF16)
    steps = lax.broadcasted_iota(I32, (16, 256), 0).astype(F32)
    results = []
    for tile in range(TILES):
        here = listed[:, tile * 256 : (tile + 1) * 256]
        number = tiles_ref[0, tile]
        left = ((number & (ACROSS - 1)) * 16).astype(F32)
        top = ((number >> 4) * 16).astype(F32)
        con_a, con_b, con_c, opacity = here[2:3], here[3:4], here[4:5], here[5:6]
        off_u = (steps + left + 0.5) - here[0:1]
        off_w = (steps + top + 0.5) - here[1:2]
        quad_u = -0.5 * con_a * off_u * off_u
        cross = -con_b * off_u
        quad_w = -0.5 * con_c * off_w * off_w
        for j in range(16):
            exponent = quad_u + quad_w[j : j + 1] + cross * off_w[j : j + 1]
            alpha_ref[j * 16 : (j + 1) * 16, :] = opacity * jnp.exp(exponent)
        alpha = alpha_ref[...]
        keep = 1.0 - alpha
        logs = split(jnp.log(keep), 2)
        before = jnp.dot(logs[0], before_mask, preferred_element_type=F32) + jnp.dot(
            logs[1], before_mask, preferred_element_type=F32
        )
        weight = jnp.exp(before) * alpha
        weights = split(weight, 2)
        colour = here[6:9]
        colour_parts = split(colour, 3)
        stacked = jnp.concatenate(
            [p.astype(F32) for p in colour_parts] + [jnp.zeros((7, 256), F32)], axis=0
        ).astype(BF16)
        nt = (((1,), (1,)), ((), ()))
        summed = lax.dot_general(
            stacked, weights[0], nt, preferred_element_type=F32
        ) + lax.dot_general(stacked, weights[1], nt, preferred_element_type=F32)
        rendered = summed[0:3] + summed[3:6] + summed[6:9]
        residual = rendered - target_ref[tile]
        residual_parts = [p.astype(F32) for p in split(residual, 3)]
        colour_wide = [p.astype(F32) for p in colour_parts]
        pairs = ((0, 0), (0, 1), (1, 0), (1, 1), (0, 2), (2, 0))
        blank = jnp.zeros((14, 256), F32)
        left_side = jnp.concatenate([residual_parts[a] for a, _ in pairs] + [blank], axis=0)
        right_side = jnp.concatenate([colour_wide[b] for _, b in pairs] + [blank], axis=0)
        pull = lax.dot_general(
            left_side.astype(BF16),
            right_side.astype(BF16),
            (((0,), (0,)), ((), ())),
            preferred_element_type=F32,
        )
        weighted = pull * weight
        flows = split(weighted, 2)
        after = jnp.dot(flows[0], after_mask, preferred_element_type=F32) + jnp.dot(
            flows[1], after_mask, preferred_element_type=F32
        )
        grad_ref[...] = weighted - after * (alpha / keep)
        stacked_res = jnp.concatenate(residual_parts + [jnp.zeros((7, 256), F32)], axis=0).astype(
            BF16
        )
        colour_sum = jnp.dot(stacked_res, weights[0], preferred_element_type=F32) + jnp.dot(
            stacked_res, weights[1], preferred_element_type=F32
        )
        colour_grad = colour_sum[0:3] + colour_sum[3:6] + colour_sum[6:9]
        zeroth = first = second = None
        for j in range(16):
            piece = grad_ref[j * 16 : (j + 1) * 16, :]
            lifted = piece * off_w[j : j + 1]
            twice = lifted * off_w[j : j + 1]
            zeroth = piece if zeroth is None else zeroth + piece
            first = lifted if first is None else first + lifted
            second = twice if second is None else second + twice

        def over(values):
            return jnp.sum(values, axis=0, keepdims=True)

        along = zeroth * off_u
        m_00, m_10, m_20 = over(zeroth), over(along), over(along * off_u)
        m_01, m_11, m_02 = over(first), over(first * off_u), over(second)
        results.append(
            jnp.concatenate(
                [
                    con_a * m_10 + con_b * m_01,
                    con_c * m_01 + con_b * m_10,
                    -0.5 * m_20,
                    -m_11,
                    -0.5 * m_02,
                    m_00,
                    colour_grad,
                    jnp.zeros((ROWS - 9, 256), F32),
                ],
                axis=0,
            )
        )
    grads = jnp.concatenate(results, axis=1)
    out_ref[...] = pack_peers(add_columns(grads, idx, hot))


def owner_kernel(recv_ref, order_ref, camera_ref, out_ref):
    values = unpack_peers(recv_ref[...])
    order = order_ref[...]
    out_ref[...] = add_columns(values, order, low_onehot(order))
    for i in range(16):
        out_ref[9 + i // 8 : 10 + i // 8, (i % 8) * 128 : (i % 8 + 1) * 128] = jnp.full(
            (1, 128), camera_ref[0, i], F32
        )


def log_one_plus(t):
    s = t / (2.0 + t)
    square = s * s
    total = jnp.full_like(s, 1.0 / 17.0)
    for odd in (15, 13, 11, 9, 7, 5, 3, 1):
        total = total * square + 1.0 / odd
    return 2.0 * s * total


def one_minus_exp(x):
    small = jnp.ones_like(x)
    for n in range(10, 1, -1):
        small = 1.0 + small * x * (1.0 / n)
    return jnp.where(x > -0.5, -x * small, 1.0 - jnp.exp(x))


def rates_column():
    row = lax.broadcasted_iota(I32, (59, 1), 0)
    rate = jnp.where(row < 14, 0.0025, 0.000125)
    rate = jnp.where(row < 11, 0.05, rate)
    rate = jnp.where(row < 10, 0.001, rate)
    rate = jnp.where(row < 6, 0.005, rate)
    return jnp.where(row < 3, 0.00016, rate)


def tree_sum(values):
    return (values[0] + values[1]) + (values[2] + values[3])


def step_kernel(
    params_ref,
    first_ref,
    second_ref,
    own_ref,
    near_ref,
    far_ref,
    last_ref,
    sources_ref,
    targets_ref,
    spread_ref,
    new_first_ref,
    new_second_ref,
    gradient_ref,
    out_ref,
):
    dense = params_ref[...].reshape(59, 8, 128)
    rows = [dense[i] for i in range(59)]
    sigma, pull_sigma = jax.vjp(covariance, rows[3:6], rows[6:10])
    position, coeffs = rows[0:3], rows[11:59]
    pos_parts, sigma_parts, coeff_parts, opacity_parts = [], [], [], []
    for ref in (own_ref, near_ref, far_ref, last_ref):
        got = ref[...].reshape(ROWS, 8, 128)
        cam = [jnp.broadcast_to(got[9 + i // 8, i % 8 : i % 8 + 1, :], (8, 128)) for i in range(16)]
        _, pull = jax.vjp(lambda p, s, c: view_rows(p, s, c, cam), position, sigma, coeffs)
        d_pos, d_sigma, d_coeff = pull([got[i] for i in (0, 1, 2, 3, 4, 6, 7, 8)])
        pos_parts.append(d_pos)
        sigma_parts.append(d_sigma)
        coeff_parts.append(d_coeff)
        opacity_parts.append(got[5])
    d_pos = [tree_sum([p[i] for p in pos_parts]) for i in range(3)]
    d_sigma = [tree_sum([p[i] for p in sigma_parts]) for i in range(6)]
    d_coeff = [tree_sum([p[i] for p in coeff_parts]) for i in range(48)]
    d_scale, d_quat = pull_sigma(d_sigma)
    opacity = 1.0 / (1.0 + jnp.exp(-rows[10]))
    d_logit = tree_sum(opacity_parts) * (1.0 - opacity)
    gradient = jnp.stack(d_pos + list(d_scale) + list(d_quat) + [d_logit] + d_coeff).reshape(
        59, LOCAL
    )
    gradient_ref[...] = gradient
    first = 0.9 * first_ref[...] + 0.1 * gradient
    second = 0.999 * second_ref[...] + 0.001 * gradient * gradient
    stepped = params_ref[...] - rates_column() * (first / BIAS_ONE) / (
        jnp.sqrt(second / BIAS_TWO) + 1e-15
    )
    sources = sources_ref[...]
    targets = targets_ref[...]
    ones = jnp.ones((8, 128), F32)
    source_hot = low_onehot(sources)
    counts = add_columns(ones, sources, source_hot)[0:1]
    landing = add_columns(ones, targets, low_onehot(targets))[0:1]
    sampled = counts > 0.5
    cleared = (counts + landing) > 0.5
    logit = stepped[10:11]
    soft = jnp.maximum(logit, 0.0) + log_one_plus(jnp.exp(-jnp.abs(logit)))
    share = -soft / (counts + 1.0)
    shared_logit = jnp.log(one_minus_exp(share)) - share
    row = lax.broadcasted_iota(I32, (59, LOCAL), 0)
    spread = jnp.where((row == 10) & sampled, shared_logit, stepped)
    spread_ref[...] = spread
    new_first_ref[...] = jnp.where(cleared, 0.0, first)
    new_second_ref[...] = jnp.where(cleared, 0.0, second)
    table = jnp.concatenate([spread, jnp.ones((5, LOCAL), F32)], axis=0)
    moved = take_columns(table, sources, source_hot)
    out_ref[...] = jnp.concatenate([moved[:, 0:PEERS], moved[:, PEERS : 2 * PEERS]], axis=0).T


def landing_kernel(recv_ref, targets_ref, spread_ref, out_ref):
    flat = recv_ref[...].T
    moved = jnp.concatenate([flat[0:64], flat[64:128]], axis=1)
    targets = targets_ref[...]
    placed = add_columns(moved, targets, low_onehot(targets))
    out_ref[...] = jnp.where(placed[59:60] > 0.5, placed[0:59], spread_ref[...])


def by_rank(pairs):
    return jnp.transpose(pairs.reshape(PEERS, 2)).reshape(1, 2 * PEERS)


def call(kernel, shapes, smem=(), scratch=(), count=0):
    vmem = pl.BlockSpec(memory_space=pltpu.VMEM)
    scalar = pl.BlockSpec(memory_space=pltpu.SMEM)
    out_shape = [jax.ShapeDtypeStruct(shape, dtype) for shape, dtype in shapes]
    return pl.pallas_call(
        kernel,
        out_shape=out_shape,
        in_specs=[scalar if i in smem else vmem for i in range(count)],
        out_specs=[vmem] * len(out_shape),
        scratch_shapes=list(scratch),
        compiler_params=pltpu.CompilerParams(vmem_limit_bytes=VMEM_LIMIT),
    )


def exchange(block):
    return lax.all_to_all(block, "gauss", split_axis=0, concat_axis=0, tiled=True)


def shards(
    params,
    first_moment,
    second_moment,
    cameras,
    target,
    tile_index,
    tile_lists,
    send_slots,
    reloc_send,
    reloc_recv,
):
    outgoing, order = call(
        send_kernel,
        [((PEERS, CAP * ROWS), F32), ((1, LOCAL), I32)],
        smem=(2,),
        count=3,
    )(params, send_slots.reshape(8, 128), cameras)
    received = exchange(outgoing)
    (row_grads,) = call(
        render_kernel,
        [((PEERS, CAP * ROWS), F32)],
        smem=(2,),
        scratch=[pltpu.VMEM((256, 256), F32), pltpu.VMEM((256, 256), F32)],
        count=4,
    )(received, tile_lists.reshape(1, LOCAL), tile_index, target.reshape(TILES, 3, 256))
    returned = exchange(row_grads)
    (own,) = call(owner_kernel, [((ROWS, LOCAL), F32)], smem=(2,), count=3)(
        returned, order, cameras
    )
    others = [
        lax.ppermute(own, "view", [(i, i ^ flip) for i in range(VIEWS)]) for flip in (1, 2, 3)
    ]
    sources = by_rank(reloc_send)
    targets = by_rank(reloc_recv)
    whole = ((59, LOCAL), F32)
    spread, new_first, new_second, gradient, moving = call(
        step_kernel,
        [whole, whole, whole, whole, ((PEERS, 128), F32)],
        count=9,
    )(params, first_moment, second_moment, own, *others, sources, targets)
    arrived = exchange(moving)
    (new_params,) = call(landing_kernel, [whole], count=3)(arrived, targets, spread)
    return (new_params, new_first, new_second, gradient)


def solution(mesh):
    in_specs = (
        P(None, "gauss"),
        P(None, "gauss"),
        P(None, "gauss"),
        P("view", None),
        P("view", "gauss", None, None),
        P("view", "gauss"),
        P("view", "gauss", None),
        P("view", "gauss", None),
        P("gauss", None),
        P("gauss", None),
    )
    out_specs = (P(None, "gauss"), P(None, "gauss"), P(None, "gauss"), P(None, "gauss"))
    return jax.shard_map(shards, mesh=mesh, in_specs=in_specs, out_specs=out_specs, check_vma=False)
```

```python
import math

import jax
import jax.numpy as jnp
from jax import lax
from jax.experimental import pallas as pl
from jax.experimental.pallas import tpu as pltpu
from jax.sharding import PartitionSpec as P

F32 = jnp.float32
BF16 = jnp.bfloat16
I32 = jnp.int32
PEERS = 64
LOCAL = 1024
CAP = 16
VIEWS = 4
TILES = 4
ACROSS = 16
ROWS = 16

SH_ZERO = 0.28209479177387814
SH_ONE = 0.4886025119029199
SH_TWO = (
    1.0925484305920792,
    -1.0925484305920792,
    0.31539156525252005,
    -1.0925484305920792,
    0.5462742152960396,
)
SH_THREE = (
    -0.5900435899266435,
    2.890611442640554,
    -0.4570457994644658,
    0.3731763325901154,
    -0.4570457994644658,
    1.445305721320277,
    -0.5900435899266435,
)
BIAS_ONE = 1.0 - math.exp(1000.0 * math.log(0.9))
BIAS_TWO = 1.0 - math.exp(1000.0 * math.log(0.999))
VMEM_LIMIT = 16 * 1024 * 1024


def split(x, parts):
    out = []
    for index in range(parts):
        piece = x.astype(BF16)
        out.append(piece)
        if index + 1 < parts:
            x = x - piece.astype(F32)
    return out


def low_onehot(idx):
    lane = lax.broadcasted_iota(I32, (128, idx.shape[1]), 0)
    return jnp.where(lane == (idx & 127), 1.0, 0.0).astype(BF16)


def take_columns(table, idx, hot):
    rows = table.shape[0]
    high = idx >> 7
    parts = split(table, 3)
    lhs = jnp.concatenate(
        [
            jnp.concatenate([p[:, c * 128 : (c + 1) * 128] for p in parts], axis=1)
            for c in range(8)
        ],
        axis=0,
    )
    rhs = jnp.concatenate([hot, hot, hot], axis=0)
    wide = jnp.dot(lhs, rhs, preferred_element_type=F32)
    total = None
    for c in range(8):
        term = jnp.where(high == c, wide[c * rows : (c + 1) * rows], 0.0)
        total = term if total is None else total + term
    return total


def add_columns(values, idx, hot):
    rows = values.shape[0]
    high = idx >> 7
    masked = jnp.concatenate([jnp.where(high == c, values, 0.0) for c in range(8)], axis=0)
    lhs = jnp.concatenate(split(masked, 3), axis=1)
    rhs = jnp.concatenate([hot, hot, hot], axis=1)
    wide = lax.dot_general(lhs, rhs, (((1,), (1,)), ((), ())), preferred_element_type=F32)
    return jnp.concatenate([wide[c * rows : (c + 1) * rows] for c in range(8)], axis=1)


def pack_peers(table):
    pieces = [table[:, k * PEERS : (k + 1) * PEERS] for k in range(CAP)]
    return jnp.concatenate(pieces, axis=0).T.reshape(2 * PEERS, 128)


def unpack_peers(block):
    flat = block.reshape(PEERS, 256).T
    return jnp.concatenate([flat[k * ROWS : (k + 1) * ROWS] for k in range(CAP)], axis=1)


def slots_by_rank(slots):
    source = lax.broadcasted_iota(I32, (128, LOCAL), 0)
    col = lax.broadcasted_iota(I32, (128, LOCAL), 1)
    pick = jnp.where(source == (col & 7) * 16 + (col >> 6), 1.0, 0.0).astype(BF16)
    upper = jnp.dot((slots >> 5).astype(F32).astype(BF16), pick, preferred_element_type=F32)
    lower = jnp.dot((slots & 31).astype(F32).astype(BF16), pick, preferred_element_type=F32)
    wide = upper * 32.0 + lower
    row = lax.broadcasted_iota(I32, (8, LOCAL), 0)
    column = lax.broadcasted_iota(I32, (8, LOCAL), 1)
    kept = jnp.where(row == ((column >> 3) & 7), wide, 0.0)
    return jnp.sum(kept, axis=0, keepdims=True).astype(I32)


def covariance(log_scale, quat):
    norm = jnp.sqrt(quat[0] * quat[0] + quat[1] * quat[1] + quat[2] * quat[2] + quat[3] * quat[3])
    quat_w, quat_x, quat_y, quat_z = [q / norm for q in quat]
    orient = [
        [
            1.0 - 2.0 * (quat_y * quat_y + quat_z * quat_z),
            2.0 * (quat_x * quat_y - quat_w * quat_z),
            2.0 * (quat_x * quat_z + quat_w * quat_y),
        ],
        [
            2.0 * (quat_x * quat_y + quat_w * quat_z),
            1.0 - 2.0 * (quat_x * quat_x + quat_z * quat_z),
            2.0 * (quat_y * quat_z - quat_w * quat_x),
        ],
        [
            2.0 * (quat_x * quat_z - quat_w * quat_y),
            2.0 * (quat_y * quat_z + quat_w * quat_x),
            1.0 - 2.0 * (quat_x * quat_x + quat_y * quat_y),
        ],
    ]
    scales = [jnp.exp(s) for s in log_scale]
    factor = [[orient[i][j] * scales[j] for j in range(3)] for i in range(3)]

    def entry(i, j):
        return (
            factor[i][0] * factor[j][0] + factor[i][1] * factor[j][1] + factor[i][2] * factor[j][2]
        )

    return [entry(0, 0), entry(0, 1), entry(0, 2), entry(1, 1), entry(1, 2), entry(2, 2)]


def harmonics(dir_x, dir_y, dir_z):
    sq_x, sq_y, sq_z = (dir_x * dir_x, dir_y * dir_y, dir_z * dir_z)
    return [
        -SH_ONE * dir_y,
        SH_ONE * dir_z,
        -SH_ONE * dir_x,
        SH_TWO[0] * dir_x * dir_y,
        SH_TWO[1] * dir_y * dir_z,
        SH_TWO[2] * (2.0 * sq_z - sq_x - sq_y),
        SH_TWO[3] * dir_x * dir_z,
        SH_TWO[4] * (sq_x - sq_y),
        SH_THREE[0] * dir_y * (3.0 * sq_x - sq_y),
        SH_THREE[1] * dir_x * dir_y * dir_z,
        SH_THREE[2] * dir_y * (4.0 * sq_z - sq_x - sq_y),
        SH_THREE[3] * dir_z * (2.0 * sq_z - 3.0 * sq_x - 3.0 * sq_y),
        SH_THREE[4] * dir_x * (4.0 * sq_z - sq_x - sq_y),
        SH_THREE[5] * dir_z * (sq_x - sq_y),
        SH_THREE[6] * dir_x * (sq_x - 3.0 * sq_y),
    ]


def view_rows(position, sigma, coeffs, cam):
    rot = [cam[0:3], cam[3:6], cam[6:9]]
    offset = cam[9:12]
    focal_x, focal_y, centre_x, centre_y = cam[12:16]
    cam_x, cam_y, cam_z = [
        rot[i][0] * position[0] + rot[i][1] * position[1] + rot[i][2] * position[2] + offset[i]
        for i in range(3)
    ]
    inverse_z = 1.0 / cam_z
    mean_u = focal_x * cam_x * inverse_z + centre_x
    mean_w = focal_y * cam_y * inverse_z + centre_y
    jac_a0 = focal_x * inverse_z
    jac_a2 = -focal_x * cam_x * inverse_z * inverse_z
    jac_b1 = focal_y * inverse_z
    jac_b2 = -focal_y * cam_y * inverse_z * inverse_z
    row_a = [jac_a0 * rot[0][i] + jac_a2 * rot[2][i] for i in range(3)]
    row_b = [jac_b1 * rot[1][i] + jac_b2 * rot[2][i] for i in range(3)]
    full = [
        [sigma[0], sigma[1], sigma[2]],
        [sigma[1], sigma[3], sigma[4]],
        [sigma[2], sigma[4], sigma[5]],
    ]

    def through(row):
        return [full[i][0] * row[0] + full[i][1] * row[1] + full[i][2] * row[2] for i in range(3)]

    def dot3(left, right):
        return left[0] * right[0] + left[1] * right[1] + left[2] * right[2]

    sigma_a = through(row_a)
    sigma_b = through(row_b)
    cov_aa = dot3(row_a, sigma_a) + 0.3
    cov_ab = dot3(row_a, sigma_b)
    cov_bb = dot3(row_b, sigma_b) + 0.3
    determinant = cov_aa * cov_bb - cov_ab * cov_ab
    inverse_det = 1.0 / determinant
    ray = [
        position[i] + (rot[0][i] * offset[0] + rot[1][i] * offset[1] + rot[2][i] * offset[2])
        for i in range(3)
    ]
    inverse_norm = 1.0 / jnp.sqrt(dot3(ray, ray))
    basis = harmonics(*[r * inverse_norm for r in ray])
    colours = []
    for channel in range(3):
        total = SH_ZERO * coeffs[channel]
        for index in range(15):
            total = total + basis[index] * coeffs[3 + 3 * index + channel]
        colours.append(jnp.maximum(total + 0.5, 0.0))
    return [
        mean_u,
        mean_w,
        cov_bb * inverse_det,
        -cov_ab * inverse_det,
        cov_aa * inverse_det,
    ] + colours


def send_kernel(
    params_hbm,
    slots_hbm,
    camera_hbm,
    lists_hbm,
    tiles_hbm,
    target_hbm,
    out_ref,
    order_ref,
    entries_ref,
    corner_ref,
    target_ref,
    params_ref,
    slots_ref,
    lists_ref,
    camera_ref,
    tiles_ref,
    sems,
):
    pairs = (
        (slots_hbm, slots_ref),
        (params_hbm, params_ref),
        (camera_hbm, camera_ref),
        (lists_hbm, lists_ref),
        (tiles_hbm, tiles_ref),
        (target_hbm, target_ref),
    )
    copies = [pltpu.make_async_copy(a, b, sems.at[i]) for i, (a, b) in enumerate(pairs)]
    for copy in copies:
        copy.start()
    copies[0].wait()
    order = slots_by_rank(slots_ref[...])
    order_ref[...] = order
    hot = low_onehot(order)
    copies[1].wait()
    copies[2].wait()
    dense = params_ref[...].reshape(59, 8, 128)
    rows = [dense[i] for i in range(59)]
    cam = [camera_ref[0, i] for i in range(16)]
    sigma = covariance(rows[3:6], rows[6:10])
    seen = view_rows(rows[0:3], sigma, rows[11:59], cam)
    opacity = 1.0 / (1.0 + jnp.exp(-rows[10]))
    listed = seen[0:5] + [opacity] + seen[5:8]
    blank = jnp.zeros((8, 128), F32)
    table = jnp.stack(listed + [blank] * (ROWS - 9)).reshape(ROWS, LOCAL)
    out_ref[...] = pack_peers(take_columns(table, order, hot))
    copies[3].wait()
    entries_ref[...] = jnp.concatenate([lists_ref[0, i : i + 1] for i in range(TILES)], axis=1)
    copies[4].wait()
    for tile in range(TILES):
        number = tiles_ref[0, tile]
        corner_ref[tile : tile + 1, :] = jnp.full(
            (1, 256), ((number & (ACROSS - 1)) * 16).astype(F32)
        )
        corner_ref[TILES + tile : TILES + tile + 1, :] = jnp.full(
            (1, 256), ((number >> 4) * 16).astype(F32)
        )
    copies[5].wait()


def render_kernel(recv_ref, entries_ref, corner_ref, target_ref, out_ref, alpha_ref, grad_ref):
    table = unpack_peers(recv_ref[...])
    entries = entries_ref[...]
    idx = jnp.where(entries < 0, -1, (entries & 15) * PEERS + (entries >> 4))
    hot = low_onehot(idx)
    listed = take_columns(table, idx, hot)
    iota_r = lax.broadcasted_iota(I32, (256, 256), 0)
    iota_c = lax.broadcasted_iota(I32, (256, 256), 1)
    before_mask = jnp.where(iota_r < iota_c, 1.0, 0.0).astype(BF16)
    after_mask = jnp.where(iota_r > iota_c, 1.0, 0.0).astype(BF16)
    steps = lax.broadcasted_iota(I32, (16, 256), 0).astype(F32)
    results = []
    for tile in range(TILES):
        here = listed[:, tile * 256 : (tile + 1) * 256]
        left = corner_ref[tile : tile + 1]
        top = corner_ref[TILES + tile : TILES + tile + 1]
        con_a, con_b, con_c, opacity = here[2:3], here[3:4], here[4:5], here[5:6]
        off_u = (steps + left + 0.5) - here[0:1]
        off_w = (steps + top + 0.5) - here[1:2]
        quad_u = -0.5 * con_a * off_u * off_u
        cross = -con_b * off_u
        quad_w = -0.5 * con_c * off_w * off_w
        for j in range(16):
            exponent = quad_u + quad_w[j : j + 1] + cross * off_w[j : j + 1]
            alpha_ref[j * 16 : (j + 1) * 16, :] = opacity * jnp.exp(exponent)
        alpha = alpha_ref[...]
        keep = 1.0 - alpha
        logs = split(jnp.log(keep), 2)
        before = jnp.dot(logs[0], before_mask, preferred_element_type=F32) + jnp.dot(
            logs[1], before_mask, preferred_element_type=F32
        )
        weight = jnp.exp(before) * alpha
        weights = split(weight, 2)
        colour = here[6:9]
        colour_parts = split(colour, 3)
        stacked = jnp.concatenate(
            [p.astype(F32) for p in colour_parts] + [jnp.zeros((7, 256), F32)], axis=0
        ).astype(BF16)
        nt = (((1,), (1,)), ((), ()))
        summed = lax.dot_general(
            stacked, weights[0], nt, preferred_element_type=F32
        ) + lax.dot_general(stacked, weights[1], nt, preferred_element_type=F32)
        rendered = summed[0:3] + summed[3:6] + summed[6:9]
        residual = rendered - target_ref[:, tile]
        residual_parts = [p.astype(F32) for p in split(residual, 3)]
        colour_wide = [p.astype(F32) for p in colour_parts]
        pairs = ((0, 0), (0, 1), (1, 0), (1, 1), (0, 2), (2, 0))
        blank = jnp.zeros((14, 256), F32)
        left_side = jnp.concatenate([residual_parts[a] for a, _ in pairs] + [blank], axis=0)
        right_side = jnp.concatenate([colour_wide[b] for _, b in pairs] + [blank], axis=0)
        pull = lax.dot_general(
            left_side.astype(BF16),
            right_side.astype(BF16),
            (((0,), (0,)), ((), ())),
            preferred_element_type=F32,
        )
        weighted = pull * weight
        flows = split(weighted, 2)
        after = jnp.dot(flows[0], after_mask, preferred_element_type=F32) + jnp.dot(
            flows[1], after_mask, preferred_element_type=F32
        )
        grad_ref[...] = weighted - after * (alpha / keep)
        stacked_res = jnp.concatenate(residual_parts + [jnp.zeros((7, 256), F32)], axis=0).astype(
            BF16
        )
        colour_sum = jnp.dot(stacked_res, weights[0], preferred_element_type=F32) + jnp.dot(
            stacked_res, weights[1], preferred_element_type=F32
        )
        colour_grad = colour_sum[0:3] + colour_sum[3:6] + colour_sum[6:9]
        zeroth = first = second = None
        for j in range(16):
            piece = grad_ref[j * 16 : (j + 1) * 16, :]
            lifted = piece * off_w[j : j + 1]
            twice = lifted * off_w[j : j + 1]
            zeroth = piece if zeroth is None else zeroth + piece
            first = lifted if first is None else first + lifted
            second = twice if second is None else second + twice

        def over(values):
            return jnp.sum(values, axis=0, keepdims=True)

        along = zeroth * off_u
        m_00, m_10, m_20 = over(zeroth), over(along), over(along * off_u)
        m_01, m_11, m_02 = over(first), over(first * off_u), over(second)
        results.append(
            jnp.concatenate(
                [
                    con_a * m_10 + con_b * m_01,
                    con_c * m_01 + con_b * m_10,
                    -0.5 * m_20,
                    -m_11,
                    -0.5 * m_02,
                    m_00,
                    colour_grad,
                    jnp.zeros((ROWS - 9, 256), F32),
                ],
                axis=0,
            )
        )
    grads = jnp.concatenate(results, axis=1)
    out_ref[...] = pack_peers(add_columns(grads, idx, hot))


def owner_kernel(recv_ref, order_ref, camera_ref, out_ref):
    values = unpack_peers(recv_ref[...])
    order = order_ref[...]
    out_ref[...] = add_columns(values, order, low_onehot(order))
    for i in range(16):
        out_ref[9 + i // 8 : 10 + i // 8, (i % 8) * 128 : (i % 8 + 1) * 128] = jnp.full(
            (1, 128), camera_ref[0, i], F32
        )


def pairs_by_rank(pairs):
    source = lax.broadcasted_iota(I32, (128, 128), 0)
    col = lax.broadcasted_iota(I32, (128, 128), 1)
    pick = jnp.where(source == (col & (PEERS - 1)) * 2 + (col >> 6), 1.0, 0.0).astype(BF16)
    wide = jnp.broadcast_to(pairs + 1, (8, 128))
    upper = jnp.dot((wide >> 5).astype(F32).astype(BF16), pick, preferred_element_type=F32)
    lower = jnp.dot((wide & 31).astype(F32).astype(BF16), pick, preferred_element_type=F32)
    return (upper * 32.0 + lower)[0:1].astype(I32) - 1


def log_one_plus(t):
    s = t / (2.0 + t)
    square = s * s
    total = jnp.full_like(s, 1.0 / 17.0)
    for odd in (15, 13, 11, 9, 7, 5, 3, 1):
        total = total * square + 1.0 / odd
    return 2.0 * s * total


def one_minus_exp(x):
    small = jnp.ones_like(x)
    for n in range(10, 1, -1):
        small = 1.0 + small * x * (1.0 / n)
    return jnp.where(x > -0.5, -x * small, 1.0 - jnp.exp(x))


def rates_column():
    row = lax.broadcasted_iota(I32, (59, 1), 0)
    rate = jnp.where(row < 14, 0.0025, 0.000125)
    rate = jnp.where(row < 11, 0.05, rate)
    rate = jnp.where(row < 10, 0.001, rate)
    rate = jnp.where(row < 6, 0.005, rate)
    return jnp.where(row < 3, 0.00016, rate)


def tree_sum(values):
    return (values[0] + values[1]) + (values[2] + values[3])


def step_kernel(
    params_ref,
    first_ref,
    second_ref,
    own_ref,
    near_ref,
    far_ref,
    last_ref,
    sources_ref,
    targets_ref,
    spread_ref,
    new_first_ref,
    new_second_ref,
    gradient_ref,
    out_ref,
):
    dense = params_ref[...].reshape(59, 8, 128)
    rows = [dense[i] for i in range(59)]
    sigma, pull_sigma = jax.vjp(covariance, rows[3:6], rows[6:10])
    position, coeffs = rows[0:3], rows[11:59]
    pos_parts, sigma_parts, coeff_parts, opacity_parts = [], [], [], []
    for ref in (own_ref, near_ref, far_ref, last_ref):
        got = ref[...].reshape(ROWS, 8, 128)
        cam = [jnp.broadcast_to(got[9 + i // 8, i % 8 : i % 8 + 1, :], (8, 128)) for i in range(16)]
        _, pull = jax.vjp(lambda p, s, c: view_rows(p, s, c, cam), position, sigma, coeffs)
        d_pos, d_sigma, d_coeff = pull([got[i] for i in (0, 1, 2, 3, 4, 6, 7, 8)])
        pos_parts.append(d_pos)
        sigma_parts.append(d_sigma)
        coeff_parts.append(d_coeff)
        opacity_parts.append(got[5])
    d_pos = [tree_sum([p[i] for p in pos_parts]) for i in range(3)]
    d_sigma = [tree_sum([p[i] for p in sigma_parts]) for i in range(6)]
    d_coeff = [tree_sum([p[i] for p in coeff_parts]) for i in range(48)]
    d_scale, d_quat = pull_sigma(d_sigma)
    opacity = 1.0 / (1.0 + jnp.exp(-rows[10]))
    d_logit = tree_sum(opacity_parts) * (1.0 - opacity)
    gradient = jnp.stack(d_pos + list(d_scale) + list(d_quat) + [d_logit] + d_coeff).reshape(
        59, LOCAL
    )
    gradient_ref[...] = gradient
    first = 0.9 * first_ref[...] + 0.1 * gradient
    second = 0.999 * second_ref[...] + 0.001 * gradient * gradient
    stepped = params_ref[...] - rates_column() * (first / BIAS_ONE) / (
        jnp.sqrt(second / BIAS_TWO) + 1e-15
    )
    sources = pairs_by_rank(sources_ref[...])
    targets = pairs_by_rank(targets_ref[...])
    ones = jnp.ones((8, 128), F32)
    source_hot = low_onehot(sources)
    counts = add_columns(ones, sources, source_hot)[0:1]
    landing = add_columns(ones, targets, low_onehot(targets))[0:1]
    sampled = counts > 0.5
    cleared = (counts + landing) > 0.5
    logit = stepped[10:11]
    soft = jnp.maximum(logit, 0.0) + log_one_plus(jnp.exp(-jnp.abs(logit)))
    share = -soft / (counts + 1.0)
    shared_logit = jnp.log(one_minus_exp(share)) - share
    row = lax.broadcasted_iota(I32, (59, LOCAL), 0)
    spread = jnp.where((row == 10) & sampled, shared_logit, stepped)
    spread_ref[...] = spread
    new_first_ref[...] = jnp.where(cleared, 0.0, first)
    new_second_ref[...] = jnp.where(cleared, 0.0, second)
    table = jnp.concatenate([spread, jnp.ones((5, LOCAL), F32)], axis=0)
    moved = take_columns(table, sources, source_hot)
    out_ref[...] = jnp.concatenate([moved[:, 0:PEERS], moved[:, PEERS : 2 * PEERS]], axis=0).T


def landing_kernel(recv_ref, targets_ref, spread_ref, out_ref):
    flat = recv_ref[...].T
    moved = jnp.concatenate([flat[0:64], flat[64:128]], axis=1)
    targets = pairs_by_rank(targets_ref[...])
    placed = add_columns(moved, targets, low_onehot(targets))
    out_ref[...] = jnp.where(placed[59:60] > 0.5, placed[0:59], spread_ref[...])


def call(kernel, shapes, ins, scratch=()):
    spec = {
        "v": pl.BlockSpec(memory_space=pltpu.VMEM),
        "s": pl.BlockSpec(memory_space=pltpu.SMEM),
        "h": pl.BlockSpec(memory_space=pltpu.HBM),
    }
    out_shape = [jax.ShapeDtypeStruct(shape, dtype) for shape, dtype in shapes]
    return pl.pallas_call(
        kernel,
        out_shape=out_shape,
        in_specs=[spec[kind] for kind in ins],
        out_specs=[spec["v"]] * len(out_shape),
        scratch_shapes=list(scratch),
        compiler_params=pltpu.CompilerParams(vmem_limit_bytes=VMEM_LIMIT),
    )


def in_hbm(array):
    return pltpu.with_memory_space_constraint(array, pltpu.HBM)


def exchange(block):
    parts = block.reshape(PEERS, -1, 128)
    got = lax.all_to_all(parts, "gauss", split_axis=0, concat_axis=0, tiled=True)
    return got.reshape(block.shape)


def shards(
    params,
    first_moment,
    second_moment,
    cameras,
    target,
    tile_index,
    tile_lists,
    send_slots,
    reloc_send,
    reloc_recv,
):
    packed = ((2 * PEERS, 128), F32)
    outgoing, order, entries, corners, wanted = call(
        send_kernel,
        [
            packed,
            ((1, LOCAL), I32),
            ((1, LOCAL), I32),
            ((2 * TILES, 256), F32),
            ((3, TILES, 256), F32),
        ],
        "hhhhhh",
        [
            pltpu.VMEM((59, LOCAL), F32),
            pltpu.VMEM((8, 128), I32),
            pltpu.VMEM((1, TILES, 256), I32),
            pltpu.SMEM((1, 16), F32),
            pltpu.SMEM((1, TILES), I32),
            pltpu.SemaphoreType.DMA((6,)),
        ],
    )(
        in_hbm(params),
        in_hbm(send_slots.reshape(8, 128)),
        in_hbm(cameras),
        in_hbm(tile_lists),
        in_hbm(tile_index),
        in_hbm(jnp.transpose(target[0], (1, 0, 2))),
    )
    received = exchange(outgoing)
    (row_grads,) = call(
        render_kernel,
        [packed],
        "vvvv",
        [pltpu.VMEM((256, 256), F32), pltpu.VMEM((256, 256), F32)],
    )(received, entries, corners, wanted)
    returned = exchange(row_grads)
    (own,) = call(owner_kernel, [((ROWS, LOCAL), F32)], "vvs")(returned, order, cameras)
    others = [
        lax.ppermute(own, "view", [(i, i ^ flip) for i in range(VIEWS)]) for flip in (1, 2, 3)
    ]
    whole = ((59, LOCAL), F32)
    spread, new_first, new_second, gradient, moving = call(
        step_kernel, [whole, whole, whole, whole, ((PEERS, 128), F32)], "vvvvvvvvv"
    )(params, first_moment, second_moment, own, *others, reloc_send, reloc_recv)
    arrived = exchange(moving)
    (new_params,) = call(landing_kernel, [whole], "vvv")(arrived, reloc_recv, spread)
    return (new_params, new_first, new_second, gradient)


def solution(mesh):
    in_specs = (
        P(None, "gauss"),
        P(None, "gauss"),
        P(None, "gauss"),
        P("view", None),
        P("view", "gauss", None, None),
        P("view", "gauss"),
        P("view", "gauss", None),
        P("view", "gauss", None),
        P("gauss", None),
        P("gauss", None),
    )
    out_specs = (P(None, "gauss"), P(None, "gauss"), P(None, "gauss"), P(None, "gauss"))
    return jax.shard_map(shards, mesh=mesh, in_specs=in_specs, out_specs=out_specs, check_vma=False)
```

```python
import math

import jax
import jax.numpy as jnp
from jax import lax
from jax.experimental import pallas as pl
from jax.experimental.pallas import tpu as pltpu
from jax.sharding import PartitionSpec as P

F32 = jnp.float32
BF16 = jnp.bfloat16
I32 = jnp.int32
PEERS = 64
LOCAL = 1024
CAP = 16
VIEWS = 4
TILES = 4
ACROSS = 16
ROWS = 16
SHARE = 48
BLOCKS = 11
AT_CAMERA = 72
AT_MOVED = 88
AT_SHARE = 104
SENT = 152

SH_ZERO = 0.28209479177387814
SH_ONE = 0.4886025119029199
SH_TWO = (
    1.0925484305920792,
    -1.0925484305920792,
    0.31539156525252005,
    -1.0925484305920792,
    0.5462742152960396,
)
SH_THREE = (
    -0.5900435899266435,
    2.890611442640554,
    -0.4570457994644658,
    0.3731763325901154,
    -0.4570457994644658,
    1.445305721320277,
    -0.5900435899266435,
)
BIAS_ONE = 1.0 - math.exp(1000.0 * math.log(0.9))
BIAS_TWO = 1.0 - math.exp(1000.0 * math.log(0.999))
VMEM_LIMIT = 16 * 1024 * 1024


def split(x, parts):
    out = []
    for index in range(parts):
        piece = x.astype(BF16)
        out.append(piece)
        if index + 1 < parts:
            x = x - piece.astype(F32)
    return out


def low_onehot(idx):
    lane = lax.broadcasted_iota(I32, (128, idx.shape[1]), 0)
    return jnp.where(lane == (idx & 127), 1.0, 0.0).astype(BF16)


def take_columns(table, idx, hot):
    rows = table.shape[0]
    high = idx >> 7
    parts = split(table, 3)
    lhs = jnp.concatenate(
        [
            jnp.concatenate([p[:, c * 128 : (c + 1) * 128] for p in parts], axis=1)
            for c in range(8)
        ],
        axis=0,
    )
    rhs = jnp.concatenate([hot, hot, hot], axis=0)
    wide = jnp.dot(lhs, rhs, preferred_element_type=F32)
    total = None
    for c in range(8):
        term = jnp.where(high == c, wide[c * rows : (c + 1) * rows], 0.0)
        total = term if total is None else total + term
    return total


def add_columns(values, idx, hot):
    rows = values.shape[0]
    high = idx >> 7
    masked = jnp.concatenate([jnp.where(high == c, values, 0.0) for c in range(8)], axis=0)
    lhs = jnp.concatenate(split(masked, 3), axis=1)
    rhs = jnp.concatenate([hot, hot, hot], axis=1)
    wide = lax.dot_general(lhs, rhs, (((1,), (1,)), ((), ())), preferred_element_type=F32)
    return jnp.concatenate([wide[c * rows : (c + 1) * rows] for c in range(8)], axis=1)


def pack_peers(table):
    pieces = [table[:, k * PEERS : (k + 1) * PEERS] for k in range(CAP)]
    return jnp.concatenate(pieces, axis=0).T


def unpack_peers(block):
    flat = block.T
    return jnp.concatenate([flat[k * 8 : (k + 1) * 8] for k in range(CAP)], axis=1)


def slots_by_rank(slots):
    source = lax.broadcasted_iota(I32, (128, LOCAL), 0)
    col = lax.broadcasted_iota(I32, (128, LOCAL), 1)
    pick = jnp.where(source == (col & 7) * 16 + (col >> 6), 1.0, 0.0).astype(BF16)
    upper = jnp.dot((slots >> 5).astype(F32).astype(BF16), pick, preferred_element_type=F32)
    lower = jnp.dot((slots & 31).astype(F32).astype(BF16), pick, preferred_element_type=F32)
    wide = upper * 32.0 + lower
    row = lax.broadcasted_iota(I32, (8, LOCAL), 0)
    column = lax.broadcasted_iota(I32, (8, LOCAL), 1)
    kept = jnp.where(row == ((column >> 3) & 7), wide, 0.0)
    return jnp.sum(kept, axis=0, keepdims=True).astype(I32)


def pairs_by_rank(pairs):
    source = lax.broadcasted_iota(I32, (128, 128), 0)
    col = lax.broadcasted_iota(I32, (128, 128), 1)
    pick = jnp.where(source == (col & (PEERS - 1)) * 2 + (col >> 6), 1.0, 0.0).astype(BF16)
    wide = jnp.broadcast_to(pairs + 1, (8, 128))
    upper = jnp.dot((wide >> 5).astype(F32).astype(BF16), pick, preferred_element_type=F32)
    lower = jnp.dot((wide & 31).astype(F32).astype(BF16), pick, preferred_element_type=F32)
    return (upper * 32.0 + lower)[0:1].astype(I32) - 1


def covariance(log_scale, quat):
    norm = jnp.sqrt(quat[0] * quat[0] + quat[1] * quat[1] + quat[2] * quat[2] + quat[3] * quat[3])
    quat_w, quat_x, quat_y, quat_z = [q / norm for q in quat]
    orient = [
        [
            1.0 - 2.0 * (quat_y * quat_y + quat_z * quat_z),
            2.0 * (quat_x * quat_y - quat_w * quat_z),
            2.0 * (quat_x * quat_z + quat_w * quat_y),
        ],
        [
            2.0 * (quat_x * quat_y + quat_w * quat_z),
            1.0 - 2.0 * (quat_x * quat_x + quat_z * quat_z),
            2.0 * (quat_y * quat_z - quat_w * quat_x),
        ],
        [
            2.0 * (quat_x * quat_z - quat_w * quat_y),
            2.0 * (quat_y * quat_z + quat_w * quat_x),
            1.0 - 2.0 * (quat_x * quat_x + quat_y * quat_y),
        ],
    ]
    scales = [jnp.exp(s) for s in log_scale]
    factor = [[orient[i][j] * scales[j] for j in range(3)] for i in range(3)]

    def entry(i, j):
        return (
            factor[i][0] * factor[j][0] + factor[i][1] * factor[j][1] + factor[i][2] * factor[j][2]
        )

    return [entry(0, 0), entry(0, 1), entry(0, 2), entry(1, 1), entry(1, 2), entry(2, 2)]


def harmonics(dir_x, dir_y, dir_z):
    sq_x, sq_y, sq_z = (dir_x * dir_x, dir_y * dir_y, dir_z * dir_z)
    return [
        -SH_ONE * dir_y,
        SH_ONE * dir_z,
        -SH_ONE * dir_x,
        SH_TWO[0] * dir_x * dir_y,
        SH_TWO[1] * dir_y * dir_z,
        SH_TWO[2] * (2.0 * sq_z - sq_x - sq_y),
        SH_TWO[3] * dir_x * dir_z,
        SH_TWO[4] * (sq_x - sq_y),
        SH_THREE[0] * dir_y * (3.0 * sq_x - sq_y),
        SH_THREE[1] * dir_x * dir_y * dir_z,
        SH_THREE[2] * dir_y * (4.0 * sq_z - sq_x - sq_y),
        SH_THREE[3] * dir_z * (2.0 * sq_z - 3.0 * sq_x - 3.0 * sq_y),
        SH_THREE[4] * dir_x * (4.0 * sq_z - sq_x - sq_y),
        SH_THREE[5] * dir_z * (sq_x - sq_y),
        SH_THREE[6] * dir_x * (sq_x - 3.0 * sq_y),
    ]


def view_rows(position, sigma, coeffs, cam):
    rot = [cam[0:3], cam[3:6], cam[6:9]]
    offset = cam[9:12]
    focal_x, focal_y, centre_x, centre_y = cam[12:16]
    cam_x, cam_y, cam_z = [
        rot[i][0] * position[0] + rot[i][1] * position[1] + rot[i][2] * position[2] + offset[i]
        for i in range(3)
    ]
    inverse_z = 1.0 / cam_z
    mean_u = focal_x * cam_x * inverse_z + centre_x
    mean_w = focal_y * cam_y * inverse_z + centre_y
    jac_a0 = focal_x * inverse_z
    jac_a2 = -focal_x * cam_x * inverse_z * inverse_z
    jac_b1 = focal_y * inverse_z
    jac_b2 = -focal_y * cam_y * inverse_z * inverse_z
    row_a = [jac_a0 * rot[0][i] + jac_a2 * rot[2][i] for i in range(3)]
    row_b = [jac_b1 * rot[1][i] + jac_b2 * rot[2][i] for i in range(3)]
    full = [
        [sigma[0], sigma[1], sigma[2]],
        [sigma[1], sigma[3], sigma[4]],
        [sigma[2], sigma[4], sigma[5]],
    ]

    def through(row):
        return [full[i][0] * row[0] + full[i][1] * row[1] + full[i][2] * row[2] for i in range(3)]

    def dot3(left, right):
        return left[0] * right[0] + left[1] * right[1] + left[2] * right[2]

    sigma_a = through(row_a)
    sigma_b = through(row_b)
    cov_aa = dot3(row_a, sigma_a) + 0.3
    cov_ab = dot3(row_a, sigma_b)
    cov_bb = dot3(row_b, sigma_b) + 0.3
    determinant = cov_aa * cov_bb - cov_ab * cov_ab
    inverse_det = 1.0 / determinant
    ray = [
        position[i] + (rot[0][i] * offset[0] + rot[1][i] * offset[1] + rot[2][i] * offset[2])
        for i in range(3)
    ]
    inverse_norm = 1.0 / jnp.sqrt(dot3(ray, ray))
    basis = harmonics(*[r * inverse_norm for r in ray])
    colours = []
    for channel in range(3):
        total = SH_ZERO * coeffs[channel]
        for index in range(15):
            total = total + basis[index] * coeffs[3 + 3 * index + channel]
        colours.append(jnp.maximum(total + 0.5, 0.0))
    return [
        mean_u,
        mean_w,
        cov_bb * inverse_det,
        -cov_ab * inverse_det,
        cov_aa * inverse_det,
    ] + colours


def send_kernel(
    params_hbm,
    first_hbm,
    second_hbm,
    slots_hbm,
    sources_hbm,
    targets_hbm,
    camera_hbm,
    lists_hbm,
    tiles_hbm,
    wanted_hbm,
    out_ref,
    order_ref,
    entries_ref,
    corner_ref,
    wanted_ref,
    counts_ref,
    landing_ref,
    shown_ref,
    params_ref,
    first_ref,
    second_ref,
    slots_ref,
    sources_ref,
    targets_ref,
    camera_ref,
    lists_ref,
    tiles_ref,
    stack_ref,
    sems,
):
    pairs = (
        (slots_hbm, slots_ref),
        (sources_hbm, sources_ref),
        (targets_hbm, targets_ref),
        (camera_hbm, camera_ref),
        (params_hbm, params_ref),
        (first_hbm, first_ref),
        (second_hbm, second_ref),
        (lists_hbm, lists_ref),
        (tiles_hbm, tiles_ref),
        (wanted_hbm, wanted_ref),
    )
    copies = [pltpu.make_async_copy(a, b, sems.at[i]) for i, (a, b) in enumerate(pairs)]
    for copy in copies:
        copy.start()
    copies[0].wait()
    order = slots_by_rank(slots_ref[...])
    order_ref[...] = order
    hot = low_onehot(order)
    copies[1].wait()
    sources = pairs_by_rank(sources_ref[...])
    source_hot = low_onehot(sources)
    counts = add_columns(jnp.ones((8, 128), F32), sources, source_hot)[0:1]
    counts_ref[...] = counts
    out_ref[pl.ds(2, PEERS, stride=3), :] = jnp.broadcast_to(sources.astype(F32), (PEERS, 128))
    copies[2].wait()
    landing_ref[...] = pairs_by_rank(targets_ref[...])
    copies[3].wait()
    copies[4].wait()
    dense = params_ref[...].reshape(59, 8, 128)
    rows = [dense[i] for i in range(59)]
    cam = [camera_ref[0, i] for i in range(16)]
    sigma = covariance(rows[3:6], rows[6:10])
    seen = view_rows(rows[0:3], sigma, rows[11:59], cam)
    opacity = 1.0 / (1.0 + jnp.exp(-rows[10]))
    listed = seen[0:5] + [opacity] + seen[5:8]
    blank = jnp.zeros((8, 128), F32)
    table = jnp.stack(listed + [blank] * (ROWS - 9)).reshape(ROWS, LOCAL)
    taken = take_columns(table, order, hot)
    out_ref[pl.ds(0, PEERS, stride=3), :] = pack_peers(taken[0:8])
    for copy in copies[5:7]:
        copy.wait()
    stack_ref[0:59, :] = params_ref[...]
    stack_ref[59:60, :] = counts
    stack_ref[60:64, :] = jnp.zeros((4, LOCAL), F32)
    stack_ref[64:123, :] = first_ref[...]
    stack_ref[123:128, :] = jnp.zeros((5, LOCAL), F32)
    stack_ref[128:187, :] = second_ref[...]
    stack_ref[187:192, :] = jnp.zeros((5, LOCAL), F32)
    plane = lax.axis_index("view")
    share = stack_ref[pl.ds(pl.multiple_of(plane * SHARE, 8), SHARE), :]
    moved = take_columns(share, sources, source_hot)
    moved = jnp.concatenate([moved[:, 0:PEERS], moved[:, PEERS:]], axis=0)
    numbers = order.astype(F32)
    pieces = []
    for k in range(CAP):
        span = slice(k * PEERS, (k + 1) * PEERS)
        pieces += [taken[8:9, span], numbers[:, span], moved[6 * k : 6 * k + 6]]
    out_ref[pl.ds(1, PEERS, stride=3), :] = jnp.concatenate(pieces, axis=0).T
    copies[7].wait()
    entries_ref[...] = jnp.concatenate([lists_ref[0, i : i + 1] for i in range(TILES)], axis=1)
    copies[8].wait()
    for tile in range(TILES):
        number = tiles_ref[0, tile]
        corner_ref[tile : tile + 1, :] = jnp.full(
            (1, 256), ((number & (ACROSS - 1)) * 16).astype(F32)
        )
        corner_ref[TILES + tile : TILES + tile + 1, :] = jnp.full(
            (1, 256), ((number >> 4) * 16).astype(F32)
        )
    for i in range(16):
        shown_ref[i : i + 1, :] = jnp.full((1, 128), cam[i], F32)
    copies[9].wait()


def render_kernel(
    recv_ref, entries_ref, corner_ref, target_ref, out_ref, share_ref, alpha_ref, grad_ref
):
    lead = recv_ref[pl.ds(0, PEERS, stride=3), :]
    tail = recv_ref[pl.ds(1, PEERS, stride=3), :]
    sources = recv_ref[pl.ds(2, PEERS, stride=3), :]
    flat = tail.T
    mine = jnp.concatenate([flat[8 * k + 2 : 8 * k + 8] for k in range(CAP)], axis=0)
    share_ref[...] = jnp.concatenate([mine[0:SHARE], mine[SHARE:]], axis=1)
    table = jnp.concatenate([unpack_peers(lead), unpack_peers(tail)], axis=0)
    entries = entries_ref[...]
    idx = jnp.where(entries < 0, -1, (entries & 15) * PEERS + (entries >> 4))
    hot = low_onehot(idx)
    listed = take_columns(table, idx, hot)
    iota_r = lax.broadcasted_iota(I32, (256, 256), 0)
    iota_c = lax.broadcasted_iota(I32, (256, 256), 1)
    before_mask = jnp.where(iota_r < iota_c, 1.0, 0.0).astype(BF16)
    after_mask = jnp.where(iota_r > iota_c, 1.0, 0.0).astype(BF16)
    steps = lax.broadcasted_iota(I32, (16, 256), 0).astype(F32)
    results = []
    for tile in range(TILES):
        here = listed[:, tile * 256 : (tile + 1) * 256]
        left = corner_ref[tile : tile + 1]
        top = corner_ref[TILES + tile : TILES + tile + 1]
        con_a, con_b, con_c, opacity = here[2:3], here[3:4], here[4:5], here[5:6]
        off_u = (steps + left + 0.5) - here[0:1]
        off_w = (steps + top + 0.5) - here[1:2]
        quad_u = -0.5 * con_a * off_u * off_u
        cross = -con_b * off_u
        quad_w = -0.5 * con_c * off_w * off_w
        for j in range(16):
            exponent = quad_u + quad_w[j : j + 1] + cross * off_w[j : j + 1]
            alpha_ref[j * 16 : (j + 1) * 16, :] = opacity * jnp.exp(exponent)
        alpha = alpha_ref[...]
        keep = 1.0 - alpha
        logs = split(jnp.log(keep), 2)
        before = jnp.dot(logs[0], before_mask, preferred_element_type=F32) + jnp.dot(
            logs[1], before_mask, preferred_element_type=F32
        )
        weight = jnp.exp(before) * alpha
        weights = split(weight, 2)
        colour = here[6:9]
        colour_parts = split(colour, 3)
        stacked = jnp.concatenate(
            [p.astype(F32) for p in colour_parts] + [jnp.zeros((7, 256), F32)], axis=0
        ).astype(BF16)
        nt = (((1,), (1,)), ((), ()))
        summed = lax.dot_general(
            stacked, weights[0], nt, preferred_element_type=F32
        ) + lax.dot_general(stacked, weights[1], nt, preferred_element_type=F32)
        rendered = summed[0:3] + summed[3:6] + summed[6:9]
        residual = rendered - target_ref[:, tile]
        residual_parts = [p.astype(F32) for p in split(residual, 3)]
        colour_wide = [p.astype(F32) for p in colour_parts]
        pairs = ((0, 0), (0, 1), (1, 0), (1, 1), (0, 2), (2, 0))
        blank = jnp.zeros((14, 256), F32)
        left_side = jnp.concatenate([residual_parts[a] for a, _ in pairs] + [blank], axis=0)
        right_side = jnp.concatenate([colour_wide[b] for _, b in pairs] + [blank], axis=0)
        pull = lax.dot_general(
            left_side.astype(BF16),
            right_side.astype(BF16),
            (((0,), (0,)), ((), ())),
            preferred_element_type=F32,
        )
        weighted = pull * weight
        flows = split(weighted, 2)
        after = jnp.dot(flows[0], after_mask, preferred_element_type=F32) + jnp.dot(
            flows[1], after_mask, preferred_element_type=F32
        )
        grad_ref[...] = weighted - after * (alpha / keep)
        stacked_res = jnp.concatenate(residual_parts + [jnp.zeros((7, 256), F32)], axis=0).astype(
            BF16
        )
        colour_sum = jnp.dot(stacked_res, weights[0], preferred_element_type=F32) + jnp.dot(
            stacked_res, weights[1], preferred_element_type=F32
        )
        colour_grad = colour_sum[0:3] + colour_sum[3:6] + colour_sum[6:9]
        zeroth = first = second = None
        for j in range(16):
            piece = grad_ref[j * 16 : (j + 1) * 16, :]
            lifted = piece * off_w[j : j + 1]
            twice = lifted * off_w[j : j + 1]
            zeroth = piece if zeroth is None else zeroth + piece
            first = lifted if first is None else first + lifted
            second = twice if second is None else second + twice

        def over(values):
            return jnp.sum(values, axis=0, keepdims=True)

        along = zeroth * off_u
        m_00, m_10, m_20 = over(zeroth), over(along), over(along * off_u)
        m_01, m_11, m_02 = over(first), over(first * off_u), over(second)
        results.append(
            jnp.concatenate(
                [
                    con_a * m_10 + con_b * m_01,
                    con_c * m_01 + con_b * m_10,
                    -0.5 * m_20,
                    -m_11,
                    -0.5 * m_02,
                    m_00,
                    colour_grad,
                    jnp.zeros((ROWS - 9, 256), F32),
                ],
                axis=0,
            )
        )
    grads = jnp.concatenate(results, axis=1)
    summed = add_columns(grads, idx, hot)
    packed = [pack_peers(summed[0:8]), pack_peers(summed[8:16])]
    out_ref[pl.ds(0, PEERS, stride=BLOCKS), :] = packed[0]
    out_ref[pl.ds(1, PEERS, stride=BLOCKS), :] = packed[1]
    gathered = [[] for _ in range(9)]
    for group in range(PEERS // 8):
        span = slice(group * 8, (group + 1) * 8)
        wanted = sources[span]
        totals = [None] * 9
        for k in range(CAP):
            same = tail[span, 8 * k + 1 : 8 * k + 2] == wanted
            for row in range(9):
                column = packed[row // 8][span, 8 * k + row % 8 : 8 * k + row % 8 + 1]
                term = jnp.where(same, column, 0.0)
                totals[row] = term if totals[row] is None else totals[row] + term
        for row in range(9):
            gathered[row].append(totals[row])
    for row in range(9):
        turned = jnp.concatenate(gathered[row], axis=0).T
        out_ref[pl.ds(2 + row, PEERS, stride=BLOCKS), :] = jnp.concatenate(
            [turned[0:PEERS], turned[PEERS:]], axis=1
        )


def owner_kernel(recv_ref, order_ref, shown_ref, share_ref, out_ref):
    values = jnp.concatenate(
        [unpack_peers(recv_ref[pl.ds(i, PEERS, stride=BLOCKS), :]) for i in range(2)], axis=0
    )
    order = order_ref[...]
    owned = add_columns(values, order, low_onehot(order))
    out_ref[0:AT_CAMERA, :] = owned[0:9].reshape(9, 8, 128).reshape(AT_CAMERA, 128)
    out_ref[AT_CAMERA:AT_MOVED, :] = shown_ref[...]
    for row in range(9):
        out_ref[AT_MOVED + row : AT_MOVED + row + 1, :] = jnp.sum(
            recv_ref[pl.ds(2 + row, PEERS, stride=BLOCKS), :], axis=0, keepdims=True
        )
    out_ref[AT_MOVED + 9 : AT_SHARE, :] = jnp.zeros((AT_SHARE - AT_MOVED - 9, 128), F32)
    out_ref[AT_SHARE:SENT, :] = share_ref[...]


def log_one_plus(t):
    s = t / (2.0 + t)
    square = s * s
    total = jnp.full_like(s, 1.0 / 17.0)
    for odd in (15, 13, 11, 9, 7, 5, 3, 1):
        total = total * square + 1.0 / odd
    return 2.0 * s * total


def one_minus_exp(x):
    small = jnp.ones_like(x)
    for n in range(10, 1, -1):
        small = 1.0 + small * x * (1.0 / n)
    return jnp.where(x > -0.5, -x * small, 1.0 - jnp.exp(x))


def rates_column():
    row = lax.broadcasted_iota(I32, (59, 1), 0)
    rate = jnp.where(row < 14, 0.0025, 0.000125)
    rate = jnp.where(row < 11, 0.05, rate)
    rate = jnp.where(row < 10, 0.001, rate)
    rate = jnp.where(row < 6, 0.005, rate)
    return jnp.where(row < 3, 0.00016, rate)


def tree_sum(values):
    return (values[0] + values[1]) + (values[2] + values[3])


def adam(params, first_old, second_old, gradient):
    first = 0.9 * first_old + 0.1 * gradient
    second = 0.999 * second_old + 0.001 * gradient * gradient
    stepped = params - rates_column() * (first / BIAS_ONE) / (jnp.sqrt(second / BIAS_TWO) + 1e-15)
    return stepped, first, second


def spread_logit(logit, counts):
    soft = jnp.maximum(logit, 0.0) + log_one_plus(jnp.exp(-jnp.abs(logit)))
    share = -soft / (counts + 1.0)
    return jnp.log(one_minus_exp(share)) - share


def sigmoid_rest(logit):
    return 1.0 - 1.0 / (1.0 + jnp.exp(-logit))


def incoming_columns(parts):
    def stacked(row):
        return jnp.concatenate([ref[row : row + 1, :] for ref in parts], axis=0)

    def folded(x):
        return (x[0:1] + x[1:2]) + (x[2:3] + x[3:4])

    def wide(x):
        return jnp.broadcast_to(x, (VIEWS, 128))

    plane = jnp.full((SHARE, 128), lax.axis_index("view"), I32)
    shares = [ref[AT_SHARE:SENT, :] for ref in parts]
    for bit in (1, 2):
        flip = (plane & bit) > 0
        shares = [jnp.where(flip, shares[i ^ bit], shares[i]) for i in range(VIEWS)]
    stack = jnp.concatenate(shares, axis=0)
    rows = [stack[i : i + 1] for i in range(59)]
    cam = [stacked(AT_CAMERA + i) for i in range(16)]
    sigma, pull_sigma = jax.vjp(covariance, rows[3:6], rows[6:10])
    _, pull = jax.vjp(
        lambda p, s, c: view_rows(p, s, c, cam),
        [wide(x) for x in rows[0:3]],
        [wide(x) for x in sigma],
        [wide(x) for x in rows[11:59]],
    )
    got = [stacked(AT_MOVED + i) for i in range(9)]
    d_pos, d_sigma, d_coeff = pull([got[i] for i in (0, 1, 2, 3, 4, 6, 7, 8)])
    d_scale, d_quat = pull_sigma([folded(x) for x in d_sigma])
    d_logit = folded(got[5]) * sigmoid_rest(rows[10])
    gradient = jnp.concatenate(
        [folded(x) for x in d_pos]
        + list(d_scale)
        + list(d_quat)
        + [d_logit]
        + [folded(x) for x in d_coeff],
        axis=0,
    )
    stepped, _, _ = adam(stack[0:59], stack[64:123], stack[128:187], gradient)
    logit = spread_logit(stepped[10:11], stack[59:60])
    row = lax.broadcasted_iota(I32, (59, 128), 0)
    return jnp.concatenate(
        [jnp.where(row == 10, logit, stepped), jnp.ones((5, 128), F32)], axis=0
    )


def step_kernel(
    params_ref,
    first_ref,
    second_ref,
    own_ref,
    near_ref,
    far_ref,
    last_ref,
    counts_ref,
    targets_ref,
    new_params_ref,
    new_first_ref,
    new_second_ref,
    gradient_ref,
):
    parts = (own_ref, near_ref, far_ref, last_ref)
    targets = targets_ref[...]
    placed = add_columns(incoming_columns(parts), targets, low_onehot(targets))
    dense = params_ref[...].reshape(59, 8, 128)
    rows = [dense[i] for i in range(59)]
    sigma, pull_sigma = jax.vjp(covariance, rows[3:6], rows[6:10])
    position, coeffs = rows[0:3], rows[11:59]
    pos_parts, sigma_parts, coeff_parts, opacity_parts = [], [], [], []
    for ref in parts:
        got = [ref[8 * i : 8 * i + 8, :] for i in range(9)]
        cam = [
            jnp.broadcast_to(ref[AT_CAMERA + i : AT_CAMERA + i + 1, :], (8, 128)) for i in range(16)
        ]
        _, pull = jax.vjp(lambda p, s, c: view_rows(p, s, c, cam), position, sigma, coeffs)
        d_pos, d_sigma, d_coeff = pull([got[i] for i in (0, 1, 2, 3, 4, 6, 7, 8)])
        pos_parts.append(d_pos)
        sigma_parts.append(d_sigma)
        coeff_parts.append(d_coeff)
        opacity_parts.append(got[5])
    d_pos = [tree_sum([p[i] for p in pos_parts]) for i in range(3)]
    d_sigma = [tree_sum([p[i] for p in sigma_parts]) for i in range(6)]
    d_coeff = [tree_sum([p[i] for p in coeff_parts]) for i in range(48)]
    d_scale, d_quat = pull_sigma(d_sigma)
    d_logit = tree_sum(opacity_parts) * sigmoid_rest(rows[10])
    gradient = jnp.stack(d_pos + list(d_scale) + list(d_quat) + [d_logit] + d_coeff).reshape(
        59, LOCAL
    )
    gradient_ref[...] = gradient
    stepped, first, second = adam(params_ref[...], first_ref[...], second_ref[...], gradient)
    counts = counts_ref[...]
    landed = placed[59:60] > 0.5
    cleared = (counts + placed[59:60]) > 0.5
    row = lax.broadcasted_iota(I32, (59, LOCAL), 0)
    spread = jnp.where(
        (row == 10) & (counts > 0.5), spread_logit(stepped[10:11], counts), stepped
    )
    new_params_ref[...] = jnp.where(landed, placed[0:59], spread)
    new_first_ref[...] = jnp.where(cleared, 0.0, first)
    new_second_ref[...] = jnp.where(cleared, 0.0, second)


def call(kernel, shapes, ins, scratch=()):
    spec = {
        "v": pl.BlockSpec(memory_space=pltpu.VMEM),
        "s": pl.BlockSpec(memory_space=pltpu.SMEM),
        "h": pl.BlockSpec(memory_space=pltpu.HBM),
    }
    out_shape = [jax.ShapeDtypeStruct(shape, dtype) for shape, dtype in shapes]
    return pl.pallas_call(
        kernel,
        out_shape=out_shape,
        in_specs=[spec[kind] for kind in ins],
        out_specs=[spec["v"]] * len(out_shape),
        scratch_shapes=list(scratch),
        compiler_params=pltpu.CompilerParams(vmem_limit_bytes=VMEM_LIMIT),
    )


def in_hbm(array):
    return pltpu.with_memory_space_constraint(array, pltpu.HBM)


def exchange(block):
    parts = block.reshape(PEERS, 1, -1)
    got = lax.all_to_all(parts, "gauss", split_axis=0, concat_axis=0, tiled=True)
    return got.reshape(block.shape)


def shards(
    params,
    first_moment,
    second_moment,
    cameras,
    target,
    tile_index,
    tile_lists,
    send_slots,
    reloc_send,
    reloc_recv,
):
    columns = ((1, LOCAL), I32)
    whole = ((59, LOCAL), F32)
    outgoing, order, entries, corners, wanted, counts, landing, shown = call(
        send_kernel,
        [
            ((3 * PEERS, 128), F32),
            columns,
            columns,
            ((2 * TILES, 256), F32),
            ((3, TILES, 256), F32),
            ((1, LOCAL), F32),
            ((1, 128), I32),
            ((16, 128), F32),
        ],
        "hhhhhhhhhh",
        [
            pltpu.VMEM((59, LOCAL), F32),
            pltpu.VMEM((59, LOCAL), F32),
            pltpu.VMEM((59, LOCAL), F32),
            pltpu.VMEM((8, 128), I32),
            pltpu.VMEM((1, 128), I32),
            pltpu.VMEM((1, 128), I32),
            pltpu.SMEM((1, 16), F32),
            pltpu.VMEM((1, TILES, 256), I32),
            pltpu.SMEM((1, TILES), I32),
            pltpu.VMEM((VIEWS * SHARE, LOCAL), F32),
            pltpu.SemaphoreType.DMA((10,)),
        ],
    )(
        in_hbm(params),
        in_hbm(first_moment),
        in_hbm(second_moment),
        in_hbm(send_slots.reshape(8, 128)),
        in_hbm(reloc_send),
        in_hbm(reloc_recv),
        in_hbm(cameras),
        in_hbm(tile_lists),
        in_hbm(tile_index),
        in_hbm(jnp.transpose(target[0], (1, 0, 2))),
    )
    received = exchange(outgoing)
    row_grads, share = call(
        render_kernel,
        [((BLOCKS * PEERS, 128), F32), ((SHARE, 128), F32)],
        "vvvv",
        [pltpu.VMEM((256, 256), F32), pltpu.VMEM((256, 256), F32)],
    )(received, entries, corners, wanted)
    returned = exchange(row_grads)
    (own,) = call(owner_kernel, [((SENT, 128), F32)], "vvvv")(returned, order, shown, share)
    others = [
        lax.ppermute(own, "view", [(i, i ^ flip) for i in range(VIEWS)]) for flip in (1, 2, 3)
    ]
    return call(step_kernel, [whole, whole, whole, whole], "vvvvvvvvv")(
        params, first_moment, second_moment, own, *others, counts, landing
    )


def solution(mesh):
    in_specs = (
        P(None, "gauss"),
        P(None, "gauss"),
        P(None, "gauss"),
        P("view", None),
        P("view", "gauss", None, None),
        P("view", "gauss"),
        P("view", "gauss", None),
        P("view", "gauss", None),
        P("gauss", None),
        P("gauss", None),
    )
    out_specs = (P(None, "gauss"), P(None, "gauss"), P(None, "gauss"), P(None, "gauss"))
    return jax.shard_map(shards, mesh=mesh, in_specs=in_specs, out_specs=out_specs, check_vma=False)
```

```python
import math

import jax
import jax.numpy as jnp
from jax import lax
from jax.experimental import pallas as pl
from jax.experimental.pallas import tpu as pltpu
from jax.sharding import PartitionSpec as P

F32 = jnp.float32
BF16 = jnp.bfloat16
I32 = jnp.int32
PEERS = 64
LOCAL = 1024
CAP = 16
VIEWS = 4
TILES = 4
ACROSS = 16
ROWS = 16
LOG2E = 1.4426950408889634
SHARE = 48
BLOCKS = 11
AT_CAMERA = 72
AT_MOVED = 88
AT_SHARE = 104
SENT = 152

SH_ZERO = 0.28209479177387814
SH_ONE = 0.4886025119029199
SH_TWO = (
    1.0925484305920792,
    -1.0925484305920792,
    0.31539156525252005,
    -1.0925484305920792,
    0.5462742152960396,
)
SH_THREE = (
    -0.5900435899266435,
    2.890611442640554,
    -0.4570457994644658,
    0.3731763325901154,
    -0.4570457994644658,
    1.445305721320277,
    -0.5900435899266435,
)
BIAS_ONE = 1.0 - math.exp(1000.0 * math.log(0.9))
BIAS_TWO = 1.0 - math.exp(1000.0 * math.log(0.999))
VMEM_LIMIT = 16 * 1024 * 1024


def split(x, parts):
    out = []
    for index in range(parts):
        piece = x.astype(BF16)
        out.append(piece)
        if index + 1 < parts:
            x = x - piece.astype(F32)
    return out


def low_onehot(idx):
    lane = lax.broadcasted_iota(I32, (128, idx.shape[1]), 0)
    return jnp.where(lane == (idx & 127), 1.0, 0.0).astype(BF16)


def take_columns(table, idx, hot):
    rows = table.shape[0]
    high = idx >> 7
    parts = split(table, 3)
    lhs = jnp.concatenate(
        [
            jnp.concatenate([p[:, c * 128 : (c + 1) * 128] for p in parts], axis=1)
            for c in range(8)
        ],
        axis=0,
    )
    rhs = jnp.concatenate([hot, hot, hot], axis=0)
    wide = jnp.dot(lhs, rhs, preferred_element_type=F32)
    total = None
    for c in range(8):
        term = jnp.where(high == c, wide[c * rows : (c + 1) * rows], 0.0)
        total = term if total is None else total + term
    return total


def add_columns(values, idx, hot, parts=3):
    rows = values.shape[0]
    high = idx >> 7
    pieces = []
    for piece in split(values, parts):
        piece = piece.astype(F32)
        pieces += [jnp.where(high == c, piece, 0.0) for c in range(8)]
    lhs = jnp.concatenate(pieces, axis=0).astype(BF16)
    wide = lax.dot_general(lhs, hot, (((1,), (1,)), ((), ())), preferred_element_type=F32)
    size = 8 * rows
    wide = sum(wide[i * size : (i + 1) * size] for i in range(1, parts)) + wide[0:size]
    return jnp.concatenate([wide[c * rows : (c + 1) * rows] for c in range(8)], axis=1)


def pack_peers(table):
    pieces = [table[:, k * PEERS : (k + 1) * PEERS] for k in range(CAP)]
    return jnp.concatenate(pieces, axis=0).T


def unpack_peers(block):
    flat = block.T
    return jnp.concatenate([flat[k * 8 : (k + 1) * 8] for k in range(CAP)], axis=1)


def slots_by_rank(slots):
    source = lax.broadcasted_iota(I32, (128, LOCAL), 0)
    col = lax.broadcasted_iota(I32, (128, LOCAL), 1)
    pick = jnp.where(source == (col & 7) * 16 + (col >> 6), 1.0, 0.0).astype(BF16)
    upper = jnp.dot((slots >> 5).astype(F32).astype(BF16), pick, preferred_element_type=F32)
    lower = jnp.dot((slots & 31).astype(F32).astype(BF16), pick, preferred_element_type=F32)
    wide = upper * 32.0 + lower
    row = lax.broadcasted_iota(I32, (8, LOCAL), 0)
    column = lax.broadcasted_iota(I32, (8, LOCAL), 1)
    kept = jnp.where(row == ((column >> 3) & 7), wide, 0.0)
    return jnp.sum(kept, axis=0, keepdims=True).astype(I32)


def pairs_by_rank(pairs):
    source = lax.broadcasted_iota(I32, (128, 128), 0)
    col = lax.broadcasted_iota(I32, (128, 128), 1)
    pick = jnp.where(source == (col & (PEERS - 1)) * 2 + (col >> 6), 1.0, 0.0).astype(BF16)
    wide = jnp.broadcast_to(pairs + 1, (8, 128))
    upper = jnp.dot((wide >> 5).astype(F32).astype(BF16), pick, preferred_element_type=F32)
    lower = jnp.dot((wide & 31).astype(F32).astype(BF16), pick, preferred_element_type=F32)
    return (upper * 32.0 + lower)[0:1].astype(I32) - 1


def covariance(log_scale, quat):
    norm = jnp.sqrt(quat[0] * quat[0] + quat[1] * quat[1] + quat[2] * quat[2] + quat[3] * quat[3])
    quat_w, quat_x, quat_y, quat_z = [q / norm for q in quat]
    orient = [
        [
            1.0 - 2.0 * (quat_y * quat_y + quat_z * quat_z),
            2.0 * (quat_x * quat_y - quat_w * quat_z),
            2.0 * (quat_x * quat_z + quat_w * quat_y),
        ],
        [
            2.0 * (quat_x * quat_y + quat_w * quat_z),
            1.0 - 2.0 * (quat_x * quat_x + quat_z * quat_z),
            2.0 * (quat_y * quat_z - quat_w * quat_x),
        ],
        [
            2.0 * (quat_x * quat_z - quat_w * quat_y),
            2.0 * (quat_y * quat_z + quat_w * quat_x),
            1.0 - 2.0 * (quat_x * quat_x + quat_y * quat_y),
        ],
    ]
    scales = [jnp.exp(s) for s in log_scale]
    factor = [[orient[i][j] * scales[j] for j in range(3)] for i in range(3)]

    def entry(i, j):
        return (
            factor[i][0] * factor[j][0] + factor[i][1] * factor[j][1] + factor[i][2] * factor[j][2]
        )

    return [entry(0, 0), entry(0, 1), entry(0, 2), entry(1, 1), entry(1, 2), entry(2, 2)]


def harmonics(dir_x, dir_y, dir_z):
    sq_x, sq_y, sq_z = (dir_x * dir_x, dir_y * dir_y, dir_z * dir_z)
    return [
        -SH_ONE * dir_y,
        SH_ONE * dir_z,
        -SH_ONE * dir_x,
        SH_TWO[0] * dir_x * dir_y,
        SH_TWO[1] * dir_y * dir_z,
        SH_TWO[2] * (2.0 * sq_z - sq_x - sq_y),
        SH_TWO[3] * dir_x * dir_z,
        SH_TWO[4] * (sq_x - sq_y),
        SH_THREE[0] * dir_y * (3.0 * sq_x - sq_y),
        SH_THREE[1] * dir_x * dir_y * dir_z,
        SH_THREE[2] * dir_y * (4.0 * sq_z - sq_x - sq_y),
        SH_THREE[3] * dir_z * (2.0 * sq_z - 3.0 * sq_x - 3.0 * sq_y),
        SH_THREE[4] * dir_x * (4.0 * sq_z - sq_x - sq_y),
        SH_THREE[5] * dir_z * (sq_x - sq_y),
        SH_THREE[6] * dir_x * (sq_x - 3.0 * sq_y),
    ]


def view_rows(position, sigma, coeffs, cam):
    rot = [cam[0:3], cam[3:6], cam[6:9]]
    offset = cam[9:12]
    focal_x, focal_y, centre_x, centre_y = cam[12:16]
    cam_x, cam_y, cam_z = [
        rot[i][0] * position[0] + rot[i][1] * position[1] + rot[i][2] * position[2] + offset[i]
        for i in range(3)
    ]
    inverse_z = 1.0 / cam_z
    mean_u = focal_x * cam_x * inverse_z + centre_x
    mean_w = focal_y * cam_y * inverse_z + centre_y
    jac_a0 = focal_x * inverse_z
    jac_a2 = -focal_x * cam_x * inverse_z * inverse_z
    jac_b1 = focal_y * inverse_z
    jac_b2 = -focal_y * cam_y * inverse_z * inverse_z
    row_a = [jac_a0 * rot[0][i] + jac_a2 * rot[2][i] for i in range(3)]
    row_b = [jac_b1 * rot[1][i] + jac_b2 * rot[2][i] for i in range(3)]
    full = [
        [sigma[0], sigma[1], sigma[2]],
        [sigma[1], sigma[3], sigma[4]],
        [sigma[2], sigma[4], sigma[5]],
    ]

    def through(row):
        return [full[i][0] * row[0] + full[i][1] * row[1] + full[i][2] * row[2] for i in range(3)]

    def dot3(left, right):
        return left[0] * right[0] + left[1] * right[1] + left[2] * right[2]

    sigma_a = through(row_a)
    sigma_b = through(row_b)
    cov_aa = dot3(row_a, sigma_a) + 0.3
    cov_ab = dot3(row_a, sigma_b)
    cov_bb = dot3(row_b, sigma_b) + 0.3
    determinant = cov_aa * cov_bb - cov_ab * cov_ab
    inverse_det = 1.0 / determinant
    ray = [
        position[i] + (rot[0][i] * offset[0] + rot[1][i] * offset[1] + rot[2][i] * offset[2])
        for i in range(3)
    ]
    inverse_norm = 1.0 / jnp.sqrt(dot3(ray, ray))
    basis = harmonics(*[r * inverse_norm for r in ray])
    colours = []
    for channel in range(3):
        total = SH_ZERO * coeffs[channel]
        for index in range(15):
            total = total + basis[index] * coeffs[3 + 3 * index + channel]
        colours.append(jnp.maximum(total + 0.5, 0.0))
    return [
        mean_u,
        mean_w,
        cov_bb * inverse_det,
        -cov_ab * inverse_det,
        cov_aa * inverse_det,
    ] + colours


def send_kernel(
    params_hbm,
    first_hbm,
    second_hbm,
    slots_hbm,
    sources_hbm,
    targets_hbm,
    camera_hbm,
    lists_hbm,
    tiles_hbm,
    wanted_hbm,
    out_ref,
    order_ref,
    entries_ref,
    corner_ref,
    wanted_ref,
    counts_ref,
    landing_ref,
    shown_ref,
    params_ref,
    first_ref,
    second_ref,
    slots_ref,
    sources_ref,
    targets_ref,
    camera_ref,
    lists_ref,
    tiles_ref,
    picked_ref,
    sems,
):
    pairs = (
        (slots_hbm, slots_ref),
        (sources_hbm, sources_ref),
        (targets_hbm, targets_ref),
        (camera_hbm, camera_ref),
        (params_hbm, params_ref),
        (first_hbm, first_ref),
        (second_hbm, second_ref),
        (lists_hbm, lists_ref),
        (tiles_hbm, tiles_ref),
        (wanted_hbm, wanted_ref),
    )
    copies = [pltpu.make_async_copy(a, b, sems.at[i]) for i, (a, b) in enumerate(pairs)]
    for copy in copies:
        copy.start()
    copies[0].wait()
    order = slots_by_rank(slots_ref[...])
    order_ref[...] = order
    hot = low_onehot(order)
    copies[1].wait()
    sources = pairs_by_rank(sources_ref[...])
    source_hot = low_onehot(sources)
    counts = add_columns(jnp.ones((8, 128), F32), sources, source_hot)[0:1]
    counts_ref[...] = counts
    out_ref[pl.ds(2, PEERS, stride=3), :] = jnp.broadcast_to(sources.astype(F32), (PEERS, 128))
    copies[2].wait()
    landing_ref[...] = pairs_by_rank(targets_ref[...])
    copies[3].wait()
    copies[4].wait()
    dense = params_ref[...].reshape(59, 8, 128)
    rows = [dense[i] for i in range(59)]
    cam = [camera_ref[0, i] for i in range(16)]
    sigma = covariance(rows[3:6], rows[6:10])
    seen = view_rows(rows[0:3], sigma, rows[11:59], cam)
    opacity = 1.0 / (1.0 + jnp.exp(-rows[10]))
    listed = seen[0:5] + [opacity] + seen[5:8]
    blank = jnp.zeros((8, 128), F32)
    table = jnp.stack(listed + [blank] * (ROWS - 9)).reshape(ROWS, LOCAL)
    taken = take_columns(table, order, hot)
    out_ref[pl.ds(0, PEERS, stride=3), :] = pack_peers(taken[0:8])
    for copy in copies[5:7]:
        copy.wait()
    plane = lax.axis_index("view")
    for quarter in range(VIEWS):

        @pl.when(plane == quarter)
        def _():
            for at, ref in enumerate((params_ref, first_ref, second_ref)):
                size = min(16, 59 - 16 * quarter)
                picked_ref[16 * at : 16 * at + size, :] = ref[16 * quarter : 16 * quarter + size, :]
                if size < 16:
                    picked_ref[16 * at + size : 16 * at + 16, :] = jnp.broadcast_to(
                        counts, (16 - size, LOCAL)
                    )

    moved = take_columns(picked_ref[...], sources, source_hot)
    moved = jnp.concatenate([moved[:, 0:PEERS], moved[:, PEERS:]], axis=0)
    numbers = order.astype(F32)
    pieces = []
    for k in range(CAP):
        span = slice(k * PEERS, (k + 1) * PEERS)
        pieces += [taken[8:9, span], numbers[:, span], moved[6 * k : 6 * k + 6]]
    out_ref[pl.ds(1, PEERS, stride=3), :] = jnp.concatenate(pieces, axis=0).T
    copies[7].wait()
    entries_ref[...] = jnp.concatenate([lists_ref[0, i : i + 1] for i in range(TILES)], axis=1)
    copies[8].wait()
    for tile in range(TILES):
        number = tiles_ref[0, tile]
        corner_ref[tile : tile + 1, :] = jnp.full(
            (1, 256), ((number & (ACROSS - 1)) * 16).astype(F32)
        )
        corner_ref[TILES + tile : TILES + tile + 1, :] = jnp.full(
            (1, 256), ((number >> 4) * 16).astype(F32)
        )
    for i in range(16):
        shown_ref[i : i + 1, :] = jnp.full((1, 128), cam[i], F32)
    copies[9].wait()


def render_kernel(
    recv_ref, entries_ref, corner_ref, target_ref, out_ref, share_ref, alpha_ref, grad_ref
):
    lead = recv_ref[pl.ds(0, PEERS, stride=3), :]
    tail = recv_ref[pl.ds(1, PEERS, stride=3), :]
    sources = recv_ref[pl.ds(2, PEERS, stride=3), :]
    flat = tail.T
    mine = jnp.concatenate([flat[8 * k + 2 : 8 * k + 8] for k in range(CAP)], axis=0)
    share_ref[...] = jnp.concatenate([mine[0:SHARE], mine[SHARE:]], axis=1)
    table = jnp.concatenate([unpack_peers(lead), unpack_peers(tail)], axis=0)
    entries = entries_ref[...]
    idx = jnp.where(entries < 0, -1, (entries & 15) * PEERS + (entries >> 4))
    hot = low_onehot(idx)
    listed = take_columns(table, idx, hot)
    iota_r = lax.broadcasted_iota(I32, (256, 256), 0)
    iota_c = lax.broadcasted_iota(I32, (256, 256), 1)
    before_mask = jnp.where(iota_r < iota_c, 1.0, 0.0).astype(BF16)
    before_mask = jnp.concatenate([before_mask, before_mask], axis=0)
    after_mask = jnp.where(iota_r > iota_c, 1.0, 0.0).astype(BF16)
    after_mask = jnp.concatenate([after_mask, after_mask], axis=0)
    steps = lax.broadcasted_iota(I32, (16, 256), 0).astype(F32)
    nt = (((1,), (1,)), ((), ()))
    tiles = range(TILES)
    heres, offs_u, offs_w = [], [], []
    for tile in tiles:
        here = listed[:, tile * 256 : (tile + 1) * 256]
        left = corner_ref[tile : tile + 1]
        top = corner_ref[TILES + tile : TILES + tile + 1]
        con_a, con_b, con_c, opacity = here[2:3], here[3:4], here[4:5], here[5:6]
        off_u = (steps + left + 0.5) - here[0:1]
        off_w = (steps + top + 0.5) - here[1:2]
        quad_u = LOG2E * (jnp.log(opacity) - 0.5 * con_a * off_u * off_u)
        cross = -LOG2E * con_b * off_u
        quad_w = (-0.5 * LOG2E) * con_c * off_w * off_w
        for j in range(16):
            exponent = quad_u + quad_w[j : j + 1] + cross * off_w[j : j + 1]
            alpha_ref[tile, j * 16 : (j + 1) * 16, :] = jnp.exp2(exponent)
        heres.append(here)
        offs_u.append(off_u)
        offs_w.append(off_w)
    log_keeps = [jnp.log(1.0 - alpha_ref[t]) for t in tiles]
    logs = [jnp.concatenate(split(x, 2), axis=1) for x in log_keeps]
    befores = [jnp.dot(x, before_mask, preferred_element_type=F32) for x in logs]
    weights = [jnp.exp(befores[t]) * alpha_ref[t] for t in tiles]
    weight_parts = [split(x, 2) for x in weights]
    colour_parts = [split(here[6:9], 3) for here in heres]
    residual_parts = []
    for tile in tiles:
        stacked = jnp.concatenate(
            [p.astype(F32) for p in colour_parts[tile]] + [jnp.zeros((7, 256), F32)], axis=0
        ).astype(BF16)
        summed = lax.dot_general(
            jnp.concatenate([stacked, stacked], axis=1),
            jnp.concatenate(weight_parts[tile], axis=1),
            nt,
            preferred_element_type=F32,
        )
        residual = summed[0:3] + summed[3:6] + summed[6:9] - target_ref[:, tile]
        residual_parts.append([p.astype(F32) for p in split(residual, 3)])
    pairs = ((0, 0), (0, 1), (1, 0), (1, 1), (0, 2), (2, 0))
    blank = jnp.zeros((14, 256), F32)
    pulls = []
    for tile in tiles:
        left_side = jnp.concatenate([residual_parts[tile][a] for a, _ in pairs] + [blank], axis=0)
        right_side = jnp.concatenate(
            [colour_parts[tile][b].astype(F32) for _, b in pairs] + [blank], axis=0
        )
        pulls.append(
            lax.dot_general(
                left_side.astype(BF16),
                right_side.astype(BF16),
                (((0,), (0,)), ((), ())),
                preferred_element_type=F32,
            )
        )
    weighteds = [pulls[t] * weights[t] for t in tiles]
    flows = [jnp.concatenate(split(x, 2), axis=1) for x in weighteds]
    afters = [jnp.dot(x, after_mask, preferred_element_type=F32) for x in flows]
    for t in tiles:
        grad_ref[t] = weighteds[t] - afters[t] * (alpha_ref[t] * jnp.exp(-log_keeps[t]))
    results = []
    for tile in tiles:
        here, off_u, off_w = heres[tile], offs_u[tile], offs_w[tile]
        con_a, con_b, con_c = here[2:3], here[3:4], here[4:5]
        stacked_res = jnp.concatenate(
            residual_parts[tile] + [jnp.zeros((7, 256), F32)], axis=0
        ).astype(BF16)
        colour_sum = jnp.dot(
            jnp.concatenate([stacked_res, stacked_res], axis=1),
            jnp.concatenate(weight_parts[tile], axis=0),
            preferred_element_type=F32,
        )
        colour_grad = colour_sum[0:3] + colour_sum[3:6] + colour_sum[6:9]
        zeroth = first = second = None
        for j in range(16):
            piece = grad_ref[tile, j * 16 : (j + 1) * 16, :]
            lifted = piece * off_w[j : j + 1]
            twice = lifted * off_w[j : j + 1]
            zeroth = piece if zeroth is None else zeroth + piece
            first = lifted if first is None else first + lifted
            second = twice if second is None else second + twice

        def over(values):
            return jnp.sum(values, axis=0, keepdims=True)

        along = zeroth * off_u
        m_00, m_10, m_20 = over(zeroth), over(along), over(along * off_u)
        m_01, m_11, m_02 = over(first), over(first * off_u), over(second)
        results.append(
            jnp.concatenate(
                [
                    con_a * m_10 + con_b * m_01,
                    con_c * m_01 + con_b * m_10,
                    -0.5 * m_20,
                    -m_11,
                    -0.5 * m_02,
                    m_00,
                    colour_grad,
                    jnp.zeros((ROWS - 9, 256), F32),
                ],
                axis=0,
            )
        )
    grads = jnp.concatenate(results, axis=1)
    summed = add_columns(grads, idx, hot, 2)
    packed = [pack_peers(summed[0:8]), pack_peers(summed[8:16])]
    out_ref[pl.ds(0, PEERS, stride=BLOCKS), :] = packed[0]
    out_ref[pl.ds(1, PEERS, stride=BLOCKS), :] = packed[1]
    wanted = sources.T
    wanted = jnp.concatenate([wanted, wanted], axis=1)
    totals = [None] * 9
    for pair in range(CAP // 2):
        span = slice(pair * 128, (pair + 1) * 128)
        same = wanted == table[9:10, span]
        for row in range(9):
            term = jnp.where(same, summed[row : row + 1, span], 0.0)
            totals[row] = term if pair == 0 else totals[row] + term
    for row in range(9):
        both = totals[row][:, 0:PEERS] + totals[row][:, PEERS:]
        out_ref[pl.ds(2 + row, PEERS, stride=BLOCKS), :] = jnp.concatenate(
            [both[0:PEERS], both[PEERS:]], axis=1
        )


def owner_kernel(recv_ref, order_ref, shown_ref, share_ref, out_ref):
    values = jnp.concatenate(
        [unpack_peers(recv_ref[pl.ds(i, PEERS, stride=BLOCKS), :]) for i in range(2)], axis=0
    )
    order = order_ref[...]
    owned = add_columns(values, order, low_onehot(order), 2)
    out_ref[0:AT_CAMERA, :] = owned[0:9].reshape(9, 8, 128).reshape(AT_CAMERA, 128)
    out_ref[AT_CAMERA:AT_MOVED, :] = shown_ref[...]
    for row in range(9):
        out_ref[AT_MOVED + row : AT_MOVED + row + 1, :] = jnp.sum(
            recv_ref[pl.ds(2 + row, PEERS, stride=BLOCKS), :], axis=0, keepdims=True
        )
    out_ref[AT_MOVED + 9 : AT_SHARE, :] = jnp.zeros((AT_SHARE - AT_MOVED - 9, 128), F32)
    out_ref[AT_SHARE:SENT, :] = share_ref[...]


def log_one_plus(t):
    s = t / (2.0 + t)
    square = s * s
    total = jnp.full_like(s, 1.0 / 17.0)
    for odd in (15, 13, 11, 9, 7, 5, 3, 1):
        total = total * square + 1.0 / odd
    return 2.0 * s * total


def one_minus_exp(x):
    small = jnp.ones_like(x)
    for n in range(10, 1, -1):
        small = 1.0 + small * x * (1.0 / n)
    return jnp.where(x > -0.5, -x * small, 1.0 - jnp.exp(x))


def rates_column():
    row = lax.broadcasted_iota(I32, (59, 1), 0)
    rate = jnp.where(row < 14, 0.0025, 0.000125)
    rate = jnp.where(row < 11, 0.05, rate)
    rate = jnp.where(row < 10, 0.001, rate)
    rate = jnp.where(row < 6, 0.005, rate)
    return jnp.where(row < 3, 0.00016, rate)


def tree_sum(values):
    return (values[0] + values[1]) + (values[2] + values[3])


def adam(params, first_old, second_old, gradient):
    first = 0.9 * first_old + 0.1 * gradient
    second = 0.999 * second_old + 0.001 * gradient * gradient
    stepped = params - rates_column() * (first / BIAS_ONE) / (jnp.sqrt(second / BIAS_TWO) + 1e-15)
    return stepped, first, second


def spread_logit(logit, counts):
    soft = jnp.maximum(logit, 0.0) + log_one_plus(jnp.exp(-jnp.abs(logit)))
    share = -soft / (counts + 1.0)
    return jnp.log(one_minus_exp(share)) - share


def sigmoid_rest(logit):
    return 1.0 - 1.0 / (1.0 + jnp.exp(-logit))


def incoming_columns(parts):
    def stacked(row):
        return jnp.concatenate([ref[row : row + 1, :] for ref in parts], axis=0)

    def folded(x):
        return (x[0:1] + x[1:2]) + (x[2:3] + x[3:4])

    def wide(x):
        return jnp.broadcast_to(x, (VIEWS, 128))

    plane = jnp.full((SHARE, 128), lax.axis_index("view"), I32)
    shares = [ref[AT_SHARE:SENT, :] for ref in parts]
    for bit in (1, 2):
        flip = (plane & bit) > 0
        shares = [jnp.where(flip, shares[i ^ bit], shares[i]) for i in range(VIEWS)]
    params, first_old, second_old = [
        jnp.concatenate([part[i : i + 16] for part in shares], axis=0) for i in (0, 16, 32)
    ]
    rows = [params[i : i + 1] for i in range(59)]
    cam = [stacked(AT_CAMERA + i) for i in range(16)]
    sigma, pull_sigma = jax.vjp(covariance, rows[3:6], rows[6:10])
    _, pull = jax.vjp(
        lambda p, s, c: view_rows(p, s, c, cam),
        [wide(x) for x in rows[0:3]],
        [wide(x) for x in sigma],
        [wide(x) for x in rows[11:59]],
    )
    got = [stacked(AT_MOVED + i) for i in range(9)]
    d_pos, d_sigma, d_coeff = pull([got[i] for i in (0, 1, 2, 3, 4, 6, 7, 8)])
    d_scale, d_quat = pull_sigma([folded(x) for x in d_sigma])
    d_logit = folded(got[5]) * sigmoid_rest(rows[10])
    gradient = jnp.concatenate(
        [folded(x) for x in d_pos]
        + list(d_scale)
        + list(d_quat)
        + [d_logit]
        + [folded(x) for x in d_coeff],
        axis=0,
    )
    stepped, _, _ = adam(params[0:59], first_old[0:59], second_old[0:59], gradient)
    logit = spread_logit(stepped[10:11], params[59:60])
    row = lax.broadcasted_iota(I32, (59, 128), 0)
    return jnp.concatenate(
        [jnp.where(row == 10, logit, stepped), jnp.ones((5, 128), F32)], axis=0
    )


def step_kernel(
    params_ref,
    first_ref,
    second_ref,
    own_ref,
    near_ref,
    far_ref,
    last_ref,
    counts_ref,
    targets_ref,
    new_params_ref,
    new_first_ref,
    new_second_ref,
    gradient_ref,
):
    parts = (own_ref, near_ref, far_ref, last_ref)
    targets = targets_ref[...]
    placed = add_columns(incoming_columns(parts), targets, low_onehot(targets))
    dense = params_ref[...].reshape(59, 8, 128)
    rows = [dense[i] for i in range(59)]
    sigma, pull_sigma = jax.vjp(covariance, rows[3:6], rows[6:10])
    position, coeffs = rows[0:3], rows[11:59]
    pos_parts, sigma_parts, coeff_parts, opacity_parts = [], [], [], []
    for ref in parts:
        got = [ref[8 * i : 8 * i + 8, :] for i in range(9)]
        cam = [
            jnp.broadcast_to(ref[AT_CAMERA + i : AT_CAMERA + i + 1, :], (8, 128)) for i in range(16)
        ]
        _, pull = jax.vjp(lambda p, s, c: view_rows(p, s, c, cam), position, sigma, coeffs)
        d_pos, d_sigma, d_coeff = pull([got[i] for i in (0, 1, 2, 3, 4, 6, 7, 8)])
        pos_parts.append(d_pos)
        sigma_parts.append(d_sigma)
        coeff_parts.append(d_coeff)
        opacity_parts.append(got[5])
    d_pos = [tree_sum([p[i] for p in pos_parts]) for i in range(3)]
    d_sigma = [tree_sum([p[i] for p in sigma_parts]) for i in range(6)]
    d_coeff = [tree_sum([p[i] for p in coeff_parts]) for i in range(48)]
    d_scale, d_quat = pull_sigma(d_sigma)
    d_logit = tree_sum(opacity_parts) * sigmoid_rest(rows[10])
    gradient = jnp.stack(d_pos + list(d_scale) + list(d_quat) + [d_logit] + d_coeff).reshape(
        59, LOCAL
    )
    gradient_ref[...] = gradient
    stepped, first, second = adam(params_ref[...], first_ref[...], second_ref[...], gradient)
    counts = counts_ref[...]
    landed = placed[59:60] > 0.5
    cleared = (counts + placed[59:60]) > 0.5
    row = lax.broadcasted_iota(I32, (59, LOCAL), 0)
    spread = jnp.where(
        (row == 10) & (counts > 0.5), spread_logit(stepped[10:11], counts), stepped
    )
    new_params_ref[...] = jnp.where(landed, placed[0:59], spread)
    new_first_ref[...] = jnp.where(cleared, 0.0, first)
    new_second_ref[...] = jnp.where(cleared, 0.0, second)


def call(kernel, shapes, ins, scratch=()):
    spec = {
        "v": pl.BlockSpec(memory_space=pltpu.VMEM),
        "s": pl.BlockSpec(memory_space=pltpu.SMEM),
        "h": pl.BlockSpec(memory_space=pltpu.HBM),
    }
    out_shape = [jax.ShapeDtypeStruct(shape, dtype) for shape, dtype in shapes]
    return pl.pallas_call(
        kernel,
        out_shape=out_shape,
        in_specs=[spec[kind] for kind in ins],
        out_specs=[spec["v"]] * len(out_shape),
        scratch_shapes=list(scratch),
        compiler_params=pltpu.CompilerParams(vmem_limit_bytes=VMEM_LIMIT),
    )


def in_hbm(array):
    return pltpu.with_memory_space_constraint(array, pltpu.HBM)


def exchange(block):
    parts = block.reshape(PEERS, 1, -1)
    got = lax.all_to_all(parts, "gauss", split_axis=0, concat_axis=0, tiled=True)
    return got.reshape(block.shape)


def shards(
    params,
    first_moment,
    second_moment,
    cameras,
    target,
    tile_index,
    tile_lists,
    send_slots,
    reloc_send,
    reloc_recv,
):
    columns = ((1, LOCAL), I32)
    whole = ((59, LOCAL), F32)
    outgoing, order, entries, corners, wanted, counts, landing, shown = call(
        send_kernel,
        [
            ((3 * PEERS, 128), F32),
            columns,
            columns,
            ((2 * TILES, 256), F32),
            ((3, TILES, 256), F32),
            ((1, LOCAL), F32),
            ((1, 128), I32),
            ((16, 128), F32),
        ],
        "hhhhhhhhhh",
        [
            pltpu.VMEM((59, LOCAL), F32),
            pltpu.VMEM((59, LOCAL), F32),
            pltpu.VMEM((59, LOCAL), F32),
            pltpu.VMEM((8, 128), I32),
            pltpu.VMEM((1, 128), I32),
            pltpu.VMEM((1, 128), I32),
            pltpu.SMEM((1, 16), F32),
            pltpu.VMEM((1, TILES, 256), I32),
            pltpu.SMEM((1, TILES), I32),
            pltpu.VMEM((SHARE, LOCAL), F32),
            pltpu.SemaphoreType.DMA((10,)),
        ],
    )(
        in_hbm(params),
        in_hbm(first_moment),
        in_hbm(second_moment),
        in_hbm(send_slots.reshape(8, 128)),
        in_hbm(reloc_send),
        in_hbm(reloc_recv),
        in_hbm(cameras),
        in_hbm(tile_lists),
        in_hbm(tile_index),
        in_hbm(jnp.transpose(target[0], (1, 0, 2))),
    )
    received = exchange(outgoing)
    row_grads, share = call(
        render_kernel,
        [((BLOCKS * PEERS, 128), F32), ((SHARE, 128), F32)],
        "vvvv",
        [pltpu.VMEM((TILES, 256, 256), F32), pltpu.VMEM((TILES, 256, 256), F32)],
    )(received, entries, corners, wanted)
    returned = exchange(row_grads)
    (own,) = call(owner_kernel, [((SENT, 128), F32)], "vvvv")(returned, order, shown, share)
    others = [
        lax.ppermute(own, "view", [(i, i ^ flip) for i in range(VIEWS)]) for flip in (1, 2, 3)
    ]
    return call(step_kernel, [whole, whole, whole, whole], "vvvvvvvvv")(
        params, first_moment, second_moment, own, *others, counts, landing
    )


def solution(mesh):
    in_specs = (
        P(None, "gauss"),
        P(None, "gauss"),
        P(None, "gauss"),
        P("view", None),
        P("view", "gauss", None, None),
        P("view", "gauss"),
        P("view", "gauss", None),
        P("view", "gauss", None),
        P("gauss", None),
        P("gauss", None),
    )
    out_specs = (P(None, "gauss"), P(None, "gauss"), P(None, "gauss"), P(None, "gauss"))
    return jax.shard_map(shards, mesh=mesh, in_specs=in_specs, out_specs=out_specs, check_vma=False)
```

```python
import math

import jax
import jax.numpy as jnp
from jax import lax
from jax.experimental import pallas as pl
from jax.experimental.pallas import tpu as pltpu
from jax.sharding import PartitionSpec as P

F32 = jnp.float32
BF16 = jnp.bfloat16
I32 = jnp.int32
PEERS = 64
LOCAL = 1024
CAP = 16
VIEWS = 4
TILES = 4
ACROSS = 16
ROWS = 16
LOG2E = 1.4426950408889634
SHARE = 48
BLOCKS = 11
AT_MOVED = 72
AT_CAMERA = 81
AT_SHARE = 88
SENT = 136

SH_ZERO = 0.28209479177387814
SH_ONE = 0.4886025119029199
SH_TWO = (
    1.0925484305920792,
    -1.0925484305920792,
    0.31539156525252005,
    -1.0925484305920792,
    0.5462742152960396,
)
SH_THREE = (
    -0.5900435899266435,
    2.890611442640554,
    -0.4570457994644658,
    0.3731763325901154,
    -0.4570457994644658,
    1.445305721320277,
    -0.5900435899266435,
)
BIAS_ONE = 1.0 - math.exp(1000.0 * math.log(0.9))
BIAS_TWO = 1.0 - math.exp(1000.0 * math.log(0.999))
VMEM_LIMIT = 16 * 1024 * 1024


def split(x, parts):
    out = []
    for index in range(parts):
        piece = x.astype(BF16)
        out.append(piece)
        if index + 1 < parts:
            x = x - piece.astype(F32)
    return out


def low_onehot(idx):
    lane = lax.broadcasted_iota(I32, (128, idx.shape[1]), 0)
    return jnp.where(lane == (idx & 127), 1.0, 0.0).astype(BF16)


def take_columns(table, idx, hot):
    rows = table.shape[0]
    high = idx >> 7
    parts = split(table, 3)
    lhs = jnp.concatenate(
        [
            jnp.concatenate([p[:, c * 128 : (c + 1) * 128] for p in parts], axis=1)
            for c in range(8)
        ],
        axis=0,
    )
    rhs = jnp.concatenate([hot, hot, hot], axis=0)
    wide = jnp.dot(lhs, rhs, preferred_element_type=F32)
    total = None
    for c in range(8):
        term = jnp.where(high == c, wide[c * rows : (c + 1) * rows], 0.0)
        total = term if total is None else total + term
    return total


def add_columns(values, idx, hot, parts=3):
    rows = values.shape[0]
    high = idx >> 7
    pieces = []
    for piece in split(values, parts):
        piece = piece.astype(F32)
        pieces += [jnp.where(high == c, piece, 0.0) for c in range(8)]
    lhs = jnp.concatenate(pieces, axis=0).astype(BF16)
    wide = lax.dot_general(lhs, hot, (((1,), (1,)), ((), ())), preferred_element_type=F32)
    size = 8 * rows
    wide = sum(wide[i * size : (i + 1) * size] for i in range(1, parts)) + wide[0:size]
    return jnp.concatenate([wide[c * rows : (c + 1) * rows] for c in range(8)], axis=1)


def pack_peers(table):
    pieces = [table[:, k * PEERS : (k + 1) * PEERS] for k in range(CAP)]
    return jnp.concatenate(pieces, axis=0).T


def unpack_peers(block):
    flat = block.T
    return jnp.concatenate([flat[k * 8 : (k + 1) * 8] for k in range(CAP)], axis=1)


def halves(row):
    block = row.reshape(8, 128)
    return jnp.concatenate([block[:, 0:PEERS], block[:, PEERS:]], axis=0)


def joined(block):
    return jnp.concatenate([block[0:8], block[8:16]], axis=1).reshape(1, LOCAL)


def slots_by_rank(slots):
    source = lax.broadcasted_iota(I32, (128, LOCAL), 0)
    col = lax.broadcasted_iota(I32, (128, LOCAL), 1)
    pick = jnp.where(source == (col & 7) * 16 + (col >> 6), 1.0, 0.0).astype(BF16)
    upper = jnp.dot((slots >> 5).astype(F32).astype(BF16), pick, preferred_element_type=F32)
    lower = jnp.dot((slots & 31).astype(F32).astype(BF16), pick, preferred_element_type=F32)
    wide = upper * 32.0 + lower
    row = lax.broadcasted_iota(I32, (8, LOCAL), 0)
    column = lax.broadcasted_iota(I32, (8, LOCAL), 1)
    kept = jnp.where(row == ((column >> 3) & 7), wide, 0.0)
    return jnp.sum(kept, axis=0, keepdims=True).astype(I32)


def pairs_by_rank(pairs):
    source = lax.broadcasted_iota(I32, (128, 128), 0)
    col = lax.broadcasted_iota(I32, (128, 128), 1)
    pick = jnp.where(source == (col & (PEERS - 1)) * 2 + (col >> 6), 1.0, 0.0).astype(BF16)
    wide = jnp.broadcast_to(pairs + 1, (8, 128))
    upper = jnp.dot((wide >> 5).astype(F32).astype(BF16), pick, preferred_element_type=F32)
    lower = jnp.dot((wide & 31).astype(F32).astype(BF16), pick, preferred_element_type=F32)
    return (upper * 32.0 + lower)[0:1].astype(I32) - 1


def covariance(log_scale, quat):
    norm = jnp.sqrt(quat[0] * quat[0] + quat[1] * quat[1] + quat[2] * quat[2] + quat[3] * quat[3])
    quat_w, quat_x, quat_y, quat_z = [q / norm for q in quat]
    orient = [
        [
            1.0 - 2.0 * (quat_y * quat_y + quat_z * quat_z),
            2.0 * (quat_x * quat_y - quat_w * quat_z),
            2.0 * (quat_x * quat_z + quat_w * quat_y),
        ],
        [
            2.0 * (quat_x * quat_y + quat_w * quat_z),
            1.0 - 2.0 * (quat_x * quat_x + quat_z * quat_z),
            2.0 * (quat_y * quat_z - quat_w * quat_x),
        ],
        [
            2.0 * (quat_x * quat_z - quat_w * quat_y),
            2.0 * (quat_y * quat_z + quat_w * quat_x),
            1.0 - 2.0 * (quat_x * quat_x + quat_y * quat_y),
        ],
    ]
    scales = [jnp.exp(s) for s in log_scale]
    factor = [[orient[i][j] * scales[j] for j in range(3)] for i in range(3)]

    def entry(i, j):
        return (
            factor[i][0] * factor[j][0] + factor[i][1] * factor[j][1] + factor[i][2] * factor[j][2]
        )

    return [entry(0, 0), entry(0, 1), entry(0, 2), entry(1, 1), entry(1, 2), entry(2, 2)]


def harmonics(dir_x, dir_y, dir_z):
    sq_x, sq_y, sq_z = (dir_x * dir_x, dir_y * dir_y, dir_z * dir_z)
    return [
        -SH_ONE * dir_y,
        SH_ONE * dir_z,
        -SH_ONE * dir_x,
        SH_TWO[0] * dir_x * dir_y,
        SH_TWO[1] * dir_y * dir_z,
        SH_TWO[2] * (2.0 * sq_z - sq_x - sq_y),
        SH_TWO[3] * dir_x * dir_z,
        SH_TWO[4] * (sq_x - sq_y),
        SH_THREE[0] * dir_y * (3.0 * sq_x - sq_y),
        SH_THREE[1] * dir_x * dir_y * dir_z,
        SH_THREE[2] * dir_y * (4.0 * sq_z - sq_x - sq_y),
        SH_THREE[3] * dir_z * (2.0 * sq_z - 3.0 * sq_x - 3.0 * sq_y),
        SH_THREE[4] * dir_x * (4.0 * sq_z - sq_x - sq_y),
        SH_THREE[5] * dir_z * (sq_x - sq_y),
        SH_THREE[6] * dir_x * (sq_x - 3.0 * sq_y),
    ]


def view_rows(position, sigma, coeffs, cam):
    rot = [cam[0:3], cam[3:6], cam[6:9]]
    offset = cam[9:12]
    focal_x, focal_y, centre_x, centre_y = cam[12:16]
    cam_x, cam_y, cam_z = [
        rot[i][0] * position[0] + rot[i][1] * position[1] + rot[i][2] * position[2] + offset[i]
        for i in range(3)
    ]
    inverse_z = 1.0 / cam_z
    mean_u = focal_x * cam_x * inverse_z + centre_x
    mean_w = focal_y * cam_y * inverse_z + centre_y
    jac_a0 = focal_x * inverse_z
    jac_a2 = -focal_x * cam_x * inverse_z * inverse_z
    jac_b1 = focal_y * inverse_z
    jac_b2 = -focal_y * cam_y * inverse_z * inverse_z
    row_a = [jac_a0 * rot[0][i] + jac_a2 * rot[2][i] for i in range(3)]
    row_b = [jac_b1 * rot[1][i] + jac_b2 * rot[2][i] for i in range(3)]
    full = [
        [sigma[0], sigma[1], sigma[2]],
        [sigma[1], sigma[3], sigma[4]],
        [sigma[2], sigma[4], sigma[5]],
    ]

    def through(row):
        return [full[i][0] * row[0] + full[i][1] * row[1] + full[i][2] * row[2] for i in range(3)]

    def dot3(left, right):
        return left[0] * right[0] + left[1] * right[1] + left[2] * right[2]

    sigma_a = through(row_a)
    sigma_b = through(row_b)
    cov_aa = dot3(row_a, sigma_a) + 0.3
    cov_ab = dot3(row_a, sigma_b)
    cov_bb = dot3(row_b, sigma_b) + 0.3
    determinant = cov_aa * cov_bb - cov_ab * cov_ab
    inverse_det = 1.0 / determinant
    ray = [
        position[i] + (rot[0][i] * offset[0] + rot[1][i] * offset[1] + rot[2][i] * offset[2])
        for i in range(3)
    ]
    inverse_norm = 1.0 / jnp.sqrt(dot3(ray, ray))
    basis = harmonics(*[r * inverse_norm for r in ray])
    colours = []
    for channel in range(3):
        total = SH_ZERO * coeffs[channel]
        for index in range(15):
            total = total + basis[index] * coeffs[3 + 3 * index + channel]
        colours.append(jnp.maximum(total + 0.5, 0.0))
    return [
        mean_u,
        mean_w,
        cov_bb * inverse_det,
        -cov_ab * inverse_det,
        cov_aa * inverse_det,
    ] + colours


def send_kernel(
    params_hbm,
    first_hbm,
    second_hbm,
    slots_hbm,
    sources_hbm,
    targets_hbm,
    camera_hbm,
    lists_hbm,
    tiles_hbm,
    wanted_hbm,
    out_ref,
    order_ref,
    entries_ref,
    corner_ref,
    wanted_ref,
    counts_ref,
    landing_ref,
    shown_ref,
    params_ref,
    first_ref,
    second_ref,
    slots_ref,
    sources_ref,
    targets_ref,
    camera_ref,
    lists_ref,
    tiles_ref,
    sems,
):
    pairs = (
        (slots_hbm, slots_ref),
        (params_hbm, params_ref),
        (camera_hbm, camera_ref),
        (sources_hbm, sources_ref),
        (targets_hbm, targets_ref),
        (lists_hbm, lists_ref),
        (tiles_hbm, tiles_ref),
        (wanted_hbm, wanted_ref),
        (first_hbm, first_ref),
        (second_hbm, second_ref),
    )
    copies = [pltpu.make_async_copy(a, b, sems.at[i]) for i, (a, b) in enumerate(pairs)]
    for copy in copies:
        copy.start()
    for at in (0, 3, 4):
        copies[at].wait()
    order = slots_by_rank(slots_ref[...])
    order_ref[...] = order
    hot = low_onehot(order)
    sources = pairs_by_rank(sources_ref[...])
    source_hot = low_onehot(sources)
    counts = add_columns(jnp.ones((8, 128), F32), sources, source_hot, 1)[0:1]
    counts_ref[...] = counts
    out_ref[pl.ds(2, PEERS, stride=3), :] = jnp.broadcast_to(sources.astype(F32), (PEERS, 128))
    landing_ref[...] = pairs_by_rank(targets_ref[...])
    for at in (1, 2, 5, 6, 7, 8, 9):
        copies[at].wait()
    dense = params_ref[...].reshape(59, 8, 128)
    rows = [dense[i] for i in range(59)]
    cam = [camera_ref[0, i] for i in range(16)]
    sigma = covariance(rows[3:6], rows[6:10])
    seen = view_rows(rows[0:3], sigma, rows[11:59], cam)
    opacity = 1.0 / (1.0 + jnp.exp(-rows[10]))
    listed = seen[0:5] + [opacity] + seen[5:8]
    blank = jnp.zeros((8, 128), F32)
    table = jnp.stack(listed + [blank] * (ROWS - 9)).reshape(ROWS, LOCAL)
    taken = take_columns(table, order, hot)
    out_ref[pl.ds(0, PEERS, stride=3), :] = pack_peers(taken[0:8])
    plane = jnp.full((16, LOCAL), lax.axis_index("view"), I32)
    share = []
    for ref in (params_ref, first_ref, second_ref):
        final = jnp.concatenate([ref[48:59, :], jnp.broadcast_to(counts, (5, LOCAL))], axis=0)
        low = jnp.where(plane == 0, ref[0:16, :], ref[16:32, :])
        share.append(jnp.where(plane < 2, low, jnp.where(plane == 2, ref[32:48, :], final)))
    moved = take_columns(jnp.concatenate(share, axis=0), sources, source_hot)
    moved = jnp.concatenate([moved[:, 0:PEERS], moved[:, PEERS:]], axis=0)
    flat = jnp.concatenate([halves(taken[8:9]), halves(order.astype(F32)), moved], axis=0)
    out_ref[pl.ds(1, PEERS, stride=3), :] = flat.T
    entries_ref[...] = jnp.concatenate([lists_ref[0, i : i + 1] for i in range(TILES)], axis=1)
    for tile in range(TILES):
        number = tiles_ref[0, tile]
        corner_ref[tile : tile + 1, :] = jnp.full(
            (1, 256), ((number & (ACROSS - 1)) * 16).astype(F32)
        )
        corner_ref[TILES + tile : TILES + tile + 1, :] = jnp.full(
            (1, 256), ((number >> 4) * 16).astype(F32)
        )
    lane = lax.broadcasted_iota(I32, (1, 128), 1)
    shown = jnp.zeros((1, 128), F32)
    for i in range(16):
        shown = jnp.where(lane == i, cam[i], shown)
    shown_ref[...] = shown


def render_kernel(
    recv_ref, entries_ref, corner_ref, target_ref, out_ref, share_ref, alpha_ref, grad_ref
):
    lead = recv_ref[pl.ds(0, PEERS, stride=3), :]
    tail = recv_ref[pl.ds(1, PEERS, stride=3), :]
    sources = recv_ref[pl.ds(2, PEERS, stride=3), :]
    flat = tail.T
    share_ref[...] = jnp.concatenate([flat[32 : 32 + SHARE], flat[32 + SHARE :]], axis=1)
    numbers = joined(flat[16:32])
    table = jnp.concatenate(
        [unpack_peers(lead), joined(flat[0:16]), jnp.zeros((ROWS - 9, LOCAL), F32)], axis=0
    )
    entries = entries_ref[...]
    idx = jnp.where(entries < 0, -1, (entries & 15) * PEERS + (entries >> 4))
    hot = low_onehot(idx)
    listed = take_columns(table, idx, hot)
    iota_r = lax.broadcasted_iota(I32, (256, 256), 0)
    iota_c = lax.broadcasted_iota(I32, (256, 256), 1)
    before_mask = jnp.where(iota_r < iota_c, 1.0, 0.0).astype(BF16)
    before_mask = jnp.concatenate([before_mask, before_mask], axis=0)
    after_mask = jnp.where(iota_r > iota_c, 1.0, 0.0).astype(BF16)
    after_mask = jnp.concatenate([after_mask, after_mask], axis=0)
    steps = lax.broadcasted_iota(I32, (16, 256), 0).astype(F32)
    nt = (((1,), (1,)), ((), ()))
    tiles = range(TILES)
    heres, offs_u, offs_w = [], [], []
    for tile in tiles:
        here = listed[:, tile * 256 : (tile + 1) * 256]
        left = corner_ref[tile : tile + 1]
        top = corner_ref[TILES + tile : TILES + tile + 1]
        con_a, con_b, con_c, opacity = here[2:3], here[3:4], here[4:5], here[5:6]
        off_u = (steps + left + 0.5) - here[0:1]
        off_w = (steps + top + 0.5) - here[1:2]
        quad_u = LOG2E * (jnp.log(opacity) - 0.5 * con_a * off_u * off_u)
        cross = -LOG2E * con_b * off_u
        quad_w = (-0.5 * LOG2E) * con_c * off_w * off_w
        for j in range(16):
            exponent = quad_u + quad_w[j : j + 1] + cross * off_w[j : j + 1]
            alpha_ref[tile, j * 16 : (j + 1) * 16, :] = jnp.exp2(exponent)
        heres.append(here)
        offs_u.append(off_u)
        offs_w.append(off_w)
    log_keeps = [jnp.log(1.0 - alpha_ref[t]) for t in tiles]
    logs = [jnp.concatenate(split(x, 2), axis=1) for x in log_keeps]
    befores = [jnp.dot(x, before_mask, preferred_element_type=F32) for x in logs]
    weights = [jnp.exp(befores[t]) * alpha_ref[t] for t in tiles]
    weight_parts = [split(x, 2) for x in weights]
    colour_parts = [split(here[6:9], 3) for here in heres]
    residual_parts = []
    for tile in tiles:
        stacked = jnp.concatenate(
            [p.astype(F32) for p in colour_parts[tile]] + [jnp.zeros((7, 256), F32)], axis=0
        ).astype(BF16)
        summed = lax.dot_general(
            jnp.concatenate([stacked, stacked], axis=1),
            jnp.concatenate(weight_parts[tile], axis=1),
            nt,
            preferred_element_type=F32,
        )
        residual = summed[0:3] + summed[3:6] + summed[6:9] - target_ref[:, tile]
        residual_parts.append([p.astype(F32) for p in split(residual, 3)])
    pairs = ((0, 0), (0, 1), (1, 0), (1, 1), (0, 2), (2, 0))
    blank = jnp.zeros((14, 256), F32)
    pulls = []
    for tile in tiles:
        left_side = jnp.concatenate([residual_parts[tile][a] for a, _ in pairs] + [blank], axis=0)
        right_side = jnp.concatenate(
            [colour_parts[tile][b].astype(F32) for _, b in pairs] + [blank], axis=0
        )
        pulls.append(
            lax.dot_general(
                left_side.astype(BF16),
                right_side.astype(BF16),
                (((0,), (0,)), ((), ())),
                preferred_element_type=F32,
            )
        )
    weighteds = [pulls[t] * weights[t] for t in tiles]
    flows = [jnp.concatenate(split(x, 2), axis=1) for x in weighteds]
    afters = [jnp.dot(x, after_mask, preferred_element_type=F32) for x in flows]
    for t in tiles:
        grad_ref[t] = weighteds[t] - afters[t] * (alpha_ref[t] * jnp.exp(-log_keeps[t]))
    results = []
    for tile in tiles:
        here, off_u, off_w = heres[tile], offs_u[tile], offs_w[tile]
        con_a, con_b, con_c = here[2:3], here[3:4], here[4:5]
        stacked_res = jnp.concatenate(
            residual_parts[tile] + [jnp.zeros((7, 256), F32)], axis=0
        ).astype(BF16)
        colour_sum = jnp.dot(
            jnp.concatenate([stacked_res, stacked_res], axis=1),
            jnp.concatenate(weight_parts[tile], axis=0),
            preferred_element_type=F32,
        )
        colour_grad = colour_sum[0:3] + colour_sum[3:6] + colour_sum[6:9]
        zeroth = first = second = None
        for j in range(16):
            piece = grad_ref[tile, j * 16 : (j + 1) * 16, :]
            lifted = piece * off_w[j : j + 1]
            twice = lifted * off_w[j : j + 1]
            zeroth = piece if zeroth is None else zeroth + piece
            first = lifted if first is None else first + lifted
            second = twice if second is None else second + twice

        def over(values):
            return jnp.sum(values, axis=0, keepdims=True)

        along = zeroth * off_u
        m_00, m_10, m_20 = over(zeroth), over(along), over(along * off_u)
        m_01, m_11, m_02 = over(first), over(first * off_u), over(second)
        results.append(
            jnp.concatenate(
                [
                    con_a * m_10 + con_b * m_01,
                    con_c * m_01 + con_b * m_10,
                    -0.5 * m_20,
                    -m_11,
                    -0.5 * m_02,
                    m_00,
                    colour_grad,
                    jnp.zeros((ROWS - 9, 256), F32),
                ],
                axis=0,
            )
        )
    grads = jnp.concatenate(results, axis=1)
    summed = add_columns(grads, idx, hot, 2)
    out_ref[pl.ds(0, PEERS, stride=BLOCKS), :] = pack_peers(summed[0:8])
    flat = jnp.concatenate([halves(summed[8:9]), jnp.zeros((112, PEERS), F32)], axis=0)
    out_ref[pl.ds(1, PEERS, stride=BLOCKS), :] = flat.T
    wanted = sources.T
    wanted = jnp.concatenate([wanted, wanted], axis=1)
    totals = [None] * 9
    for pair in range(CAP // 2):
        span = slice(pair * 128, (pair + 1) * 128)
        same = wanted == numbers[:, span]
        for row in range(9):
            term = jnp.where(same, summed[row : row + 1, span], 0.0)
            totals[row] = term if pair == 0 else totals[row] + term
    for row in range(9):
        both = totals[row][:, 0:PEERS] + totals[row][:, PEERS:]
        out_ref[pl.ds(2 + row, PEERS, stride=BLOCKS), :] = jnp.concatenate(
            [both[0:PEERS], both[PEERS:]], axis=1
        )


def owner_kernel(recv_ref, order_ref, shown_ref, share_ref, out_ref):
    lead = unpack_peers(recv_ref[pl.ds(0, PEERS, stride=BLOCKS), :])
    last = joined(recv_ref[pl.ds(1, PEERS, stride=BLOCKS), :].T[0:16])
    values = jnp.concatenate([lead, last, jnp.zeros((ROWS - 9, LOCAL), F32)], axis=0)
    order = order_ref[...]
    owned = add_columns(values, order, low_onehot(order), 2)
    out_ref[0:AT_MOVED, :] = owned[0:9].reshape(9, 8, 128).reshape(AT_MOVED, 128)
    for row in range(9):
        out_ref[AT_MOVED + row : AT_MOVED + row + 1, :] = jnp.sum(
            recv_ref[pl.ds(2 + row, PEERS, stride=BLOCKS), :], axis=0, keepdims=True
        )
    out_ref[AT_CAMERA : AT_CAMERA + 1, :] = shown_ref[...]
    out_ref[AT_CAMERA + 1 : AT_SHARE, :] = jnp.zeros((AT_SHARE - AT_CAMERA - 1, 128), F32)
    out_ref[AT_SHARE:SENT, :] = share_ref[...]


def log_one_plus(t):
    s = t / (2.0 + t)
    square = s * s
    total = jnp.full_like(s, 1.0 / 17.0)
    for odd in (15, 13, 11, 9, 7, 5, 3, 1):
        total = total * square + 1.0 / odd
    return 2.0 * s * total


def one_minus_exp(x):
    small = jnp.ones_like(x)
    for n in range(10, 1, -1):
        small = 1.0 + small * x * (1.0 / n)
    return jnp.where(x > -0.5, -x * small, 1.0 - jnp.exp(x))


def rates_column():
    row = lax.broadcasted_iota(I32, (59, 1), 0)
    rate = jnp.where(row < 14, 0.0025, 0.000125)
    rate = jnp.where(row < 11, 0.05, rate)
    rate = jnp.where(row < 10, 0.001, rate)
    rate = jnp.where(row < 6, 0.005, rate)
    return jnp.where(row < 3, 0.00016, rate)


def tree_sum(values):
    return (values[0] + values[1]) + (values[2] + values[3])


def adam(params, first_old, second_old, gradient):
    first = 0.9 * first_old + 0.1 * gradient
    second = 0.999 * second_old + 0.001 * gradient * gradient
    stepped = params - rates_column() * (first / BIAS_ONE) / (jnp.sqrt(second / BIAS_TWO) + 1e-15)
    return stepped, first, second


def spread_logit(logit, counts):
    soft = jnp.maximum(logit, 0.0) + log_one_plus(jnp.exp(-jnp.abs(logit)))
    share = -soft / (counts + 1.0)
    return jnp.log(one_minus_exp(share)) - share


def sigmoid_rest(logit):
    return 1.0 - 1.0 / (1.0 + jnp.exp(-logit))


def incoming_columns(parts):
    def stacked(row):
        return jnp.concatenate([ref[row : row + 1, :] for ref in parts], axis=0)

    def folded(x):
        return (x[0:1] + x[1:2]) + (x[2:3] + x[3:4])

    def wide(x):
        return jnp.broadcast_to(x, (VIEWS, 128))

    plane = jnp.full((SHARE, 128), lax.axis_index("view"), I32)
    shares = [ref[AT_SHARE:SENT, :] for ref in parts]
    for bit in (1, 2):
        flip = (plane & bit) > 0
        shares = [jnp.where(flip, shares[i ^ bit], shares[i]) for i in range(VIEWS)]
    params, first_old, second_old = [
        jnp.concatenate([part[i : i + 16] for part in shares], axis=0) for i in (0, 16, 32)
    ]
    rows = [params[i : i + 1] for i in range(59)]
    shown = stacked(AT_CAMERA)
    cam = [wide(shown[:, i : i + 1]) for i in range(16)]
    sigma, pull_sigma = jax.vjp(covariance, rows[3:6], rows[6:10])
    _, pull = jax.vjp(
        lambda p, s, c: view_rows(p, s, c, cam),
        [wide(x) for x in rows[0:3]],
        [wide(x) for x in sigma],
        [wide(x) for x in rows[11:59]],
    )
    got = [stacked(AT_MOVED + i) for i in range(9)]
    d_pos, d_sigma, d_coeff = pull([got[i] for i in (0, 1, 2, 3, 4, 6, 7, 8)])
    d_scale, d_quat = pull_sigma([folded(x) for x in d_sigma])
    d_logit = folded(got[5]) * sigmoid_rest(rows[10])
    gradient = jnp.concatenate(
        [folded(x) for x in d_pos]
        + list(d_scale)
        + list(d_quat)
        + [d_logit]
        + [folded(x) for x in d_coeff],
        axis=0,
    )
    stepped, _, _ = adam(params[0:59], first_old[0:59], second_old[0:59], gradient)
    logit = spread_logit(stepped[10:11], params[59:60])
    row = lax.broadcasted_iota(I32, (59, 128), 0)
    return jnp.concatenate(
        [jnp.where(row == 10, logit, stepped), jnp.ones((5, 128), F32)], axis=0
    )


def step_kernel(
    params_ref,
    first_ref,
    second_ref,
    own_ref,
    near_ref,
    far_ref,
    last_ref,
    counts_ref,
    targets_ref,
    new_params_ref,
    new_first_ref,
    new_second_ref,
    gradient_ref,
):
    parts = (own_ref, near_ref, far_ref, last_ref)
    targets = targets_ref[...]
    placed = add_columns(incoming_columns(parts), targets, low_onehot(targets))
    dense = params_ref[...].reshape(59, 8, 128)
    rows = [dense[i] for i in range(59)]
    sigma, pull_sigma = jax.vjp(covariance, rows[3:6], rows[6:10])
    position, coeffs = rows[0:3], rows[11:59]
    pos_parts, sigma_parts, coeff_parts, opacity_parts = [], [], [], []
    for ref in parts:
        got = [ref[8 * i : 8 * i + 8, :] for i in range(9)]
        shown = jnp.broadcast_to(ref[AT_CAMERA : AT_CAMERA + 1, :], (8, 128))
        cam = [jnp.broadcast_to(shown[:, i : i + 1], (8, 128)) for i in range(16)]
        _, pull = jax.vjp(lambda p, s, c: view_rows(p, s, c, cam), position, sigma, coeffs)
        d_pos, d_sigma, d_coeff = pull([got[i] for i in (0, 1, 2, 3, 4, 6, 7, 8)])
        pos_parts.append(d_pos)
        sigma_parts.append(d_sigma)
        coeff_parts.append(d_coeff)
        opacity_parts.append(got[5])
    d_pos = [tree_sum([p[i] for p in pos_parts]) for i in range(3)]
    d_sigma = [tree_sum([p[i] for p in sigma_parts]) for i in range(6)]
    d_coeff = [tree_sum([p[i] for p in coeff_parts]) for i in range(48)]
    d_scale, d_quat = pull_sigma(d_sigma)
    d_logit = tree_sum(opacity_parts) * sigmoid_rest(rows[10])
    gradient = jnp.stack(d_pos + list(d_scale) + list(d_quat) + [d_logit] + d_coeff).reshape(
        59, LOCAL
    )
    gradient_ref[...] = gradient
    stepped, first, second = adam(params_ref[...], first_ref[...], second_ref[...], gradient)
    counts = counts_ref[...]
    landed = placed[59:60] > 0.5
    cleared = (counts + placed[59:60]) > 0.5
    row = lax.broadcasted_iota(I32, (59, LOCAL), 0)
    spread = jnp.where(
        (row == 10) & (counts > 0.5), spread_logit(stepped[10:11], counts), stepped
    )
    new_params_ref[...] = jnp.where(landed, placed[0:59], spread)
    new_first_ref[...] = jnp.where(cleared, 0.0, first)
    new_second_ref[...] = jnp.where(cleared, 0.0, second)


def call(kernel, shapes, ins, scratch=()):
    spec = {
        "v": pl.BlockSpec(memory_space=pltpu.VMEM),
        "s": pl.BlockSpec(memory_space=pltpu.SMEM),
        "h": pl.BlockSpec(memory_space=pltpu.HBM),
    }
    out_shape = [jax.ShapeDtypeStruct(shape, dtype) for shape, dtype in shapes]
    return pl.pallas_call(
        kernel,
        out_shape=out_shape,
        in_specs=[spec[kind] for kind in ins],
        out_specs=[spec["v"]] * len(out_shape),
        scratch_shapes=list(scratch),
        compiler_params=pltpu.CompilerParams(vmem_limit_bytes=VMEM_LIMIT),
    )


def in_hbm(array):
    return pltpu.with_memory_space_constraint(array, pltpu.HBM)


def exchange(block):
    parts = block.reshape(PEERS, 1, -1)
    got = lax.all_to_all(parts, "gauss", split_axis=0, concat_axis=0, tiled=True)
    return got.reshape(block.shape)


def shards(
    params,
    first_moment,
    second_moment,
    cameras,
    target,
    tile_index,
    tile_lists,
    send_slots,
    reloc_send,
    reloc_recv,
):
    columns = ((1, LOCAL), I32)
    whole = ((59, LOCAL), F32)
    outgoing, order, entries, corners, wanted, counts, landing, shown = call(
        send_kernel,
        [
            ((3 * PEERS, 128), F32),
            columns,
            columns,
            ((2 * TILES, 256), F32),
            ((3, TILES, 256), F32),
            ((1, LOCAL), F32),
            ((1, 128), I32),
            ((1, 128), F32),
        ],
        "hhhhhhhhhh",
        [
            pltpu.VMEM((59, LOCAL), F32),
            pltpu.VMEM((59, LOCAL), F32),
            pltpu.VMEM((59, LOCAL), F32),
            pltpu.VMEM((8, 128), I32),
            pltpu.VMEM((1, 128), I32),
            pltpu.VMEM((1, 128), I32),
            pltpu.SMEM((1, 16), F32),
            pltpu.VMEM((1, TILES, 256), I32),
            pltpu.SMEM((1, TILES), I32),
            pltpu.SemaphoreType.DMA((10,)),
        ],
    )(
        in_hbm(params),
        in_hbm(first_moment),
        in_hbm(second_moment),
        in_hbm(send_slots.reshape(8, 128)),
        in_hbm(reloc_send),
        in_hbm(reloc_recv),
        in_hbm(cameras),
        in_hbm(tile_lists),
        in_hbm(tile_index),
        in_hbm(jnp.transpose(target[0], (1, 0, 2))),
    )
    received = exchange(outgoing)
    row_grads, share = call(
        render_kernel,
        [((BLOCKS * PEERS, 128), F32), ((SHARE, 128), F32)],
        "vvvv",
        [pltpu.VMEM((TILES, 256, 256), F32), pltpu.VMEM((TILES, 256, 256), F32)],
    )(received, entries, corners, wanted)
    returned = exchange(row_grads)
    (own,) = call(owner_kernel, [((SENT, 128), F32)], "vvvv")(returned, order, shown, share)
    others = [
        lax.ppermute(own, "view", [(i, i ^ flip) for i in range(VIEWS)]) for flip in (1, 2, 3)
    ]
    return call(step_kernel, [whole, whole, whole, whole], "vvvvvvvvv")(
        params, first_moment, second_moment, own, *others, counts, landing
    )


def solution(mesh):
    in_specs = (
        P(None, "gauss"),
        P(None, "gauss"),
        P(None, "gauss"),
        P("view", None),
        P("view", "gauss", None, None),
        P("view", "gauss"),
        P("view", "gauss", None),
        P("view", "gauss", None),
        P("gauss", None),
        P("gauss", None),
    )
    out_specs = (P(None, "gauss"), P(None, "gauss"), P(None, "gauss"), P(None, "gauss"))
    return jax.shard_map(shards, mesh=mesh, in_specs=in_specs, out_specs=out_specs, check_vma=False)
```

```python
import math

import jax
import jax.numpy as jnp
from jax import lax
from jax.experimental import pallas as pl
from jax.experimental.pallas import tpu as pltpu
from jax.sharding import PartitionSpec as P

F32 = jnp.float32
BF16 = jnp.bfloat16
I32 = jnp.int32
PEERS = 64
LOCAL = 1024
CAP = 16
VIEWS = 4
TILES = 4
ACROSS = 16
ROWS = 16
LOG2E = 1.4426950408889634
SHARE = 48
BLOCKS = 6
AT_MOVED = 72
AT_CAMERA = 81
AT_SHARE = 88
SENT = 136

SH_ZERO = 0.28209479177387814
SH_ONE = 0.4886025119029199
SH_TWO = (
    1.0925484305920792,
    -1.0925484305920792,
    0.31539156525252005,
    -1.0925484305920792,
    0.5462742152960396,
)
SH_THREE = (
    -0.5900435899266435,
    2.890611442640554,
    -0.4570457994644658,
    0.3731763325901154,
    -0.4570457994644658,
    1.445305721320277,
    -0.5900435899266435,
)
BIAS_ONE = 1.0 - math.exp(1000.0 * math.log(0.9))
BIAS_TWO = 1.0 - math.exp(1000.0 * math.log(0.999))
VMEM_LIMIT = 16 * 1024 * 1024


def split(x, parts):
    out = []
    for index in range(parts):
        piece = x.astype(BF16)
        out.append(piece)
        if index + 1 < parts:
            x = x - piece.astype(F32)
    return out


def low_onehot(idx):
    lane = lax.broadcasted_iota(I32, (128, idx.shape[1]), 0)
    return jnp.where(lane == (idx & 127), 1.0, 0.0).astype(BF16)


def take_columns(table, idx, hot):
    rows = table.shape[0]
    high = idx >> 7
    parts = split(table, 3)
    lhs = jnp.concatenate(
        [
            jnp.concatenate([p[:, c * 128 : (c + 1) * 128] for p in parts], axis=1)
            for c in range(8)
        ],
        axis=0,
    )
    rhs = jnp.concatenate([hot, hot, hot], axis=0)
    wide = jnp.dot(lhs, rhs, preferred_element_type=F32)
    total = None
    for c in range(8):
        term = jnp.where(high == c, wide[c * rows : (c + 1) * rows], 0.0)
        total = term if total is None else total + term
    return total


def add_columns(values, idx, hot, parts=3):
    rows = values.shape[0]
    high = idx >> 7
    pieces = []
    for piece in split(values, parts):
        piece = piece.astype(F32)
        pieces += [jnp.where(high == c, piece, 0.0) for c in range(8)]
    lhs = jnp.concatenate(pieces, axis=0).astype(BF16)
    wide = lax.dot_general(lhs, hot, (((1,), (1,)), ((), ())), preferred_element_type=F32)
    size = 8 * rows
    wide = sum(wide[i * size : (i + 1) * size] for i in range(1, parts)) + wide[0:size]
    return jnp.concatenate([wide[c * rows : (c + 1) * rows] for c in range(8)], axis=1)


def pack_peers(table):
    pieces = [table[:, k * PEERS : (k + 1) * PEERS] for k in range(CAP)]
    return jnp.concatenate(pieces, axis=0).T


def unpack_peers(block):
    flat = block.T
    return jnp.concatenate([flat[k * 8 : (k + 1) * 8] for k in range(CAP)], axis=1)


def halves(row):
    block = row.reshape(8, 128)
    return jnp.concatenate([block[:, 0:PEERS], block[:, PEERS:]], axis=0)


def joined(block):
    return jnp.concatenate([block[0:8], block[8:16]], axis=1).reshape(1, LOCAL)


def slots_by_rank(slots):
    source = lax.broadcasted_iota(I32, (128, LOCAL), 0)
    col = lax.broadcasted_iota(I32, (128, LOCAL), 1)
    pick = jnp.where(source == (col & 7) * 16 + (col >> 6), 1.0, 0.0).astype(BF16)
    upper = jnp.dot((slots >> 5).astype(F32).astype(BF16), pick, preferred_element_type=F32)
    lower = jnp.dot((slots & 31).astype(F32).astype(BF16), pick, preferred_element_type=F32)
    wide = upper * 32.0 + lower
    row = lax.broadcasted_iota(I32, (8, LOCAL), 0)
    column = lax.broadcasted_iota(I32, (8, LOCAL), 1)
    kept = jnp.where(row == ((column >> 3) & 7), wide, 0.0)
    return jnp.sum(kept, axis=0, keepdims=True).astype(I32)


def pairs_by_rank(pairs):
    source = lax.broadcasted_iota(I32, (128, 128), 0)
    col = lax.broadcasted_iota(I32, (128, 128), 1)
    pick = jnp.where(source == (col & (PEERS - 1)) * 2 + (col >> 6), 1.0, 0.0).astype(BF16)
    wide = jnp.broadcast_to(pairs + 1, (8, 128))
    upper = jnp.dot((wide >> 5).astype(F32).astype(BF16), pick, preferred_element_type=F32)
    lower = jnp.dot((wide & 31).astype(F32).astype(BF16), pick, preferred_element_type=F32)
    return (upper * 32.0 + lower)[0:1].astype(I32) - 1


def covariance(log_scale, quat):
    norm = jnp.sqrt(quat[0] * quat[0] + quat[1] * quat[1] + quat[2] * quat[2] + quat[3] * quat[3])
    quat_w, quat_x, quat_y, quat_z = [q / norm for q in quat]
    orient = [
        [
            1.0 - 2.0 * (quat_y * quat_y + quat_z * quat_z),
            2.0 * (quat_x * quat_y - quat_w * quat_z),
            2.0 * (quat_x * quat_z + quat_w * quat_y),
        ],
        [
            2.0 * (quat_x * quat_y + quat_w * quat_z),
            1.0 - 2.0 * (quat_x * quat_x + quat_z * quat_z),
            2.0 * (quat_y * quat_z - quat_w * quat_x),
        ],
        [
            2.0 * (quat_x * quat_z - quat_w * quat_y),
            2.0 * (quat_y * quat_z + quat_w * quat_x),
            1.0 - 2.0 * (quat_x * quat_x + quat_y * quat_y),
        ],
    ]
    scales = [jnp.exp(s) for s in log_scale]
    factor = [[orient[i][j] * scales[j] for j in range(3)] for i in range(3)]

    def entry(i, j):
        return (
            factor[i][0] * factor[j][0] + factor[i][1] * factor[j][1] + factor[i][2] * factor[j][2]
        )

    return [entry(0, 0), entry(0, 1), entry(0, 2), entry(1, 1), entry(1, 2), entry(2, 2)]


def harmonics(dir_x, dir_y, dir_z):
    sq_x, sq_y, sq_z = (dir_x * dir_x, dir_y * dir_y, dir_z * dir_z)
    return [
        -SH_ONE * dir_y,
        SH_ONE * dir_z,
        -SH_ONE * dir_x,
        SH_TWO[0] * dir_x * dir_y,
        SH_TWO[1] * dir_y * dir_z,
        SH_TWO[2] * (2.0 * sq_z - sq_x - sq_y),
        SH_TWO[3] * dir_x * dir_z,
        SH_TWO[4] * (sq_x - sq_y),
        SH_THREE[0] * dir_y * (3.0 * sq_x - sq_y),
        SH_THREE[1] * dir_x * dir_y * dir_z,
        SH_THREE[2] * dir_y * (4.0 * sq_z - sq_x - sq_y),
        SH_THREE[3] * dir_z * (2.0 * sq_z - 3.0 * sq_x - 3.0 * sq_y),
        SH_THREE[4] * dir_x * (4.0 * sq_z - sq_x - sq_y),
        SH_THREE[5] * dir_z * (sq_x - sq_y),
        SH_THREE[6] * dir_x * (sq_x - 3.0 * sq_y),
    ]


def view_rows(position, sigma, coeffs, cam):
    rot = [cam[0:3], cam[3:6], cam[6:9]]
    offset = cam[9:12]
    focal_x, focal_y, centre_x, centre_y = cam[12:16]
    cam_x, cam_y, cam_z = [
        rot[i][0] * position[0] + rot[i][1] * position[1] + rot[i][2] * position[2] + offset[i]
        for i in range(3)
    ]
    inverse_z = 1.0 / cam_z
    mean_u = focal_x * cam_x * inverse_z + centre_x
    mean_w = focal_y * cam_y * inverse_z + centre_y
    jac_a0 = focal_x * inverse_z
    jac_a2 = -focal_x * cam_x * inverse_z * inverse_z
    jac_b1 = focal_y * inverse_z
    jac_b2 = -focal_y * cam_y * inverse_z * inverse_z
    row_a = [jac_a0 * rot[0][i] + jac_a2 * rot[2][i] for i in range(3)]
    row_b = [jac_b1 * rot[1][i] + jac_b2 * rot[2][i] for i in range(3)]
    full = [
        [sigma[0], sigma[1], sigma[2]],
        [sigma[1], sigma[3], sigma[4]],
        [sigma[2], sigma[4], sigma[5]],
    ]

    def through(row):
        return [full[i][0] * row[0] + full[i][1] * row[1] + full[i][2] * row[2] for i in range(3)]

    def dot3(left, right):
        return left[0] * right[0] + left[1] * right[1] + left[2] * right[2]

    sigma_a = through(row_a)
    sigma_b = through(row_b)
    cov_aa = dot3(row_a, sigma_a) + 0.3
    cov_ab = dot3(row_a, sigma_b)
    cov_bb = dot3(row_b, sigma_b) + 0.3
    determinant = cov_aa * cov_bb - cov_ab * cov_ab
    inverse_det = 1.0 / determinant
    ray = [
        position[i] + (rot[0][i] * offset[0] + rot[1][i] * offset[1] + rot[2][i] * offset[2])
        for i in range(3)
    ]
    inverse_norm = 1.0 / jnp.sqrt(dot3(ray, ray))
    basis = harmonics(*[r * inverse_norm for r in ray])
    colours = []
    for channel in range(3):
        total = SH_ZERO * coeffs[channel]
        for index in range(15):
            total = total + basis[index] * coeffs[3 + 3 * index + channel]
        colours.append(jnp.maximum(total + 0.5, 0.0))
    return [
        mean_u,
        mean_w,
        cov_bb * inverse_det,
        -cov_ab * inverse_det,
        cov_aa * inverse_det,
    ] + colours


def send_kernel(
    params_hbm,
    first_hbm,
    second_hbm,
    slots_hbm,
    sources_hbm,
    targets_hbm,
    camera_hbm,
    lists_hbm,
    tiles_hbm,
    wanted_hbm,
    out_ref,
    order_ref,
    entries_ref,
    corner_ref,
    wanted_ref,
    counts_ref,
    landing_ref,
    shown_ref,
    params_ref,
    first_ref,
    second_ref,
    slots_ref,
    sources_ref,
    targets_ref,
    camera_ref,
    lists_ref,
    tiles_ref,
    sems,
):
    pairs = (
        (slots_hbm, slots_ref),
        (params_hbm, params_ref),
        (camera_hbm, camera_ref),
        (sources_hbm, sources_ref),
        (targets_hbm, targets_ref),
        (lists_hbm, lists_ref),
        (tiles_hbm, tiles_ref),
        (wanted_hbm, wanted_ref),
        (first_hbm, first_ref),
        (second_hbm, second_ref),
    )
    copies = [pltpu.make_async_copy(a, b, sems.at[i]) for i, (a, b) in enumerate(pairs)]
    for copy in copies:
        copy.start()
    for at in (0, 3, 4):
        copies[at].wait()
    order = slots_by_rank(slots_ref[...])
    order_ref[...] = order
    hot = low_onehot(order)
    sources = pairs_by_rank(sources_ref[...])
    source_hot = low_onehot(sources)
    counts = add_columns(jnp.ones((8, 128), F32), sources, source_hot, 1)[0:1]
    counts_ref[...] = counts
    out_ref[pl.ds(2, PEERS, stride=3), :] = jnp.broadcast_to(sources.astype(F32), (PEERS, 128))
    landing_ref[...] = pairs_by_rank(targets_ref[...])
    for at in (1, 2, 5, 6, 7, 8, 9):
        copies[at].wait()
    dense = params_ref[...].reshape(59, 8, 128)
    rows = [dense[i] for i in range(59)]
    cam = [camera_ref[0, i] for i in range(16)]
    sigma = covariance(rows[3:6], rows[6:10])
    seen = view_rows(rows[0:3], sigma, rows[11:59], cam)
    opacity = 1.0 / (1.0 + jnp.exp(-rows[10]))
    listed = seen[0:5] + [opacity] + seen[5:8]
    blank = jnp.zeros((8, 128), F32)
    table = jnp.stack(listed + [blank] * (ROWS - 9)).reshape(ROWS, LOCAL)
    taken = take_columns(table, order, hot)
    out_ref[pl.ds(0, PEERS, stride=3), :] = pack_peers(taken[0:8])
    plane = jnp.full((16, LOCAL), lax.axis_index("view"), I32)
    share = []
    for ref in (params_ref, first_ref, second_ref):
        final = jnp.concatenate([ref[48:59, :], jnp.broadcast_to(counts, (5, LOCAL))], axis=0)
        low = jnp.where(plane == 0, ref[0:16, :], ref[16:32, :])
        share.append(jnp.where(plane < 2, low, jnp.where(plane == 2, ref[32:48, :], final)))
    moved = take_columns(jnp.concatenate(share, axis=0), sources, source_hot)
    moved = jnp.concatenate([moved[:, 0:PEERS], moved[:, PEERS:]], axis=0)
    flat = jnp.concatenate([halves(taken[8:9]), halves(order.astype(F32)), moved], axis=0)
    out_ref[pl.ds(1, PEERS, stride=3), :] = flat.T
    entries_ref[...] = jnp.concatenate([lists_ref[0, i : i + 1] for i in range(TILES)], axis=1)
    for tile in range(TILES):
        number = tiles_ref[0, tile]
        corner_ref[tile : tile + 1, :] = jnp.full(
            (1, 256), ((number & (ACROSS - 1)) * 16).astype(F32)
        )
        corner_ref[TILES + tile : TILES + tile + 1, :] = jnp.full(
            (1, 256), ((number >> 4) * 16).astype(F32)
        )
    lane = lax.broadcasted_iota(I32, (1, 128), 1)
    shown = jnp.zeros((1, 128), F32)
    for i in range(16):
        shown = jnp.where(lane == i, cam[i], shown)
    shown_ref[...] = shown


def render_kernel(
    recv_ref, entries_ref, corner_ref, target_ref, out_ref, give_ref, share_ref, alpha_ref, grad_ref
):
    lead = recv_ref[pl.ds(0, PEERS, stride=3), :]
    tail = recv_ref[pl.ds(1, PEERS, stride=3), :]
    sources = recv_ref[pl.ds(2, PEERS, stride=3), :]
    flat = tail.T
    share_ref[...] = jnp.concatenate([flat[32 : 32 + SHARE], flat[32 + SHARE :]], axis=1)
    numbers = joined(flat[16:32])
    table = jnp.concatenate(
        [unpack_peers(lead), joined(flat[0:16]), jnp.zeros((ROWS - 9, LOCAL), F32)], axis=0
    )
    entries = entries_ref[...]
    idx = jnp.where(entries < 0, -1, (entries & 15) * PEERS + (entries >> 4))
    hot = low_onehot(idx)
    listed = take_columns(table, idx, hot)
    iota_r = lax.broadcasted_iota(I32, (256, 256), 0)
    iota_c = lax.broadcasted_iota(I32, (256, 256), 1)
    before_mask = jnp.where(iota_r < iota_c, 1.0, 0.0).astype(BF16)
    before_mask = jnp.concatenate([before_mask, before_mask], axis=0)
    after_mask = jnp.where(iota_r > iota_c, 1.0, 0.0).astype(BF16)
    after_mask = jnp.concatenate([after_mask, after_mask], axis=0)
    steps = lax.broadcasted_iota(I32, (16, 256), 0).astype(F32)
    nt = (((1,), (1,)), ((), ()))
    tiles = range(TILES)
    heres, offs_u, offs_w = [], [], []
    for tile in tiles:
        here = listed[:, tile * 256 : (tile + 1) * 256]
        left = corner_ref[tile : tile + 1]
        top = corner_ref[TILES + tile : TILES + tile + 1]
        con_a, con_b, con_c, opacity = here[2:3], here[3:4], here[4:5], here[5:6]
        off_u = (steps + left + 0.5) - here[0:1]
        off_w = (steps + top + 0.5) - here[1:2]
        quad_u = LOG2E * (jnp.log(opacity) - 0.5 * con_a * off_u * off_u)
        cross = -LOG2E * con_b * off_u
        quad_w = (-0.5 * LOG2E) * con_c * off_w * off_w
        for j in range(16):
            exponent = quad_u + quad_w[j : j + 1] + cross * off_w[j : j + 1]
            alpha_ref[tile, j * 16 : (j + 1) * 16, :] = jnp.exp2(exponent)
        heres.append(here)
        offs_u.append(off_u)
        offs_w.append(off_w)
    log_keeps = [jnp.log(1.0 - alpha_ref[t]) for t in tiles]
    logs = [jnp.concatenate(split(x, 2), axis=1) for x in log_keeps]
    befores = [jnp.dot(x, before_mask, preferred_element_type=F32) for x in logs]
    weights = [jnp.exp(befores[t]) * alpha_ref[t] for t in tiles]
    weight_parts = [split(x, 2) for x in weights]
    colour_parts = [split(here[6:9], 3) for here in heres]
    residual_parts = []
    for tile in tiles:
        stacked = jnp.concatenate(
            [p.astype(F32) for p in colour_parts[tile]] + [jnp.zeros((7, 256), F32)], axis=0
        ).astype(BF16)
        summed = lax.dot_general(
            jnp.concatenate([stacked, stacked], axis=1),
            jnp.concatenate(weight_parts[tile], axis=1),
            nt,
            preferred_element_type=F32,
        )
        residual = summed[0:3] + summed[3:6] + summed[6:9] - target_ref[:, tile]
        residual_parts.append([p.astype(F32) for p in split(residual, 3)])
    pairs = ((0, 0), (0, 1), (1, 0), (1, 1), (0, 2), (2, 0))
    blank = jnp.zeros((14, 256), F32)
    pulls = []
    for tile in tiles:
        left_side = jnp.concatenate([residual_parts[tile][a] for a, _ in pairs] + [blank], axis=0)
        right_side = jnp.concatenate(
            [colour_parts[tile][b].astype(F32) for _, b in pairs] + [blank], axis=0
        )
        pulls.append(
            lax.dot_general(
                left_side.astype(BF16),
                right_side.astype(BF16),
                (((0,), (0,)), ((), ())),
                preferred_element_type=F32,
            )
        )
    weighteds = [pulls[t] * weights[t] for t in tiles]
    flows = [jnp.concatenate(split(x, 2), axis=1) for x in weighteds]
    afters = [jnp.dot(x, after_mask, preferred_element_type=F32) for x in flows]
    for t in tiles:
        grad_ref[t] = weighteds[t] - afters[t] * (alpha_ref[t] * jnp.exp(-log_keeps[t]))
    results = []
    for tile in tiles:
        here, off_u, off_w = heres[tile], offs_u[tile], offs_w[tile]
        con_a, con_b, con_c = here[2:3], here[3:4], here[4:5]
        stacked_res = jnp.concatenate(
            residual_parts[tile] + [jnp.zeros((7, 256), F32)], axis=0
        ).astype(BF16)
        colour_sum = jnp.dot(
            jnp.concatenate([stacked_res, stacked_res], axis=1),
            jnp.concatenate(weight_parts[tile], axis=0),
            preferred_element_type=F32,
        )
        colour_grad = colour_sum[0:3] + colour_sum[3:6] + colour_sum[6:9]
        zeroth = first = second = grad_ref[tile, 240:256, :]
        for j in range(14, -1, -1):
            zeroth = zeroth + grad_ref[tile, j * 16 : (j + 1) * 16, :]
            first = first + zeroth
            second = second + first
        start = off_w[0:1]
        by_step = first - zeroth
        by_square = 2.0 * second - 3.0 * by_step - 2.0 * zeroth
        first = start * zeroth + by_step
        second = start * (first + by_step) + by_square

        def over(values):
            return jnp.sum(values, axis=0, keepdims=True)

        along = zeroth * off_u
        m_00, m_10, m_20 = over(zeroth), over(along), over(along * off_u)
        m_01, m_11, m_02 = over(first), over(first * off_u), over(second)
        results.append(
            jnp.concatenate(
                [
                    con_a * m_10 + con_b * m_01,
                    con_c * m_01 + con_b * m_10,
                    -0.5 * m_20,
                    -m_11,
                    -0.5 * m_02,
                    m_00,
                    colour_grad,
                    jnp.zeros((ROWS - 9, 256), F32),
                ],
                axis=0,
            )
        )
    grads = jnp.concatenate(results, axis=1)
    summed = add_columns(grads, idx, hot, 2)
    out_ref[pl.ds(0, PEERS, stride=BLOCKS), :] = pack_peers(summed[0:8])
    give_ref[pl.ds(0, PEERS, stride=BLOCKS), :] = jnp.zeros((PEERS, 128), F32)
    flat = jnp.concatenate([halves(summed[8:9]), jnp.zeros((112, PEERS), F32)], axis=0)
    ninth = flat.T
    odd = jnp.full((8, 128), lax.axis_index("gauss") & 1, I32) > 0
    right = lax.broadcasted_iota(I32, (8, 128), 1) >= PEERS
    turned = sources.T
    wanted = jnp.concatenate([turned[0:PEERS], turned[PEERS:]], axis=1)
    rows = [[] for _ in range(10)]
    for k in range(CAP):
        span = slice(k * PEERS, (k + 1) * PEERS)
        lines = jnp.concatenate([summed[0:9, span], numbers[:, span]], axis=0)
        lines = jnp.concatenate([lines, lines], axis=1)
        for row in range(10):
            rows[row].append(jnp.broadcast_to(lines[row : row + 1], (8, 128)))
    for group in range(PEERS // 8):
        ask = wanted[group * 8 : (group + 1) * 8]
        totals = [None] * 9
        for k in range(CAP):
            same = ask == rows[9][k]
            for row in range(9):
                term = jnp.where(same, rows[row][k], 0.0)
                totals[row] = term if k == 0 else totals[row] + term
        start = group * 8 * BLOCKS
        turn = pltpu.roll(totals[8], PEERS, axis=1)
        keep = jnp.where(odd, totals[8], turn)
        give = jnp.where(odd, turn, totals[8])
        at = pl.ds(start + 1, 8, stride=BLOCKS)
        out_ref[at, :] = jnp.where(right, keep, ninth[group * 8 : (group + 1) * 8])
        give_ref[at, :] = jnp.where(right, give, 0.0)
        for row in range(4):
            at = pl.ds(start + 2 + row, 8, stride=BLOCKS)
            out_ref[at, :] = jnp.where(odd, totals[4 + row], totals[row])
            give_ref[at, :] = jnp.where(odd, totals[row], totals[4 + row])


def owner_kernel(recv_ref, order_ref, shown_ref, share_ref, out_ref):
    lead = unpack_peers(recv_ref[pl.ds(0, PEERS, stride=BLOCKS), :])
    last = joined(recv_ref[pl.ds(1, PEERS, stride=BLOCKS), :].T[0:16])
    values = jnp.concatenate([lead, last, jnp.zeros((ROWS - 9, LOCAL), F32)], axis=0)
    order = order_ref[...]
    owned = add_columns(values, order, low_onehot(order), 2)
    out_ref[0:AT_MOVED, :] = owned[0:9].reshape(9, 8, 128).reshape(AT_MOVED, 128)
    odd = (lax.broadcasted_iota(I32, (PEERS, 128), 0) & 1) > 0

    def sums(block):
        values = recv_ref[pl.ds(block, PEERS, stride=BLOCKS), :]
        return [
            jnp.sum(jnp.where(odd, 0.0, values), axis=0, keepdims=True),
            jnp.sum(jnp.where(odd, values, 0.0), axis=0, keepdims=True),
        ]

    for row in range(4):
        even_sum, odd_sum = sums(2 + row)
        out_ref[AT_MOVED + row : AT_MOVED + row + 1, :] = even_sum
        out_ref[AT_MOVED + 4 + row : AT_MOVED + 5 + row, :] = odd_sum
    even_sum, odd_sum = sums(1)
    out_ref[AT_MOVED + 8 : AT_MOVED + 9, :] = jnp.concatenate(
        [even_sum[:, PEERS:], odd_sum[:, PEERS:]], axis=1
    )
    out_ref[AT_CAMERA : AT_CAMERA + 1, :] = shown_ref[...]
    out_ref[AT_CAMERA + 1 : AT_SHARE, :] = jnp.zeros((AT_SHARE - AT_CAMERA - 1, 128), F32)
    out_ref[AT_SHARE:SENT, :] = share_ref[...]


def log_one_plus(t):
    s = t / (2.0 + t)
    square = s * s
    total = jnp.full_like(s, 1.0 / 17.0)
    for odd in (15, 13, 11, 9, 7, 5, 3, 1):
        total = total * square + 1.0 / odd
    return 2.0 * s * total


def one_minus_exp(x):
    small = jnp.ones_like(x)
    for n in range(10, 1, -1):
        small = 1.0 + small * x * (1.0 / n)
    return jnp.where(x > -0.5, -x * small, 1.0 - jnp.exp(x))


def rates_column():
    row = lax.broadcasted_iota(I32, (59, 1), 0)
    rate = jnp.where(row < 14, 0.0025, 0.000125)
    rate = jnp.where(row < 11, 0.05, rate)
    rate = jnp.where(row < 10, 0.001, rate)
    rate = jnp.where(row < 6, 0.005, rate)
    return jnp.where(row < 3, 0.00016, rate)


def tree_sum(values):
    return (values[0] + values[1]) + (values[2] + values[3])


def adam(params, first_old, second_old, gradient):
    first = 0.9 * first_old + 0.1 * gradient
    second = 0.999 * second_old + 0.001 * gradient * gradient
    stepped = params - rates_column() * (first / BIAS_ONE) / (jnp.sqrt(second / BIAS_TWO) + 1e-15)
    return stepped, first, second


def spread_logit(logit, counts):
    soft = jnp.maximum(logit, 0.0) + log_one_plus(jnp.exp(-jnp.abs(logit)))
    share = -soft / (counts + 1.0)
    return jnp.log(one_minus_exp(share)) - share


def sigmoid_rest(logit):
    return 1.0 - 1.0 / (1.0 + jnp.exp(-logit))


def incoming_columns(parts):
    def stacked(row):
        return jnp.concatenate([ref[row : row + 1, :] for ref in parts], axis=0)

    def folded(x):
        return (x[0:1] + x[1:2]) + (x[2:3] + x[3:4])

    def wide(x):
        return jnp.broadcast_to(x, (VIEWS, 128))

    plane = jnp.full((SHARE, 128), lax.axis_index("view"), I32)
    shares = [ref[AT_SHARE:SENT, :] for ref in parts]
    for bit in (1, 2):
        flip = (plane & bit) > 0
        shares = [jnp.where(flip, shares[i ^ bit], shares[i]) for i in range(VIEWS)]
    params, first_old, second_old = [
        jnp.concatenate([part[i : i + 16] for part in shares], axis=0) for i in (0, 16, 32)
    ]
    rows = [params[i : i + 1] for i in range(59)]
    shown = stacked(AT_CAMERA)
    cam = [wide(shown[:, i : i + 1]) for i in range(16)]
    sigma, pull_sigma = jax.vjp(covariance, rows[3:6], rows[6:10])
    _, pull = jax.vjp(
        lambda p, s, c: view_rows(p, s, c, cam),
        [wide(x) for x in rows[0:3]],
        [wide(x) for x in sigma],
        [wide(x) for x in rows[11:59]],
    )
    got = [stacked(AT_MOVED + i) for i in range(9)]
    d_pos, d_sigma, d_coeff = pull([got[i] for i in (0, 1, 2, 3, 4, 6, 7, 8)])
    d_scale, d_quat = pull_sigma([folded(x) for x in d_sigma])
    d_logit = folded(got[5]) * sigmoid_rest(rows[10])
    gradient = jnp.concatenate(
        [folded(x) for x in d_pos]
        + list(d_scale)
        + list(d_quat)
        + [d_logit]
        + [folded(x) for x in d_coeff],
        axis=0,
    )
    stepped, _, _ = adam(params[0:59], first_old[0:59], second_old[0:59], gradient)
    logit = spread_logit(stepped[10:11], params[59:60])
    row = lax.broadcasted_iota(I32, (59, 128), 0)
    return jnp.concatenate(
        [jnp.where(row == 10, logit, stepped), jnp.ones((5, 128), F32)], axis=0
    )


def step_kernel(
    params_ref,
    first_ref,
    second_ref,
    own_ref,
    near_ref,
    far_ref,
    last_ref,
    counts_ref,
    targets_ref,
    new_params_ref,
    new_first_ref,
    new_second_ref,
    gradient_ref,
):
    parts = (own_ref, near_ref, far_ref, last_ref)
    targets = targets_ref[...]
    placed = add_columns(incoming_columns(parts), targets, low_onehot(targets))
    dense = params_ref[...].reshape(59, 8, 128)
    rows = [dense[i] for i in range(59)]
    sigma, pull_sigma = jax.vjp(covariance, rows[3:6], rows[6:10])
    position, coeffs = rows[0:3], rows[11:59]
    pos_parts, sigma_parts, coeff_parts, opacity_parts = [], [], [], []
    for ref in parts:
        got = [ref[8 * i : 8 * i + 8, :] for i in range(9)]
        shown = jnp.broadcast_to(ref[AT_CAMERA : AT_CAMERA + 1, :], (8, 128))
        cam = [jnp.broadcast_to(shown[:, i : i + 1], (8, 128)) for i in range(16)]
        _, pull = jax.vjp(lambda p, s, c: view_rows(p, s, c, cam), position, sigma, coeffs)
        d_pos, d_sigma, d_coeff = pull([got[i] for i in (0, 1, 2, 3, 4, 6, 7, 8)])
        pos_parts.append(d_pos)
        sigma_parts.append(d_sigma)
        coeff_parts.append(d_coeff)
        opacity_parts.append(got[5])
    d_pos = [tree_sum([p[i] for p in pos_parts]) for i in range(3)]
    d_sigma = [tree_sum([p[i] for p in sigma_parts]) for i in range(6)]
    d_coeff = [tree_sum([p[i] for p in coeff_parts]) for i in range(48)]
    d_scale, d_quat = pull_sigma(d_sigma)
    d_logit = tree_sum(opacity_parts) * sigmoid_rest(rows[10])
    gradient = jnp.stack(d_pos + list(d_scale) + list(d_quat) + [d_logit] + d_coeff).reshape(
        59, LOCAL
    )
    gradient_ref[...] = gradient
    stepped, first, second = adam(params_ref[...], first_ref[...], second_ref[...], gradient)
    counts = counts_ref[...]
    landed = placed[59:60] > 0.5
    cleared = (counts + placed[59:60]) > 0.5
    row = lax.broadcasted_iota(I32, (59, LOCAL), 0)
    spread = jnp.where(
        (row == 10) & (counts > 0.5), spread_logit(stepped[10:11], counts), stepped
    )
    new_params_ref[...] = jnp.where(landed, placed[0:59], spread)
    new_first_ref[...] = jnp.where(cleared, 0.0, first)
    new_second_ref[...] = jnp.where(cleared, 0.0, second)


def call(kernel, shapes, ins, scratch=()):
    spec = {
        "v": pl.BlockSpec(memory_space=pltpu.VMEM),
        "s": pl.BlockSpec(memory_space=pltpu.SMEM),
        "h": pl.BlockSpec(memory_space=pltpu.HBM),
    }
    out_shape = [jax.ShapeDtypeStruct(shape, dtype) for shape, dtype in shapes]
    return pl.pallas_call(
        kernel,
        out_shape=out_shape,
        in_specs=[spec[kind] for kind in ins],
        out_specs=[spec["v"]] * len(out_shape),
        scratch_shapes=list(scratch),
        compiler_params=pltpu.CompilerParams(vmem_limit_bytes=VMEM_LIMIT),
    )


def in_hbm(array):
    return pltpu.with_memory_space_constraint(array, pltpu.HBM)


def exchange(block):
    parts = block.reshape(PEERS, 1, -1)
    got = lax.all_to_all(parts, "gauss", split_axis=0, concat_axis=0, tiled=True)
    return got.reshape(block.shape)


def shards(
    params,
    first_moment,
    second_moment,
    cameras,
    target,
    tile_index,
    tile_lists,
    send_slots,
    reloc_send,
    reloc_recv,
):
    columns = ((1, LOCAL), I32)
    whole = ((59, LOCAL), F32)
    outgoing, order, entries, corners, wanted, counts, landing, shown = call(
        send_kernel,
        [
            ((3 * PEERS, 128), F32),
            columns,
            columns,
            ((2 * TILES, 256), F32),
            ((3, TILES, 256), F32),
            ((1, LOCAL), F32),
            ((1, 128), I32),
            ((1, 128), F32),
        ],
        "hhhhhhhhhh",
        [
            pltpu.VMEM((59, LOCAL), F32),
            pltpu.VMEM((59, LOCAL), F32),
            pltpu.VMEM((59, LOCAL), F32),
            pltpu.VMEM((8, 128), I32),
            pltpu.VMEM((1, 128), I32),
            pltpu.VMEM((1, 128), I32),
            pltpu.SMEM((1, 16), F32),
            pltpu.VMEM((1, TILES, 256), I32),
            pltpu.SMEM((1, TILES), I32),
            pltpu.SemaphoreType.DMA((10,)),
        ],
    )(
        in_hbm(params),
        in_hbm(first_moment),
        in_hbm(second_moment),
        in_hbm(send_slots.reshape(8, 128)),
        in_hbm(reloc_send),
        in_hbm(reloc_recv),
        in_hbm(cameras),
        in_hbm(tile_lists),
        in_hbm(tile_index),
        in_hbm(jnp.transpose(target[0], (1, 0, 2))),
    )
    received = exchange(outgoing)
    back = ((BLOCKS * PEERS, 128), F32)
    row_grads, give, share = call(
        render_kernel,
        [back, back, ((SHARE, 128), F32)],
        "vvvv",
        [pltpu.VMEM((TILES, 256, 256), F32), pltpu.VMEM((TILES, 256, 256), F32)],
    )(received, entries, corners, wanted)
    sibling = lax.ppermute(give, "gauss", [(i, i ^ 1) for i in range(PEERS)])
    returned = exchange(row_grads + sibling)
    (own,) = call(owner_kernel, [((SENT, 128), F32)], "vvvv")(returned, order, shown, share)
    others = [
        lax.ppermute(own, "view", [(i, i ^ flip) for i in range(VIEWS)]) for flip in (1, 2, 3)
    ]
    return call(step_kernel, [whole, whole, whole, whole], "vvvvvvvvv")(
        params, first_moment, second_moment, own, *others, counts, landing
    )


def solution(mesh):
    in_specs = (
        P(None, "gauss"),
        P(None, "gauss"),
        P(None, "gauss"),
        P("view", None),
        P("view", "gauss", None, None),
        P("view", "gauss"),
        P("view", "gauss", None),
        P("view", "gauss", None),
        P("gauss", None),
        P("gauss", None),
    )
    out_specs = (P(None, "gauss"), P(None, "gauss"), P(None, "gauss"), P(None, "gauss"))
    return jax.shard_map(shards, mesh=mesh, in_specs=in_specs, out_specs=out_specs, check_vma=False)
```

```python
import math

import jax
import jax.numpy as jnp
from jax import lax
from jax.experimental import pallas as pl
from jax.experimental.pallas import tpu as pltpu
from jax.sharding import PartitionSpec as P

F32 = jnp.float32
BF16 = jnp.bfloat16
I32 = jnp.int32
PEERS = 64
LOCAL = 1024
CAP = 16
VIEWS = 4
TILES = 4
ACROSS = 16
ROWS = 16
LOG2E = 1.4426950408889634
SHARE = 48
BLOCKS = 6
AT_MOVED = 72
AT_CAMERA = 81
AT_SHARE = 88
SENT = 136

SH_ZERO = 0.28209479177387814
SH_ONE = 0.4886025119029199
SH_TWO = (
    1.0925484305920792,
    -1.0925484305920792,
    0.31539156525252005,
    -1.0925484305920792,
    0.5462742152960396,
)
SH_THREE = (
    -0.5900435899266435,
    2.890611442640554,
    -0.4570457994644658,
    0.3731763325901154,
    -0.4570457994644658,
    1.445305721320277,
    -0.5900435899266435,
)
BIAS_ONE = 1.0 - math.exp(1000.0 * math.log(0.9))
BIAS_TWO = 1.0 - math.exp(1000.0 * math.log(0.999))
VMEM_LIMIT = 16 * 1024 * 1024


def split(x, parts):
    out = []
    for index in range(parts):
        piece = x.astype(BF16)
        out.append(piece)
        if index + 1 < parts:
            x = x - piece.astype(F32)
    return out


def low_onehot(idx):
    lane = lax.broadcasted_iota(I32, (128, idx.shape[1]), 0)
    return jnp.where(lane == (idx & 127), 1.0, 0.0).astype(BF16)


def take_columns(table, idx, hot):
    rows = table.shape[0]
    high = idx >> 7
    parts = split(table, 3)
    lhs = jnp.concatenate(
        [
            jnp.concatenate([p[:, c * 128 : (c + 1) * 128] for p in parts], axis=1)
            for c in range(8)
        ],
        axis=0,
    )
    rhs = jnp.concatenate([hot, hot, hot], axis=0)
    wide = jnp.dot(lhs, rhs, preferred_element_type=F32)
    total = None
    for c in range(8):
        term = jnp.where(high == c, wide[c * rows : (c + 1) * rows], 0.0)
        total = term if total is None else total + term
    return total


def add_columns(values, idx, hot, parts=3):
    rows = values.shape[0]
    high = idx >> 7
    pieces = []
    for piece in split(values, parts):
        piece = piece.astype(F32)
        pieces += [jnp.where(high == c, piece, 0.0) for c in range(8)]
    lhs = jnp.concatenate(pieces, axis=0).astype(BF16)
    wide = lax.dot_general(lhs, hot, (((1,), (1,)), ((), ())), preferred_element_type=F32)
    size = 8 * rows
    wide = sum(wide[i * size : (i + 1) * size] for i in range(1, parts)) + wide[0:size]
    return jnp.concatenate([wide[c * rows : (c + 1) * rows] for c in range(8)], axis=1)


def pack_peers(table):
    pieces = [table[:, k * PEERS : (k + 1) * PEERS] for k in range(CAP)]
    return jnp.concatenate(pieces, axis=0).T


def unpack_peers(block):
    flat = block.T
    return jnp.concatenate([flat[k * 8 : (k + 1) * 8] for k in range(CAP)], axis=1)


def halves(row):
    block = row.reshape(8, 128)
    return jnp.concatenate([block[:, 0:PEERS], block[:, PEERS:]], axis=0)


def joined(block):
    return jnp.concatenate([block[0:8], block[8:16]], axis=1).reshape(1, LOCAL)


def slots_by_rank(slots):
    source = lax.broadcasted_iota(I32, (128, LOCAL), 0)
    col = lax.broadcasted_iota(I32, (128, LOCAL), 1)
    pick = jnp.where(source == (col & 7) * 16 + (col >> 6), 1.0, 0.0).astype(BF16)
    upper = jnp.dot((slots >> 5).astype(F32).astype(BF16), pick, preferred_element_type=F32)
    lower = jnp.dot((slots & 31).astype(F32).astype(BF16), pick, preferred_element_type=F32)
    wide = upper * 32.0 + lower
    row = lax.broadcasted_iota(I32, (8, LOCAL), 0)
    column = lax.broadcasted_iota(I32, (8, LOCAL), 1)
    kept = jnp.where(row == ((column >> 3) & 7), wide, 0.0)
    return jnp.sum(kept, axis=0, keepdims=True).astype(I32)


def pairs_by_rank(pairs):
    source = lax.broadcasted_iota(I32, (128, 128), 0)
    col = lax.broadcasted_iota(I32, (128, 128), 1)
    pick = jnp.where(source == (col & (PEERS - 1)) * 2 + (col >> 6), 1.0, 0.0).astype(BF16)
    wide = jnp.broadcast_to(pairs + 1, (8, 128))
    upper = jnp.dot((wide >> 5).astype(F32).astype(BF16), pick, preferred_element_type=F32)
    lower = jnp.dot((wide & 31).astype(F32).astype(BF16), pick, preferred_element_type=F32)
    return (upper * 32.0 + lower)[0:1].astype(I32) - 1


def covariance(log_scale, quat):
    norm = jnp.sqrt(quat[0] * quat[0] + quat[1] * quat[1] + quat[2] * quat[2] + quat[3] * quat[3])
    quat_w, quat_x, quat_y, quat_z = [q / norm for q in quat]
    orient = [
        [
            1.0 - 2.0 * (quat_y * quat_y + quat_z * quat_z),
            2.0 * (quat_x * quat_y - quat_w * quat_z),
            2.0 * (quat_x * quat_z + quat_w * quat_y),
        ],
        [
            2.0 * (quat_x * quat_y + quat_w * quat_z),
            1.0 - 2.0 * (quat_x * quat_x + quat_z * quat_z),
            2.0 * (quat_y * quat_z - quat_w * quat_x),
        ],
        [
            2.0 * (quat_x * quat_z - quat_w * quat_y),
            2.0 * (quat_y * quat_z + quat_w * quat_x),
            1.0 - 2.0 * (quat_x * quat_x + quat_y * quat_y),
        ],
    ]
    scales = [jnp.exp(s) for s in log_scale]
    factor = [[orient[i][j] * scales[j] for j in range(3)] for i in range(3)]

    def entry(i, j):
        return (
            factor[i][0] * factor[j][0] + factor[i][1] * factor[j][1] + factor[i][2] * factor[j][2]
        )

    return [entry(0, 0), entry(0, 1), entry(0, 2), entry(1, 1), entry(1, 2), entry(2, 2)]


def harmonics(dir_x, dir_y, dir_z):
    sq_x, sq_y, sq_z = (dir_x * dir_x, dir_y * dir_y, dir_z * dir_z)
    return [
        -SH_ONE * dir_y,
        SH_ONE * dir_z,
        -SH_ONE * dir_x,
        SH_TWO[0] * dir_x * dir_y,
        SH_TWO[1] * dir_y * dir_z,
        SH_TWO[2] * (2.0 * sq_z - sq_x - sq_y),
        SH_TWO[3] * dir_x * dir_z,
        SH_TWO[4] * (sq_x - sq_y),
        SH_THREE[0] * dir_y * (3.0 * sq_x - sq_y),
        SH_THREE[1] * dir_x * dir_y * dir_z,
        SH_THREE[2] * dir_y * (4.0 * sq_z - sq_x - sq_y),
        SH_THREE[3] * dir_z * (2.0 * sq_z - 3.0 * sq_x - 3.0 * sq_y),
        SH_THREE[4] * dir_x * (4.0 * sq_z - sq_x - sq_y),
        SH_THREE[5] * dir_z * (sq_x - sq_y),
        SH_THREE[6] * dir_x * (sq_x - 3.0 * sq_y),
    ]


def view_rows(position, sigma, coeffs, cam):
    rot = [cam[0:3], cam[3:6], cam[6:9]]
    offset = cam[9:12]
    focal_x, focal_y, centre_x, centre_y = cam[12:16]
    cam_x, cam_y, cam_z = [
        rot[i][0] * position[0] + rot[i][1] * position[1] + rot[i][2] * position[2] + offset[i]
        for i in range(3)
    ]
    inverse_z = 1.0 / cam_z
    mean_u = focal_x * cam_x * inverse_z + centre_x
    mean_w = focal_y * cam_y * inverse_z + centre_y
    jac_a0 = focal_x * inverse_z
    jac_a2 = -focal_x * cam_x * inverse_z * inverse_z
    jac_b1 = focal_y * inverse_z
    jac_b2 = -focal_y * cam_y * inverse_z * inverse_z
    row_a = [jac_a0 * rot[0][i] + jac_a2 * rot[2][i] for i in range(3)]
    row_b = [jac_b1 * rot[1][i] + jac_b2 * rot[2][i] for i in range(3)]
    full = [
        [sigma[0], sigma[1], sigma[2]],
        [sigma[1], sigma[3], sigma[4]],
        [sigma[2], sigma[4], sigma[5]],
    ]

    def through(row):
        return [full[i][0] * row[0] + full[i][1] * row[1] + full[i][2] * row[2] for i in range(3)]

    def dot3(left, right):
        return left[0] * right[0] + left[1] * right[1] + left[2] * right[2]

    sigma_a = through(row_a)
    sigma_b = through(row_b)
    cov_aa = dot3(row_a, sigma_a) + 0.3
    cov_ab = dot3(row_a, sigma_b)
    cov_bb = dot3(row_b, sigma_b) + 0.3
    determinant = cov_aa * cov_bb - cov_ab * cov_ab
    inverse_det = 1.0 / determinant
    ray = [
        position[i] + (rot[0][i] * offset[0] + rot[1][i] * offset[1] + rot[2][i] * offset[2])
        for i in range(3)
    ]
    inverse_norm = 1.0 / jnp.sqrt(dot3(ray, ray))
    basis = harmonics(*[r * inverse_norm for r in ray])
    colours = []
    for channel in range(3):
        total = SH_ZERO * coeffs[channel]
        for index in range(15):
            total = total + basis[index] * coeffs[3 + 3 * index + channel]
        colours.append(jnp.maximum(total + 0.5, 0.0))
    return [
        mean_u,
        mean_w,
        cov_bb * inverse_det,
        -cov_ab * inverse_det,
        cov_aa * inverse_det,
    ] + colours


def send_kernel(
    params_hbm,
    first_hbm,
    second_hbm,
    slots_hbm,
    sources_hbm,
    targets_hbm,
    camera_hbm,
    lists_hbm,
    tiles_hbm,
    wanted_hbm,
    out_ref,
    order_ref,
    entries_ref,
    corner_ref,
    wanted_ref,
    counts_ref,
    landing_ref,
    shown_ref,
    params_ref,
    first_ref,
    second_ref,
    slots_ref,
    sources_ref,
    targets_ref,
    camera_ref,
    lists_ref,
    tiles_ref,
    sems,
):
    pairs = (
        (slots_hbm, slots_ref),
        (params_hbm, params_ref),
        (camera_hbm, camera_ref),
        (sources_hbm, sources_ref),
        (targets_hbm, targets_ref),
        (lists_hbm, lists_ref),
        (tiles_hbm, tiles_ref),
        (wanted_hbm, wanted_ref),
        (first_hbm, first_ref),
        (second_hbm, second_ref),
    )
    copies = [pltpu.make_async_copy(a, b, sems.at[i]) for i, (a, b) in enumerate(pairs)]
    for copy in copies:
        copy.start()
    for at in (0, 3, 4):
        copies[at].wait()
    order = slots_by_rank(slots_ref[...])
    order_ref[...] = order
    hot = low_onehot(order)
    sources = pairs_by_rank(sources_ref[...])
    source_hot = low_onehot(sources)
    counts = add_columns(jnp.ones((8, 128), F32), sources, source_hot, 1)[0:1]
    counts_ref[...] = counts
    out_ref[pl.ds(2, PEERS, stride=3), :] = jnp.broadcast_to(sources.astype(F32), (PEERS, 128))
    landing_ref[...] = pairs_by_rank(targets_ref[...])
    for at in (1, 2, 5, 6, 7, 8, 9):
        copies[at].wait()
    dense = params_ref[...].reshape(59, 8, 128)
    rows = [dense[i] for i in range(59)]
    cam = [camera_ref[0, i] for i in range(16)]
    sigma = covariance(rows[3:6], rows[6:10])
    seen = view_rows(rows[0:3], sigma, rows[11:59], cam)
    opacity = 1.0 / (1.0 + jnp.exp(-rows[10]))
    listed = seen[0:5] + [opacity] + seen[5:8]
    blank = jnp.zeros((8, 128), F32)
    table = jnp.stack(listed + [blank] * (ROWS - 9)).reshape(ROWS, LOCAL)
    taken = take_columns(table, order, hot)
    out_ref[pl.ds(0, PEERS, stride=3), :] = pack_peers(taken[0:8])
    plane = jnp.full((16, LOCAL), lax.axis_index("view"), I32)
    share = []
    for ref in (params_ref, first_ref, second_ref):
        final = jnp.concatenate([ref[48:59, :], jnp.broadcast_to(counts, (5, LOCAL))], axis=0)
        low = jnp.where(plane == 0, ref[0:16, :], ref[16:32, :])
        share.append(jnp.where(plane < 2, low, jnp.where(plane == 2, ref[32:48, :], final)))
    moved = take_columns(jnp.concatenate(share, axis=0), sources, source_hot)
    moved = jnp.concatenate([moved[:, 0:PEERS], moved[:, PEERS:]], axis=0)
    flat = jnp.concatenate([halves(taken[8:9]), halves(order.astype(F32)), moved], axis=0)
    out_ref[pl.ds(1, PEERS, stride=3), :] = flat.T
    entries_ref[...] = jnp.concatenate([lists_ref[0, i : i + 1] for i in range(TILES)], axis=1)
    for tile in range(TILES):
        number = tiles_ref[0, tile]
        corner_ref[tile : tile + 1, :] = jnp.full(
            (1, 256), ((number & (ACROSS - 1)) * 16).astype(F32)
        )
        corner_ref[TILES + tile : TILES + tile + 1, :] = jnp.full(
            (1, 256), ((number >> 4) * 16).astype(F32)
        )
    lane = lax.broadcasted_iota(I32, (1, 128), 1)
    shown = jnp.zeros((1, 128), F32)
    for i in range(16):
        shown = jnp.where(lane == i, cam[i], shown)
    shown_ref[...] = shown


def write_sums(out_ref, summed, numbers, wanted, give, left):
    odd = jnp.full((8, 128), lax.axis_index("gauss") & 1, I32) > 0
    right = lax.broadcasted_iota(I32, (8, 128), 1) >= PEERS
    upper = jnp.full((4, LOCAL), lax.axis_index("gauss") & 1, I32) > 0
    pair = (summed[0:4], summed[4:8]) if give else (summed[4:8], summed[0:4])
    stack = jnp.concatenate([jnp.where(upper, *pair), summed[8:9], numbers], axis=0)
    rows = [[] for _ in range(6)]
    for k in range(CAP):
        lines = stack[:, k * PEERS : (k + 1) * PEERS]
        lines = jnp.concatenate([lines, lines], axis=1)
        for row in range(6):
            rows[row].append(jnp.broadcast_to(lines[row : row + 1], (8, 128)))
    for group in range(PEERS // 8):
        span = slice(group * 8, (group + 1) * 8)
        totals = [None] * 5
        for k in range(CAP):
            same = wanted[span] == rows[5][k]
            for row in range(5):
                term = jnp.where(same, rows[row][k], 0.0)
                totals[row] = term if k == 0 else totals[row] + term
        start = group * 8 * BLOCKS
        turn = pltpu.roll(totals[4], PEERS, axis=1)
        half = jnp.where(odd, turn, totals[4]) if give else jnp.where(odd, totals[4], turn)
        out_ref[pl.ds(start + 1, 8, stride=BLOCKS), :] = jnp.where(right, half, left[span])
        for row in range(4):
            out_ref[pl.ds(start + 2 + row, 8, stride=BLOCKS), :] = totals[row]


def render_kernel(
    recv_ref,
    entries_ref,
    corner_ref,
    target_ref,
    give_ref,
    share_ref,
    summed_ref,
    numbers_ref,
    wanted_ref,
    alpha_ref,
    grad_ref,
):
    lead = recv_ref[pl.ds(0, PEERS, stride=3), :]
    tail = recv_ref[pl.ds(1, PEERS, stride=3), :]
    sources = recv_ref[pl.ds(2, PEERS, stride=3), :]
    flat = tail.T
    share_ref[...] = jnp.concatenate([flat[32 : 32 + SHARE], flat[32 + SHARE :]], axis=1)
    numbers = joined(flat[16:32])
    table = jnp.concatenate(
        [unpack_peers(lead), joined(flat[0:16]), jnp.zeros((ROWS - 9, LOCAL), F32)], axis=0
    )
    entries = entries_ref[...]
    idx = jnp.where(entries < 0, -1, (entries & 15) * PEERS + (entries >> 4))
    hot = low_onehot(idx)
    listed = take_columns(table, idx, hot)
    iota_r = lax.broadcasted_iota(I32, (256, 256), 0)
    iota_c = lax.broadcasted_iota(I32, (256, 256), 1)
    before_mask = jnp.where(iota_r < iota_c, 1.0, 0.0).astype(BF16)
    before_mask = jnp.concatenate([before_mask, before_mask], axis=0)
    after_mask = jnp.where(iota_r > iota_c, 1.0, 0.0).astype(BF16)
    after_mask = jnp.concatenate([after_mask, after_mask], axis=0)
    steps = lax.broadcasted_iota(I32, (16, 256), 0).astype(F32)
    nt = (((1,), (1,)), ((), ()))
    tiles = range(TILES)
    heres, offs_u, offs_w = [], [], []
    for tile in tiles:
        here = listed[:, tile * 256 : (tile + 1) * 256]
        left = corner_ref[tile : tile + 1]
        top = corner_ref[TILES + tile : TILES + tile + 1]
        con_a, con_b, con_c, opacity = here[2:3], here[3:4], here[4:5], here[5:6]
        off_u = (steps + left + 0.5) - here[0:1]
        off_w = (steps + top + 0.5) - here[1:2]
        quad_u = LOG2E * (jnp.log(opacity) - 0.5 * con_a * off_u * off_u)
        cross = -LOG2E * con_b * off_u
        quad_w = (-0.5 * LOG2E) * con_c * off_w * off_w
        for j in range(16):
            exponent = quad_u + quad_w[j : j + 1] + cross * off_w[j : j + 1]
            alpha_ref[tile, j * 16 : (j + 1) * 16, :] = jnp.exp2(exponent)
        heres.append(here)
        offs_u.append(off_u)
        offs_w.append(off_w)
    log_keeps = [jnp.log(1.0 - alpha_ref[t]) for t in tiles]
    logs = [jnp.concatenate(split(x, 2), axis=1) for x in log_keeps]
    befores = [jnp.dot(x, before_mask, preferred_element_type=F32) for x in logs]
    weights = [jnp.exp(befores[t]) * alpha_ref[t] for t in tiles]
    weight_parts = [split(x, 2) for x in weights]
    colour_parts = [split(here[6:9], 3) for here in heres]
    residual_parts = []
    for tile in tiles:
        stacked = jnp.concatenate(
            [p.astype(F32) for p in colour_parts[tile]] + [jnp.zeros((7, 256), F32)], axis=0
        ).astype(BF16)
        summed = lax.dot_general(
            jnp.concatenate([stacked, stacked], axis=1),
            jnp.concatenate(weight_parts[tile], axis=1),
            nt,
            preferred_element_type=F32,
        )
        residual = summed[0:3] + summed[3:6] + summed[6:9] - target_ref[:, tile]
        residual_parts.append([p.astype(F32) for p in split(residual, 3)])
    pairs = ((0, 0), (0, 1), (1, 0), (1, 1), (0, 2), (2, 0))
    blank = jnp.zeros((14, 256), F32)
    pulls = []
    for tile in tiles:
        left_side = jnp.concatenate([residual_parts[tile][a] for a, _ in pairs] + [blank], axis=0)
        right_side = jnp.concatenate(
            [colour_parts[tile][b].astype(F32) for _, b in pairs] + [blank], axis=0
        )
        pulls.append(
            lax.dot_general(
                left_side.astype(BF16),
                right_side.astype(BF16),
                (((0,), (0,)), ((), ())),
                preferred_element_type=F32,
            )
        )
    weighteds = [pulls[t] * weights[t] for t in tiles]
    flows = [jnp.concatenate(split(x, 2), axis=1) for x in weighteds]
    afters = [jnp.dot(x, after_mask, preferred_element_type=F32) for x in flows]
    for t in tiles:
        grad_ref[t] = weighteds[t] - afters[t] * (alpha_ref[t] * jnp.exp(-log_keeps[t]))
    results = []
    for tile in tiles:
        here, off_u, off_w = heres[tile], offs_u[tile], offs_w[tile]
        con_a, con_b, con_c = here[2:3], here[3:4], here[4:5]
        stacked_res = jnp.concatenate(
            residual_parts[tile] + [jnp.zeros((7, 256), F32)], axis=0
        ).astype(BF16)
        colour_sum = jnp.dot(
            jnp.concatenate([stacked_res, stacked_res], axis=1),
            jnp.concatenate(weight_parts[tile], axis=0),
            preferred_element_type=F32,
        )
        colour_grad = colour_sum[0:3] + colour_sum[3:6] + colour_sum[6:9]
        zeroth = first = second = grad_ref[tile, 240:256, :]
        for j in range(14, -1, -1):
            zeroth = zeroth + grad_ref[tile, j * 16 : (j + 1) * 16, :]
            first = first + zeroth
            second = second + first
        start = off_w[0:1]
        by_step = first - zeroth
        by_square = 2.0 * second - 3.0 * by_step - 2.0 * zeroth
        first = start * zeroth + by_step
        second = start * (first + by_step) + by_square

        def over(values):
            return jnp.sum(values, axis=0, keepdims=True)

        along = zeroth * off_u
        m_00, m_10, m_20 = over(zeroth), over(along), over(along * off_u)
        m_01, m_11, m_02 = over(first), over(first * off_u), over(second)
        results.append(
            jnp.concatenate(
                [
                    con_a * m_10 + con_b * m_01,
                    con_c * m_01 + con_b * m_10,
                    -0.5 * m_20,
                    -m_11,
                    -0.5 * m_02,
                    m_00,
                    colour_grad,
                    jnp.zeros((ROWS - 9, 256), F32),
                ],
                axis=0,
            )
        )
    grads = jnp.concatenate(results, axis=1)
    summed = add_columns(grads, idx, hot, 2)
    turned = sources.T
    wanted = jnp.concatenate([turned[0:PEERS], turned[PEERS:]], axis=1)
    summed_ref[...] = summed
    numbers_ref[...] = numbers
    wanted_ref[...] = wanted
    give_ref[pl.ds(0, PEERS, stride=BLOCKS), :] = jnp.zeros((PEERS, 128), F32)
    write_sums(give_ref, summed, numbers, wanted, True, jnp.zeros((PEERS, 128), F32))


def keep_kernel(summed_ref, numbers_ref, wanted_ref, out_ref):
    summed = summed_ref[...]
    out_ref[pl.ds(0, PEERS, stride=BLOCKS), :] = pack_peers(summed[0:8])
    flat = jnp.concatenate([halves(summed[8:9]), jnp.zeros((112, PEERS), F32)], axis=0)
    write_sums(out_ref, summed, numbers_ref[...], wanted_ref[...], False, flat.T)


def owner_kernel(recv_ref, order_ref, shown_ref, share_ref, out_ref):
    lead = unpack_peers(recv_ref[pl.ds(0, PEERS, stride=BLOCKS), :])
    last = joined(recv_ref[pl.ds(1, PEERS, stride=BLOCKS), :].T[0:16])
    values = jnp.concatenate([lead, last, jnp.zeros((ROWS - 9, LOCAL), F32)], axis=0)
    order = order_ref[...]
    owned = add_columns(values, order, low_onehot(order), 2)
    out_ref[0:AT_MOVED, :] = owned[0:9].reshape(9, 8, 128).reshape(AT_MOVED, 128)
    odd = (lax.broadcasted_iota(I32, (PEERS, 128), 0) & 1) > 0

    def sums(block):
        values = recv_ref[pl.ds(block, PEERS, stride=BLOCKS), :]
        return [
            jnp.sum(jnp.where(odd, 0.0, values), axis=0, keepdims=True),
            jnp.sum(jnp.where(odd, values, 0.0), axis=0, keepdims=True),
        ]

    for row in range(4):
        even_sum, odd_sum = sums(2 + row)
        out_ref[AT_MOVED + row : AT_MOVED + row + 1, :] = even_sum
        out_ref[AT_MOVED + 4 + row : AT_MOVED + 5 + row, :] = odd_sum
    even_sum, odd_sum = sums(1)
    out_ref[AT_MOVED + 8 : AT_MOVED + 9, :] = jnp.concatenate(
        [even_sum[:, PEERS:], odd_sum[:, PEERS:]], axis=1
    )
    out_ref[AT_CAMERA : AT_CAMERA + 1, :] = shown_ref[...]
    out_ref[AT_CAMERA + 1 : AT_SHARE, :] = jnp.zeros((AT_SHARE - AT_CAMERA - 1, 128), F32)
    out_ref[AT_SHARE:SENT, :] = share_ref[...]


def log_one_plus(t):
    s = t / (2.0 + t)
    square = s * s
    total = jnp.full_like(s, 1.0 / 17.0)
    for odd in (15, 13, 11, 9, 7, 5, 3, 1):
        total = total * square + 1.0 / odd
    return 2.0 * s * total


def one_minus_exp(x):
    small = jnp.ones_like(x)
    for n in range(10, 1, -1):
        small = 1.0 + small * x * (1.0 / n)
    return jnp.where(x > -0.5, -x * small, 1.0 - jnp.exp(x))


def rates_column():
    row = lax.broadcasted_iota(I32, (59, 1), 0)
    rate = jnp.where(row < 14, 0.0025, 0.000125)
    rate = jnp.where(row < 11, 0.05, rate)
    rate = jnp.where(row < 10, 0.001, rate)
    rate = jnp.where(row < 6, 0.005, rate)
    return jnp.where(row < 3, 0.00016, rate)


def tree_sum(values):
    return (values[0] + values[1]) + (values[2] + values[3])


def adam(params, first_old, second_old, gradient):
    first = 0.9 * first_old + 0.1 * gradient
    second = 0.999 * second_old + 0.001 * gradient * gradient
    stepped = params - rates_column() * (first / BIAS_ONE) / (jnp.sqrt(second / BIAS_TWO) + 1e-15)
    return stepped, first, second


def spread_logit(logit, counts):
    soft = jnp.maximum(logit, 0.0) + log_one_plus(jnp.exp(-jnp.abs(logit)))
    share = -soft / (counts + 1.0)
    return jnp.log(one_minus_exp(share)) - share


def sigmoid_rest(logit):
    return 1.0 - 1.0 / (1.0 + jnp.exp(-logit))


def incoming_columns(parts):
    def stacked(row):
        return jnp.concatenate([ref[row : row + 1, :] for ref in parts], axis=0)

    def folded(x):
        return (x[0:1] + x[1:2]) + (x[2:3] + x[3:4])

    def wide(x):
        return jnp.broadcast_to(x, (VIEWS, 128))

    plane = jnp.full((SHARE, 128), lax.axis_index("view"), I32)
    shares = [ref[AT_SHARE:SENT, :] for ref in parts]
    for bit in (1, 2):
        flip = (plane & bit) > 0
        shares = [jnp.where(flip, shares[i ^ bit], shares[i]) for i in range(VIEWS)]
    params, first_old, second_old = [
        jnp.concatenate([part[i : i + 16] for part in shares], axis=0) for i in (0, 16, 32)
    ]
    rows = [params[i : i + 1] for i in range(59)]
    shown = stacked(AT_CAMERA)
    cam = [wide(shown[:, i : i + 1]) for i in range(16)]
    sigma, pull_sigma = jax.vjp(covariance, rows[3:6], rows[6:10])
    _, pull = jax.vjp(
        lambda p, s, c: view_rows(p, s, c, cam),
        [wide(x) for x in rows[0:3]],
        [wide(x) for x in sigma],
        [wide(x) for x in rows[11:59]],
    )
    got = [stacked(AT_MOVED + i) for i in range(9)]
    d_pos, d_sigma, d_coeff = pull([got[i] for i in (0, 1, 2, 3, 4, 6, 7, 8)])
    d_scale, d_quat = pull_sigma([folded(x) for x in d_sigma])
    d_logit = folded(got[5]) * sigmoid_rest(rows[10])
    gradient = jnp.concatenate(
        [folded(x) for x in d_pos]
        + list(d_scale)
        + list(d_quat)
        + [d_logit]
        + [folded(x) for x in d_coeff],
        axis=0,
    )
    stepped, _, _ = adam(params[0:59], first_old[0:59], second_old[0:59], gradient)
    logit = spread_logit(stepped[10:11], params[59:60])
    row = lax.broadcasted_iota(I32, (59, 128), 0)
    return jnp.concatenate(
        [jnp.where(row == 10, logit, stepped), jnp.ones((5, 128), F32)], axis=0
    )


def pull_view(ref, position, sigma, coeffs):
    got = [ref[8 * i : 8 * i + 8, :] for i in range(9)]
    shown = jnp.broadcast_to(ref[AT_CAMERA : AT_CAMERA + 1, :], (8, 128))
    cam = [jnp.broadcast_to(shown[:, i : i + 1], (8, 128)) for i in range(16)]
    _, pull = jax.vjp(lambda p, s, c: view_rows(p, s, c, cam), position, sigma, coeffs)
    d_pos, d_sigma, d_coeff = pull([got[i] for i in (0, 1, 2, 3, 4, 6, 7, 8)])
    return list(d_pos) + list(d_sigma) + list(d_coeff)


def early_kernel(params_ref, own_ref, last_ref, dense_ref, own_part_ref, last_part_ref):
    dense = params_ref[...].reshape(59, 8, 128)
    dense_ref[...] = dense.reshape(59 * 8, 128)
    rows = [dense[i] for i in range(59)]
    sigma = covariance(rows[3:6], rows[6:10])
    for ref, part_ref in ((own_ref, own_part_ref), (last_ref, last_part_ref)):
        for i, piece in enumerate(pull_view(ref, rows[0:3], sigma, rows[11:59])):
            part_ref[8 * i : 8 * i + 8, :] = piece


def step_kernel(
    dense_ref,
    own_part_ref,
    last_part_ref,
    params_ref,
    first_ref,
    second_ref,
    own_ref,
    near_ref,
    far_ref,
    last_ref,
    counts_ref,
    targets_ref,
    new_params_ref,
    new_first_ref,
    new_second_ref,
    gradient_ref,
):
    parts = (own_ref, near_ref, far_ref, last_ref)
    targets = targets_ref[...]
    placed = add_columns(incoming_columns(parts), targets, low_onehot(targets))
    rows = [dense_ref[8 * i : 8 * i + 8, :] for i in range(59)]
    sigma, pull_sigma = jax.vjp(covariance, rows[3:6], rows[6:10])
    near, far = [pull_view(ref, rows[0:3], sigma, rows[11:59]) for ref in (near_ref, far_ref)]
    total = []
    for i in range(57):
        own, last = [ref[8 * i : 8 * i + 8, :] for ref in (own_part_ref, last_part_ref)]
        total.append((own + near[i]) + (far[i] + last))
    d_pos, d_sigma, d_coeff = total[0:3], total[3:9], total[9:57]
    opacity_parts = [ref[40:48, :] for ref in parts]
    d_scale, d_quat = pull_sigma(d_sigma)
    d_logit = tree_sum(opacity_parts) * sigmoid_rest(rows[10])
    gradient = jnp.stack(d_pos + list(d_scale) + list(d_quat) + [d_logit] + d_coeff).reshape(
        59, LOCAL
    )
    gradient_ref[...] = gradient
    stepped, first, second = adam(params_ref[...], first_ref[...], second_ref[...], gradient)
    counts = counts_ref[...]
    landed = placed[59:60] > 0.5
    cleared = (counts + placed[59:60]) > 0.5
    row = lax.broadcasted_iota(I32, (59, LOCAL), 0)
    spread = jnp.where(
        (row == 10) & (counts > 0.5), spread_logit(stepped[10:11], counts), stepped
    )
    new_params_ref[...] = jnp.where(landed, placed[0:59], spread)
    new_first_ref[...] = jnp.where(cleared, 0.0, first)
    new_second_ref[...] = jnp.where(cleared, 0.0, second)


def call(kernel, shapes, ins, scratch=()):
    spec = {
        "v": pl.BlockSpec(memory_space=pltpu.VMEM),
        "s": pl.BlockSpec(memory_space=pltpu.SMEM),
        "h": pl.BlockSpec(memory_space=pltpu.HBM),
    }
    out_shape = [jax.ShapeDtypeStruct(shape, dtype) for shape, dtype in shapes]
    return pl.pallas_call(
        kernel,
        out_shape=out_shape,
        in_specs=[spec[kind] for kind in ins],
        out_specs=[spec["v"]] * len(out_shape),
        scratch_shapes=list(scratch),
        compiler_params=pltpu.CompilerParams(vmem_limit_bytes=VMEM_LIMIT),
    )


def in_hbm(array):
    return pltpu.with_memory_space_constraint(array, pltpu.HBM)


def exchange(block):
    parts = block.reshape(PEERS, 1, -1)
    got = lax.all_to_all(parts, "gauss", split_axis=0, concat_axis=0, tiled=True)
    return got.reshape(block.shape)


def shards(
    params,
    first_moment,
    second_moment,
    cameras,
    target,
    tile_index,
    tile_lists,
    send_slots,
    reloc_send,
    reloc_recv,
):
    columns = ((1, LOCAL), I32)
    whole = ((59, LOCAL), F32)
    outgoing, order, entries, corners, wanted, counts, landing, shown = call(
        send_kernel,
        [
            ((3 * PEERS, 128), F32),
            columns,
            columns,
            ((2 * TILES, 256), F32),
            ((3, TILES, 256), F32),
            ((1, LOCAL), F32),
            ((1, 128), I32),
            ((1, 128), F32),
        ],
        "hhhhhhhhhh",
        [
            pltpu.VMEM((59, LOCAL), F32),
            pltpu.VMEM((59, LOCAL), F32),
            pltpu.VMEM((59, LOCAL), F32),
            pltpu.VMEM((8, 128), I32),
            pltpu.VMEM((1, 128), I32),
            pltpu.VMEM((1, 128), I32),
            pltpu.SMEM((1, 16), F32),
            pltpu.VMEM((1, TILES, 256), I32),
            pltpu.SMEM((1, TILES), I32),
            pltpu.SemaphoreType.DMA((10,)),
        ],
    )(
        in_hbm(params),
        in_hbm(first_moment),
        in_hbm(second_moment),
        in_hbm(send_slots.reshape(8, 128)),
        in_hbm(reloc_send),
        in_hbm(reloc_recv),
        in_hbm(cameras),
        in_hbm(tile_lists),
        in_hbm(tile_index),
        in_hbm(jnp.transpose(target[0], (1, 0, 2))),
    )
    received = exchange(outgoing)
    back = ((BLOCKS * PEERS, 128), F32)
    give, share, summed, numbers, asked = call(
        render_kernel,
        [back, ((SHARE, 128), F32), ((ROWS, LOCAL), F32), ((1, LOCAL), F32), ((PEERS, 128), F32)],
        "vvvv",
        [pltpu.VMEM((TILES, 256, 256), F32), pltpu.VMEM((TILES, 256, 256), F32)],
    )(received, entries, corners, wanted)
    sibling = lax.ppermute(give, "gauss", [(i, i ^ 1) for i in range(PEERS)])
    (kept,) = call(keep_kernel, [back], "vvv")(summed, numbers, asked)
    returned = exchange(kept + sibling)
    (own,) = call(owner_kernel, [((SENT, 128), F32)], "vvvv")(returned, order, shown, share)
    others = [
        lax.ppermute(own, "view", [(i, i ^ flip) for i in range(VIEWS)]) for flip in (1, 2, 3)
    ]
    tiles = ((57 * 8, 128), F32)
    dense, own_part, last_part = call(early_kernel, [((59 * 8, 128), F32), tiles, tiles], "vvv")(
        params, own, others[2]
    )
    return call(step_kernel, [whole, whole, whole, whole], "vvvvvvvvvvvv")(
        dense, own_part, last_part, params, first_moment, second_moment, own, *others, counts, landing
    )


def solution(mesh):
    in_specs = (
        P(None, "gauss"),
        P(None, "gauss"),
        P(None, "gauss"),
        P("view", None),
        P("view", "gauss", None, None),
        P("view", "gauss"),
        P("view", "gauss", None),
        P("view", "gauss", None),
        P("gauss", None),
        P("gauss", None),
    )
    out_specs = (P(None, "gauss"), P(None, "gauss"), P(None, "gauss"), P(None, "gauss"))
    return jax.shard_map(shards, mesh=mesh, in_specs=in_specs, out_specs=out_specs, check_vma=False)
```

```python
import math

import jax
import jax.numpy as jnp
from jax import lax
from jax.experimental import pallas as pl
from jax.experimental.pallas import tpu as pltpu
from jax.sharding import PartitionSpec as P

F32 = jnp.float32
BF16 = jnp.bfloat16
I32 = jnp.int32
PEERS = 64
LOCAL = 1024
CAP = 16
VIEWS = 4
TILES = 4
ACROSS = 16
ROWS = 16
LOG2E = 1.4426950408889634
SHARE = 48
BLOCKS = 6
AT_MOVED = 72
AT_CAMERA = 81
AT_SHARE = 88
SENT = 136

SH_ZERO = 0.28209479177387814
SH_ONE = 0.4886025119029199
SH_TWO = (
    1.0925484305920792,
    -1.0925484305920792,
    0.31539156525252005,
    -1.0925484305920792,
    0.5462742152960396,
)
SH_THREE = (
    -0.5900435899266435,
    2.890611442640554,
    -0.4570457994644658,
    0.3731763325901154,
    -0.4570457994644658,
    1.445305721320277,
    -0.5900435899266435,
)
BIAS_ONE = 1.0 - math.exp(1000.0 * math.log(0.9))
BIAS_TWO = 1.0 - math.exp(1000.0 * math.log(0.999))
VMEM_LIMIT = 16 * 1024 * 1024


def split(x, parts):
    out = []
    for index in range(parts):
        piece = x.astype(BF16)
        out.append(piece)
        if index + 1 < parts:
            x = x - piece.astype(F32)
    return out


def low_onehot(idx):
    lane = lax.broadcasted_iota(I32, (128, idx.shape[1]), 0)
    return jnp.where(lane == (idx & 127), 1.0, 0.0).astype(BF16)


def take_columns(table, idx, hot):
    rows = table.shape[0]
    high = idx >> 7
    parts = split(table, 3)
    lhs = jnp.concatenate(
        [
            jnp.concatenate([p[:, c * 128 : (c + 1) * 128] for p in parts], axis=1)
            for c in range(8)
        ],
        axis=0,
    )
    rhs = jnp.concatenate([hot, hot, hot], axis=0)
    wide = jnp.dot(lhs, rhs, preferred_element_type=F32)
    total = None
    for c in range(8):
        term = jnp.where(high == c, wide[c * rows : (c + 1) * rows], 0.0)
        total = term if total is None else total + term
    return total


def add_columns(values, idx, hot, parts=3):
    rows = values.shape[0]
    high = idx >> 7
    pieces = []
    for piece in split(values, parts):
        piece = piece.astype(F32)
        pieces += [jnp.where(high == c, piece, 0.0) for c in range(8)]
    lhs = jnp.concatenate(pieces, axis=0).astype(BF16)
    wide = lax.dot_general(lhs, hot, (((1,), (1,)), ((), ())), preferred_element_type=F32)
    size = 8 * rows
    wide = sum(wide[i * size : (i + 1) * size] for i in range(1, parts)) + wide[0:size]
    return jnp.concatenate([wide[c * rows : (c + 1) * rows] for c in range(8)], axis=1)


def pack_peers(table):
    pieces = [table[:, k * PEERS : (k + 1) * PEERS] for k in range(CAP)]
    return jnp.concatenate(pieces, axis=0).T


def unpack_peers(block):
    flat = block.T
    return jnp.concatenate([flat[k * 8 : (k + 1) * 8] for k in range(CAP)], axis=1)


def halves(row):
    block = row.reshape(8, 128)
    return jnp.concatenate([block[:, 0:PEERS], block[:, PEERS:]], axis=0)


def joined(block):
    return jnp.concatenate([block[0:8], block[8:16]], axis=1).reshape(1, LOCAL)


def slots_by_rank(slots):
    source = lax.broadcasted_iota(I32, (128, LOCAL), 0)
    col = lax.broadcasted_iota(I32, (128, LOCAL), 1)
    pick = jnp.where(source == (col & 7) * 16 + (col >> 6), 1.0, 0.0).astype(BF16)
    upper = jnp.dot((slots >> 5).astype(F32).astype(BF16), pick, preferred_element_type=F32)
    lower = jnp.dot((slots & 31).astype(F32).astype(BF16), pick, preferred_element_type=F32)
    wide = upper * 32.0 + lower
    row = lax.broadcasted_iota(I32, (8, LOCAL), 0)
    column = lax.broadcasted_iota(I32, (8, LOCAL), 1)
    kept = jnp.where(row == ((column >> 3) & 7), wide, 0.0)
    return jnp.sum(kept, axis=0, keepdims=True).astype(I32)


def pairs_by_rank(pairs):
    source = lax.broadcasted_iota(I32, (128, 128), 0)
    col = lax.broadcasted_iota(I32, (128, 128), 1)
    pick = jnp.where(source == (col & (PEERS - 1)) * 2 + (col >> 6), 1.0, 0.0).astype(BF16)
    wide = jnp.broadcast_to(pairs + 1, (8, 128))
    upper = jnp.dot((wide >> 5).astype(F32).astype(BF16), pick, preferred_element_type=F32)
    lower = jnp.dot((wide & 31).astype(F32).astype(BF16), pick, preferred_element_type=F32)
    return (upper * 32.0 + lower)[0:1].astype(I32) - 1


def covariance(log_scale, quat):
    norm = jnp.sqrt(quat[0] * quat[0] + quat[1] * quat[1] + quat[2] * quat[2] + quat[3] * quat[3])
    quat_w, quat_x, quat_y, quat_z = [q / norm for q in quat]
    orient = [
        [
            1.0 - 2.0 * (quat_y * quat_y + quat_z * quat_z),
            2.0 * (quat_x * quat_y - quat_w * quat_z),
            2.0 * (quat_x * quat_z + quat_w * quat_y),
        ],
        [
            2.0 * (quat_x * quat_y + quat_w * quat_z),
            1.0 - 2.0 * (quat_x * quat_x + quat_z * quat_z),
            2.0 * (quat_y * quat_z - quat_w * quat_x),
        ],
        [
            2.0 * (quat_x * quat_z - quat_w * quat_y),
            2.0 * (quat_y * quat_z + quat_w * quat_x),
            1.0 - 2.0 * (quat_x * quat_x + quat_y * quat_y),
        ],
    ]
    scales = [jnp.exp(s) for s in log_scale]
    factor = [[orient[i][j] * scales[j] for j in range(3)] for i in range(3)]

    def entry(i, j):
        return (
            factor[i][0] * factor[j][0] + factor[i][1] * factor[j][1] + factor[i][2] * factor[j][2]
        )

    return [entry(0, 0), entry(0, 1), entry(0, 2), entry(1, 1), entry(1, 2), entry(2, 2)]


def harmonics(dir_x, dir_y, dir_z):
    sq_x, sq_y, sq_z = (dir_x * dir_x, dir_y * dir_y, dir_z * dir_z)
    return [
        -SH_ONE * dir_y,
        SH_ONE * dir_z,
        -SH_ONE * dir_x,
        SH_TWO[0] * dir_x * dir_y,
        SH_TWO[1] * dir_y * dir_z,
        SH_TWO[2] * (2.0 * sq_z - sq_x - sq_y),
        SH_TWO[3] * dir_x * dir_z,
        SH_TWO[4] * (sq_x - sq_y),
        SH_THREE[0] * dir_y * (3.0 * sq_x - sq_y),
        SH_THREE[1] * dir_x * dir_y * dir_z,
        SH_THREE[2] * dir_y * (4.0 * sq_z - sq_x - sq_y),
        SH_THREE[3] * dir_z * (2.0 * sq_z - 3.0 * sq_x - 3.0 * sq_y),
        SH_THREE[4] * dir_x * (4.0 * sq_z - sq_x - sq_y),
        SH_THREE[5] * dir_z * (sq_x - sq_y),
        SH_THREE[6] * dir_x * (sq_x - 3.0 * sq_y),
    ]


def view_rows(position, sigma, coeffs, cam):
    rot = [cam[0:3], cam[3:6], cam[6:9]]
    offset = cam[9:12]
    focal_x, focal_y, centre_x, centre_y = cam[12:16]
    cam_x, cam_y, cam_z = [
        rot[i][0] * position[0] + rot[i][1] * position[1] + rot[i][2] * position[2] + offset[i]
        for i in range(3)
    ]
    inverse_z = 1.0 / cam_z
    mean_u = focal_x * cam_x * inverse_z + centre_x
    mean_w = focal_y * cam_y * inverse_z + centre_y
    jac_a0 = focal_x * inverse_z
    jac_a2 = -focal_x * cam_x * inverse_z * inverse_z
    jac_b1 = focal_y * inverse_z
    jac_b2 = -focal_y * cam_y * inverse_z * inverse_z
    row_a = [jac_a0 * rot[0][i] + jac_a2 * rot[2][i] for i in range(3)]
    row_b = [jac_b1 * rot[1][i] + jac_b2 * rot[2][i] for i in range(3)]
    full = [
        [sigma[0], sigma[1], sigma[2]],
        [sigma[1], sigma[3], sigma[4]],
        [sigma[2], sigma[4], sigma[5]],
    ]

    def through(row):
        return [full[i][0] * row[0] + full[i][1] * row[1] + full[i][2] * row[2] for i in range(3)]

    def dot3(left, right):
        return left[0] * right[0] + left[1] * right[1] + left[2] * right[2]

    sigma_a = through(row_a)
    sigma_b = through(row_b)
    cov_aa = dot3(row_a, sigma_a) + 0.3
    cov_ab = dot3(row_a, sigma_b)
    cov_bb = dot3(row_b, sigma_b) + 0.3
    determinant = cov_aa * cov_bb - cov_ab * cov_ab
    inverse_det = 1.0 / determinant
    ray = [
        position[i] + (rot[0][i] * offset[0] + rot[1][i] * offset[1] + rot[2][i] * offset[2])
        for i in range(3)
    ]
    inverse_norm = 1.0 / jnp.sqrt(dot3(ray, ray))
    basis = harmonics(*[r * inverse_norm for r in ray])
    colours = []
    for channel in range(3):
        total = SH_ZERO * coeffs[channel]
        for index in range(15):
            total = total + basis[index] * coeffs[3 + 3 * index + channel]
        colours.append(jnp.maximum(total + 0.5, 0.0))
    return [
        mean_u,
        mean_w,
        cov_bb * inverse_det,
        -cov_ab * inverse_det,
        cov_aa * inverse_det,
    ] + colours


def send_kernel(
    params_hbm,
    first_hbm,
    second_hbm,
    slots_hbm,
    sources_hbm,
    targets_hbm,
    camera_hbm,
    lists_hbm,
    tiles_hbm,
    wanted_hbm,
    out_ref,
    order_ref,
    entries_ref,
    corner_ref,
    wanted_ref,
    counts_ref,
    landing_ref,
    shown_ref,
    params_ref,
    first_ref,
    second_ref,
    slots_ref,
    sources_ref,
    targets_ref,
    camera_ref,
    lists_ref,
    tiles_ref,
    sems,
):
    pairs = (
        (slots_hbm, slots_ref),
        (params_hbm, params_ref),
        (camera_hbm, camera_ref),
        (sources_hbm, sources_ref),
        (targets_hbm, targets_ref),
        (lists_hbm, lists_ref),
        (tiles_hbm, tiles_ref),
        (wanted_hbm, wanted_ref),
        (first_hbm, first_ref),
        (second_hbm, second_ref),
    )
    copies = [pltpu.make_async_copy(a, b, sems.at[i]) for i, (a, b) in enumerate(pairs)]
    for copy in copies:
        copy.start()
    for at in (0, 3, 4):
        copies[at].wait()
    order = slots_by_rank(slots_ref[...])
    order_ref[...] = order
    hot = low_onehot(order)
    sources = pairs_by_rank(sources_ref[...])
    source_hot = low_onehot(sources)
    counts = add_columns(jnp.ones((8, 128), F32), sources, source_hot, 1)[0:1]
    counts_ref[...] = counts
    out_ref[pl.ds(2, PEERS, stride=3), :] = jnp.broadcast_to(sources.astype(F32), (PEERS, 128))
    landing_ref[...] = pairs_by_rank(targets_ref[...])
    for at in (1, 2, 5, 6, 7, 8, 9):
        copies[at].wait()
    dense = params_ref[...].reshape(59, 8, 128)
    rows = [dense[i] for i in range(59)]
    cam = [camera_ref[0, i] for i in range(16)]
    sigma = covariance(rows[3:6], rows[6:10])
    seen = view_rows(rows[0:3], sigma, rows[11:59], cam)
    opacity = 1.0 / (1.0 + jnp.exp(-rows[10]))
    listed = seen[0:5] + [opacity] + seen[5:8]
    blank = jnp.zeros((8, 128), F32)
    table = jnp.stack(listed + [blank] * (ROWS - 9)).reshape(ROWS, LOCAL)
    taken = take_columns(table, order, hot)
    out_ref[pl.ds(0, PEERS, stride=3), :] = pack_peers(taken[0:8])
    plane = jnp.full((16, LOCAL), lax.axis_index("view"), I32)
    share = []
    for ref in (params_ref, first_ref, second_ref):
        final = jnp.concatenate([ref[48:59, :], jnp.broadcast_to(counts, (5, LOCAL))], axis=0)
        low = jnp.where(plane == 0, ref[0:16, :], ref[16:32, :])
        share.append(jnp.where(plane < 2, low, jnp.where(plane == 2, ref[32:48, :], final)))
    moved = take_columns(jnp.concatenate(share, axis=0), sources, source_hot)
    moved = jnp.concatenate([moved[:, 0:PEERS], moved[:, PEERS:]], axis=0)
    flat = jnp.concatenate([halves(taken[8:9]), halves(order.astype(F32)), moved], axis=0)
    out_ref[pl.ds(1, PEERS, stride=3), :] = flat.T
    entries_ref[...] = jnp.concatenate([lists_ref[0, i : i + 1] for i in range(TILES)], axis=1)
    for tile in range(TILES):
        number = tiles_ref[0, tile]
        corner_ref[tile : tile + 1, :] = jnp.full(
            (1, 256), ((number & (ACROSS - 1)) * 16).astype(F32)
        )
        corner_ref[TILES + tile : TILES + tile + 1, :] = jnp.full(
            (1, 256), ((number >> 4) * 16).astype(F32)
        )
    lane = lax.broadcasted_iota(I32, (1, 128), 1)
    shown = jnp.zeros((1, 128), F32)
    for i in range(16):
        shown = jnp.where(lane == i, cam[i], shown)
    shown_ref[...] = shown


def odd_core(shape):
    return jnp.full(shape, lax.axis_index("gauss") & 1, I32) > 0


def write_sums(out_ref, four, ninth, numbers, wanted, give, left):
    odd = odd_core((8, 128))
    right = lax.broadcasted_iota(I32, (8, 128), 1) >= PEERS
    stack = jnp.concatenate([four, ninth, numbers], axis=0)
    rows = [[] for _ in range(6)]
    for k in range(CAP):
        lines = stack[:, k * PEERS : (k + 1) * PEERS]
        lines = jnp.concatenate([lines, lines], axis=1)
        for row in range(6):
            rows[row].append(jnp.broadcast_to(lines[row : row + 1], (8, 128)))
    for group in range(PEERS // 8):
        span = slice(group * 8, (group + 1) * 8)
        totals = [None] * 5
        for k in range(CAP):
            same = wanted[span] == rows[5][k]
            for row in range(5):
                term = jnp.where(same, rows[row][k], 0.0)
                totals[row] = term if k == 0 else totals[row] + term
        start = group * 8 * BLOCKS
        turn = pltpu.roll(totals[4], PEERS, axis=1)
        half = jnp.where(odd, turn, totals[4]) if give else jnp.where(odd, totals[4], turn)
        out_ref[pl.ds(start + 1, 8, stride=BLOCKS), :] = jnp.where(right, half, left[span])
        for row in range(4):
            out_ref[pl.ds(start + 2 + row, 8, stride=BLOCKS), :] = totals[row]


def render_kernel(
    recv_ref,
    entries_ref,
    corner_ref,
    target_ref,
    give_ref,
    share_ref,
    given_ref,
    rest_ref,
    index_ref,
    numbers_ref,
    wanted_ref,
    alpha_ref,
    grad_ref,
):
    lead = recv_ref[pl.ds(0, PEERS, stride=3), :]
    tail = recv_ref[pl.ds(1, PEERS, stride=3), :]
    sources = recv_ref[pl.ds(2, PEERS, stride=3), :]
    flat = tail.T
    share_ref[...] = jnp.concatenate([flat[32 : 32 + SHARE], flat[32 + SHARE :]], axis=1)
    numbers = joined(flat[16:32])
    table = jnp.concatenate(
        [unpack_peers(lead), joined(flat[0:16]), jnp.zeros((ROWS - 9, LOCAL), F32)], axis=0
    )
    entries = entries_ref[...]
    idx = jnp.where(entries < 0, -1, (entries & 15) * PEERS + (entries >> 4))
    hot = low_onehot(idx)
    listed = take_columns(table, idx, hot)
    iota_r = lax.broadcasted_iota(I32, (256, 256), 0)
    iota_c = lax.broadcasted_iota(I32, (256, 256), 1)
    before_mask = jnp.where(iota_r < iota_c, 1.0, 0.0).astype(BF16)
    before_mask = jnp.concatenate([before_mask, before_mask], axis=0)
    after_mask = jnp.where(iota_r > iota_c, 1.0, 0.0).astype(BF16)
    after_mask = jnp.concatenate([after_mask, after_mask], axis=0)
    steps = lax.broadcasted_iota(I32, (16, 256), 0).astype(F32)
    nt = (((1,), (1,)), ((), ()))
    tiles = range(TILES)
    heres, offs_u, offs_w = [], [], []
    for tile in tiles:
        here = listed[:, tile * 256 : (tile + 1) * 256]
        left = corner_ref[tile : tile + 1]
        top = corner_ref[TILES + tile : TILES + tile + 1]
        con_a, con_b, con_c, opacity = here[2:3], here[3:4], here[4:5], here[5:6]
        off_u = (steps + left + 0.5) - here[0:1]
        off_w = (steps + top + 0.5) - here[1:2]
        quad_u = LOG2E * (jnp.log(opacity) - 0.5 * con_a * off_u * off_u)
        cross = -LOG2E * con_b * off_u
        quad_w = (-0.5 * LOG2E) * con_c * off_w * off_w
        for j in range(16):
            exponent = quad_u + quad_w[j : j + 1] + cross * off_w[j : j + 1]
            alpha_ref[tile, j * 16 : (j + 1) * 16, :] = jnp.exp2(exponent)
        heres.append(here)
        offs_u.append(off_u)
        offs_w.append(off_w)
    log_keeps = [jnp.log(1.0 - alpha_ref[t]) for t in tiles]
    logs = [jnp.concatenate(split(x, 2), axis=1) for x in log_keeps]
    befores = [jnp.dot(x, before_mask, preferred_element_type=F32) for x in logs]
    weights = [jnp.exp(befores[t]) * alpha_ref[t] for t in tiles]
    weight_parts = [split(x, 2) for x in weights]
    colour_parts = [split(here[6:9], 3) for here in heres]
    residual_parts = []
    for tile in tiles:
        stacked = jnp.concatenate(
            [p.astype(F32) for p in colour_parts[tile]] + [jnp.zeros((7, 256), F32)], axis=0
        ).astype(BF16)
        summed = lax.dot_general(
            jnp.concatenate([stacked, stacked], axis=1),
            jnp.concatenate(weight_parts[tile], axis=1),
            nt,
            preferred_element_type=F32,
        )
        residual = summed[0:3] + summed[3:6] + summed[6:9] - target_ref[:, tile]
        residual_parts.append([p.astype(F32) for p in split(residual, 3)])
    pairs = ((0, 0), (0, 1), (1, 0), (1, 1), (0, 2), (2, 0))
    blank = jnp.zeros((14, 256), F32)
    pulls = []
    for tile in tiles:
        left_side = jnp.concatenate([residual_parts[tile][a] for a, _ in pairs] + [blank], axis=0)
        right_side = jnp.concatenate(
            [colour_parts[tile][b].astype(F32) for _, b in pairs] + [blank], axis=0
        )
        pulls.append(
            lax.dot_general(
                left_side.astype(BF16),
                right_side.astype(BF16),
                (((0,), (0,)), ((), ())),
                preferred_element_type=F32,
            )
        )
    weighteds = [pulls[t] * weights[t] for t in tiles]
    flows = [jnp.concatenate(split(x, 2), axis=1) for x in weighteds]
    afters = [jnp.dot(x, after_mask, preferred_element_type=F32) for x in flows]
    for t in tiles:
        grad_ref[t] = weighteds[t] - afters[t] * (alpha_ref[t] * jnp.exp(-log_keeps[t]))
    results = []
    for tile in tiles:
        here, off_u, off_w = heres[tile], offs_u[tile], offs_w[tile]
        con_a, con_b, con_c = here[2:3], here[3:4], here[4:5]
        stacked_res = jnp.concatenate(
            residual_parts[tile] + [jnp.zeros((7, 256), F32)], axis=0
        ).astype(BF16)
        colour_sum = jnp.dot(
            jnp.concatenate([stacked_res, stacked_res], axis=1),
            jnp.concatenate(weight_parts[tile], axis=0),
            preferred_element_type=F32,
        )
        colour_grad = colour_sum[0:3] + colour_sum[3:6] + colour_sum[6:9]
        zeroth = first = second = grad_ref[tile, 240:256, :]
        for j in range(14, -1, -1):
            zeroth = zeroth + grad_ref[tile, j * 16 : (j + 1) * 16, :]
            first = first + zeroth
            second = second + first
        start = off_w[0:1]
        by_step = first - zeroth
        by_square = 2.0 * second - 3.0 * by_step - 2.0 * zeroth
        first = start * zeroth + by_step
        second = start * (first + by_step) + by_square

        def over(values):
            return jnp.sum(values, axis=0, keepdims=True)

        along = zeroth * off_u
        m_00, m_10, m_20 = over(zeroth), over(along), over(along * off_u)
        m_01, m_11, m_02 = over(first), over(first * off_u), over(second)
        results.append(
            jnp.concatenate(
                [
                    con_a * m_10 + con_b * m_01,
                    con_c * m_01 + con_b * m_10,
                    -0.5 * m_20,
                    -m_11,
                    -0.5 * m_02,
                    m_00,
                    colour_grad,
                    jnp.zeros((ROWS - 9, 256), F32),
                ],
                axis=0,
            )
        )
    grads = jnp.concatenate(results, axis=1)
    odd = odd_core((4, LOCAL))
    first = jnp.where(odd, grads[0:4], grads[4:8])
    first = jnp.concatenate([first, grads[8:9], jnp.zeros((3, LOCAL), F32)], axis=0)
    given = add_columns(first, idx, hot, 2)
    given_ref[...] = given
    rest_ref[...] = jnp.concatenate(
        [jnp.where(odd, grads[4:8], grads[0:4]), jnp.zeros((4, LOCAL), F32)], axis=0
    )
    index_ref[...] = idx
    turned = sources.T
    wanted = jnp.concatenate([turned[0:PEERS], turned[PEERS:]], axis=1)
    numbers_ref[...] = numbers
    wanted_ref[...] = wanted
    blank = jnp.zeros((PEERS, 128), F32)
    give_ref[pl.ds(0, PEERS, stride=BLOCKS), :] = blank
    write_sums(give_ref, given[0:4], given[4:5], numbers, wanted, True, blank)


def keep_kernel(given_ref, rest_ref, index_ref, numbers_ref, wanted_ref, out_ref):
    idx = index_ref[...]
    given = given_ref[...]
    kept = add_columns(rest_ref[...], idx, low_onehot(idx), 2)[0:4]
    odd = odd_core((4, LOCAL))
    halves_in_order = [jnp.where(odd, given[0:4], kept), jnp.where(odd, kept, given[0:4])]
    out_ref[pl.ds(0, PEERS, stride=BLOCKS), :] = pack_peers(
        jnp.concatenate(halves_in_order, axis=0)
    )
    flat = jnp.concatenate([halves(given[4:5]), jnp.zeros((112, PEERS), F32)], axis=0)
    write_sums(out_ref, kept, given[4:5], numbers_ref[...], wanted_ref[...], False, flat.T)


def owner_kernel(recv_ref, order_ref, shown_ref, share_ref, out_ref):
    lead = unpack_peers(recv_ref[pl.ds(0, PEERS, stride=BLOCKS), :])
    last = joined(recv_ref[pl.ds(1, PEERS, stride=BLOCKS), :].T[0:16])
    values = jnp.concatenate([lead, last, jnp.zeros((ROWS - 9, LOCAL), F32)], axis=0)
    order = order_ref[...]
    owned = add_columns(values, order, low_onehot(order), 2)
    out_ref[0:AT_MOVED, :] = owned[0:9].reshape(9, 8, 128).reshape(AT_MOVED, 128)
    odd = (lax.broadcasted_iota(I32, (PEERS, 128), 0) & 1) > 0

    def sums(block):
        values = recv_ref[pl.ds(block, PEERS, stride=BLOCKS), :]
        return [
            jnp.sum(jnp.where(odd, 0.0, values), axis=0, keepdims=True),
            jnp.sum(jnp.where(odd, values, 0.0), axis=0, keepdims=True),
        ]

    for row in range(4):
        even_sum, odd_sum = sums(2 + row)
        out_ref[AT_MOVED + row : AT_MOVED + row + 1, :] = even_sum
        out_ref[AT_MOVED + 4 + row : AT_MOVED + 5 + row, :] = odd_sum
    even_sum, odd_sum = sums(1)
    out_ref[AT_MOVED + 8 : AT_MOVED + 9, :] = jnp.concatenate(
        [even_sum[:, PEERS:], odd_sum[:, PEERS:]], axis=1
    )
    out_ref[AT_CAMERA : AT_CAMERA + 1, :] = shown_ref[...]
    out_ref[AT_CAMERA + 1 : AT_SHARE, :] = jnp.zeros((AT_SHARE - AT_CAMERA - 1, 128), F32)
    out_ref[AT_SHARE:SENT, :] = share_ref[...]


def log_one_plus(t):
    s = t / (2.0 + t)
    square = s * s
    total = jnp.full_like(s, 1.0 / 17.0)
    for odd in (15, 13, 11, 9, 7, 5, 3, 1):
        total = total * square + 1.0 / odd
    return 2.0 * s * total


def one_minus_exp(x):
    small = jnp.ones_like(x)
    for n in range(10, 1, -1):
        small = 1.0 + small * x * (1.0 / n)
    return jnp.where(x > -0.5, -x * small, 1.0 - jnp.exp(x))


def rates_column():
    row = lax.broadcasted_iota(I32, (59, 1), 0)
    rate = jnp.where(row < 14, 0.0025, 0.000125)
    rate = jnp.where(row < 11, 0.05, rate)
    rate = jnp.where(row < 10, 0.001, rate)
    rate = jnp.where(row < 6, 0.005, rate)
    return jnp.where(row < 3, 0.00016, rate)


def tree_sum(values):
    return (values[0] + values[1]) + (values[2] + values[3])


def adam(params, first_old, second_old, gradient):
    first = 0.9 * first_old + 0.1 * gradient
    second = 0.999 * second_old + 0.001 * gradient * gradient
    stepped = params - rates_column() * (first / BIAS_ONE) / (jnp.sqrt(second / BIAS_TWO) + 1e-15)
    return stepped, first, second


def spread_logit(logit, counts):
    soft = jnp.maximum(logit, 0.0) + log_one_plus(jnp.exp(-jnp.abs(logit)))
    share = -soft / (counts + 1.0)
    return jnp.log(one_minus_exp(share)) - share


def sigmoid_rest(logit):
    return 1.0 - 1.0 / (1.0 + jnp.exp(-logit))


def incoming_columns(parts):
    def stacked(row):
        return jnp.concatenate([ref[row : row + 1, :] for ref in parts], axis=0)

    def folded(x):
        return (x[0:1] + x[1:2]) + (x[2:3] + x[3:4])

    def wide(x):
        return jnp.broadcast_to(x, (VIEWS, 128))

    plane = jnp.full((SHARE, 128), lax.axis_index("view"), I32)
    shares = [ref[AT_SHARE:SENT, :] for ref in parts]
    for bit in (1, 2):
        flip = (plane & bit) > 0
        shares = [jnp.where(flip, shares[i ^ bit], shares[i]) for i in range(VIEWS)]
    params, first_old, second_old = [
        jnp.concatenate([part[i : i + 16] for part in shares], axis=0) for i in (0, 16, 32)
    ]
    rows = [params[i : i + 1] for i in range(59)]
    shown = stacked(AT_CAMERA)
    cam = [wide(shown[:, i : i + 1]) for i in range(16)]
    sigma, pull_sigma = jax.vjp(covariance, rows[3:6], rows[6:10])
    _, pull = jax.vjp(
        lambda p, s, c: view_rows(p, s, c, cam),
        [wide(x) for x in rows[0:3]],
        [wide(x) for x in sigma],
        [wide(x) for x in rows[11:59]],
    )
    got = [stacked(AT_MOVED + i) for i in range(9)]
    d_pos, d_sigma, d_coeff = pull([got[i] for i in (0, 1, 2, 3, 4, 6, 7, 8)])
    d_scale, d_quat = pull_sigma([folded(x) for x in d_sigma])
    d_logit = folded(got[5]) * sigmoid_rest(rows[10])
    gradient = jnp.concatenate(
        [folded(x) for x in d_pos]
        + list(d_scale)
        + list(d_quat)
        + [d_logit]
        + [folded(x) for x in d_coeff],
        axis=0,
    )
    stepped, _, _ = adam(params[0:59], first_old[0:59], second_old[0:59], gradient)
    logit = spread_logit(stepped[10:11], params[59:60])
    row = lax.broadcasted_iota(I32, (59, 128), 0)
    return jnp.concatenate(
        [jnp.where(row == 10, logit, stepped), jnp.ones((5, 128), F32)], axis=0
    )


def pull_view(ref, position, sigma, coeffs):
    got = [ref[8 * i : 8 * i + 8, :] for i in range(9)]
    shown = jnp.broadcast_to(ref[AT_CAMERA : AT_CAMERA + 1, :], (8, 128))
    cam = [jnp.broadcast_to(shown[:, i : i + 1], (8, 128)) for i in range(16)]
    _, pull = jax.vjp(lambda p, s, c: view_rows(p, s, c, cam), position, sigma, coeffs)
    d_pos, d_sigma, d_coeff = pull([got[i] for i in (0, 1, 2, 3, 4, 6, 7, 8)])
    return list(d_pos) + list(d_sigma) + list(d_coeff)


def early_kernel(params_ref, own_ref, last_ref, dense_ref, own_part_ref, last_part_ref):
    dense = params_ref[...].reshape(59, 8, 128)
    dense_ref[...] = dense.reshape(59 * 8, 128)
    rows = [dense[i] for i in range(59)]
    sigma = covariance(rows[3:6], rows[6:10])
    for ref, part_ref in ((own_ref, own_part_ref), (last_ref, last_part_ref)):
        for i, piece in enumerate(pull_view(ref, rows[0:3], sigma, rows[11:59])):
            part_ref[8 * i : 8 * i + 8, :] = piece


def step_kernel(
    dense_ref,
    own_part_ref,
    last_part_ref,
    params_ref,
    first_ref,
    second_ref,
    own_ref,
    near_ref,
    far_ref,
    last_ref,
    counts_ref,
    targets_ref,
    new_params_ref,
    new_first_ref,
    new_second_ref,
    gradient_ref,
):
    parts = (own_ref, near_ref, far_ref, last_ref)
    targets = targets_ref[...]
    placed = add_columns(incoming_columns(parts), targets, low_onehot(targets))
    rows = [dense_ref[8 * i : 8 * i + 8, :] for i in range(59)]
    sigma, pull_sigma = jax.vjp(covariance, rows[3:6], rows[6:10])
    near, far = [pull_view(ref, rows[0:3], sigma, rows[11:59]) for ref in (near_ref, far_ref)]
    total = []
    for i in range(57):
        own, last = [ref[8 * i : 8 * i + 8, :] for ref in (own_part_ref, last_part_ref)]
        total.append((own + near[i]) + (far[i] + last))
    d_pos, d_sigma, d_coeff = total[0:3], total[3:9], total[9:57]
    opacity_parts = [ref[40:48, :] for ref in parts]
    d_scale, d_quat = pull_sigma(d_sigma)
    d_logit = tree_sum(opacity_parts) * sigmoid_rest(rows[10])
    gradient = jnp.stack(d_pos + list(d_scale) + list(d_quat) + [d_logit] + d_coeff).reshape(
        59, LOCAL
    )
    gradient_ref[...] = gradient
    stepped, first, second = adam(params_ref[...], first_ref[...], second_ref[...], gradient)
    counts = counts_ref[...]
    landed = placed[59:60] > 0.5
    cleared = (counts + placed[59:60]) > 0.5
    row = lax.broadcasted_iota(I32, (59, LOCAL), 0)
    spread = jnp.where(
        (row == 10) & (counts > 0.5), spread_logit(stepped[10:11], counts), stepped
    )
    new_params_ref[...] = jnp.where(landed, placed[0:59], spread)
    new_first_ref[...] = jnp.where(cleared, 0.0, first)
    new_second_ref[...] = jnp.where(cleared, 0.0, second)


def call(kernel, shapes, ins, scratch=()):
    spec = {
        "v": pl.BlockSpec(memory_space=pltpu.VMEM),
        "s": pl.BlockSpec(memory_space=pltpu.SMEM),
        "h": pl.BlockSpec(memory_space=pltpu.HBM),
    }
    out_shape = [jax.ShapeDtypeStruct(shape, dtype) for shape, dtype in shapes]
    return pl.pallas_call(
        kernel,
        out_shape=out_shape,
        in_specs=[spec[kind] for kind in ins],
        out_specs=[spec["v"]] * len(out_shape),
        scratch_shapes=list(scratch),
        compiler_params=pltpu.CompilerParams(vmem_limit_bytes=VMEM_LIMIT),
    )


def in_hbm(array):
    return pltpu.with_memory_space_constraint(array, pltpu.HBM)


def exchange(block):
    parts = block.reshape(PEERS, 1, -1)
    got = lax.all_to_all(parts, "gauss", split_axis=0, concat_axis=0, tiled=True)
    return got.reshape(block.shape)


def shards(
    params,
    first_moment,
    second_moment,
    cameras,
    target,
    tile_index,
    tile_lists,
    send_slots,
    reloc_send,
    reloc_recv,
):
    columns = ((1, LOCAL), I32)
    whole = ((59, LOCAL), F32)
    outgoing, order, entries, corners, wanted, counts, landing, shown = call(
        send_kernel,
        [
            ((3 * PEERS, 128), F32),
            columns,
            columns,
            ((2 * TILES, 256), F32),
            ((3, TILES, 256), F32),
            ((1, LOCAL), F32),
            ((1, 128), I32),
            ((1, 128), F32),
        ],
        "hhhhhhhhhh",
        [
            pltpu.VMEM((59, LOCAL), F32),
            pltpu.VMEM((59, LOCAL), F32),
            pltpu.VMEM((59, LOCAL), F32),
            pltpu.VMEM((8, 128), I32),
            pltpu.VMEM((1, 128), I32),
            pltpu.VMEM((1, 128), I32),
            pltpu.SMEM((1, 16), F32),
            pltpu.VMEM((1, TILES, 256), I32),
            pltpu.SMEM((1, TILES), I32),
            pltpu.SemaphoreType.DMA((10,)),
        ],
    )(
        in_hbm(params),
        in_hbm(first_moment),
        in_hbm(second_moment),
        in_hbm(send_slots.reshape(8, 128)),
        in_hbm(reloc_send),
        in_hbm(reloc_recv),
        in_hbm(cameras),
        in_hbm(tile_lists),
        in_hbm(tile_index),
        in_hbm(jnp.transpose(target[0], (1, 0, 2))),
    )
    received = exchange(outgoing)
    back = ((BLOCKS * PEERS, 128), F32)
    eight = ((8, LOCAL), F32)
    give, share, given, rest, index, numbers, asked = call(
        render_kernel,
        [
            back,
            ((SHARE, 128), F32),
            eight,
            eight,
            columns,
            ((1, LOCAL), F32),
            ((PEERS, 128), F32),
        ],
        "vvvv",
        [pltpu.VMEM((TILES, 256, 256), F32), pltpu.VMEM((TILES, 256, 256), F32)],
    )(received, entries, corners, wanted)
    sibling = lax.ppermute(give, "gauss", [(i, i ^ 1) for i in range(PEERS)])
    (kept,) = call(keep_kernel, [back], "vvvvv")(given, rest, index, numbers, asked)
    returned = exchange(kept + sibling)
    (own,) = call(owner_kernel, [((SENT, 128), F32)], "vvvv")(returned, order, shown, share)
    others = [
        lax.ppermute(own, "view", [(i, i ^ flip) for i in range(VIEWS)]) for flip in (1, 2, 3)
    ]
    tiles = ((57 * 8, 128), F32)
    dense, own_part, last_part = call(early_kernel, [((59 * 8, 128), F32), tiles, tiles], "vvv")(
        params, own, others[2]
    )
    return call(step_kernel, [whole, whole, whole, whole], "vvvvvvvvvvvv")(
        dense, own_part, last_part, params, first_moment, second_moment, own, *others, counts, landing
    )


def solution(mesh):
    in_specs = (
        P(None, "gauss"),
        P(None, "gauss"),
        P(None, "gauss"),
        P("view", None),
        P("view", "gauss", None, None),
        P("view", "gauss"),
        P("view", "gauss", None),
        P("view", "gauss", None),
        P("gauss", None),
        P("gauss", None),
    )
    out_specs = (P(None, "gauss"), P(None, "gauss"), P(None, "gauss"), P(None, "gauss"))
    return jax.shard_map(shards, mesh=mesh, in_specs=in_specs, out_specs=out_specs, check_vma=False)
```

```python
import math

import jax
import jax.numpy as jnp
from jax import lax
from jax.experimental import pallas as pl
from jax.experimental.pallas import tpu as pltpu
from jax.sharding import PartitionSpec as P

F32 = jnp.float32
BF16 = jnp.bfloat16
I32 = jnp.int32
PEERS = 64
LOCAL = 1024
CAP = 16
VIEWS = 4
TILES = 4
ACROSS = 16
ROWS = 16
LOG2E = 1.4426950408889634
SHARE = 48
BLOCKS = 6
AT_MOVED = 72
AT_CAMERA = 81
AT_SHARE = 88
SENT = 136

SH_ZERO = 0.28209479177387814
SH_ONE = 0.4886025119029199
SH_TWO = (
    1.0925484305920792,
    -1.0925484305920792,
    0.31539156525252005,
    -1.0925484305920792,
    0.5462742152960396,
)
SH_THREE = (
    -0.5900435899266435,
    2.890611442640554,
    -0.4570457994644658,
    0.3731763325901154,
    -0.4570457994644658,
    1.445305721320277,
    -0.5900435899266435,
)
BIAS_ONE = 1.0 - math.exp(1000.0 * math.log(0.9))
BIAS_TWO = 1.0 - math.exp(1000.0 * math.log(0.999))
VMEM_LIMIT = 16 * 1024 * 1024


def split(x, parts):
    out = []
    for index in range(parts):
        piece = x.astype(BF16)
        out.append(piece)
        if index + 1 < parts:
            x = x - piece.astype(F32)
    return out


def low_onehot(idx):
    lane = lax.broadcasted_iota(I32, (128, idx.shape[1]), 0)
    return jnp.where(lane == (idx & 127), 1.0, 0.0).astype(BF16)


def take_columns(table, idx, hot):
    rows = table.shape[0]
    high = idx >> 7
    parts = split(table, 3)
    lhs = jnp.concatenate(
        [
            jnp.concatenate([p[:, c * 128 : (c + 1) * 128] for p in parts], axis=1)
            for c in range(8)
        ],
        axis=0,
    )
    rhs = jnp.concatenate([hot, hot, hot], axis=0)
    wide = jnp.dot(lhs, rhs, preferred_element_type=F32)
    total = None
    for c in range(8):
        term = jnp.where(high == c, wide[c * rows : (c + 1) * rows], 0.0)
        total = term if total is None else total + term
    return total


def add_columns(values, idx, hot, parts=3):
    rows = values.shape[0]
    high = idx >> 7
    pieces = []
    for piece in split(values, parts):
        piece = piece.astype(F32)
        pieces += [jnp.where(high == c, piece, 0.0) for c in range(8)]
    lhs = jnp.concatenate(pieces, axis=0).astype(BF16)
    wide = lax.dot_general(lhs, hot, (((1,), (1,)), ((), ())), preferred_element_type=F32)
    size = 8 * rows
    wide = sum(wide[i * size : (i + 1) * size] for i in range(1, parts)) + wide[0:size]
    return jnp.concatenate([wide[c * rows : (c + 1) * rows] for c in range(8)], axis=1)


def pack_peers(table):
    pieces = [table[:, k * PEERS : (k + 1) * PEERS] for k in range(CAP)]
    return jnp.concatenate(pieces, axis=0).T


def unpack_peers(block):
    flat = block.T
    return jnp.concatenate([flat[k * 8 : (k + 1) * 8] for k in range(CAP)], axis=1)


def halves(row):
    block = row.reshape(8, 128)
    return jnp.concatenate([block[:, 0:PEERS], block[:, PEERS:]], axis=0)


def joined(block):
    return jnp.concatenate([block[0:8], block[8:16]], axis=1).reshape(1, LOCAL)


def slots_by_rank(slots):
    source = lax.broadcasted_iota(I32, (128, LOCAL), 0)
    col = lax.broadcasted_iota(I32, (128, LOCAL), 1)
    pick = jnp.where(source == (col & 7) * 16 + (col >> 6), 1.0, 0.0).astype(BF16)
    upper = jnp.dot((slots >> 5).astype(F32).astype(BF16), pick, preferred_element_type=F32)
    lower = jnp.dot((slots & 31).astype(F32).astype(BF16), pick, preferred_element_type=F32)
    wide = upper * 32.0 + lower
    row = lax.broadcasted_iota(I32, (8, LOCAL), 0)
    column = lax.broadcasted_iota(I32, (8, LOCAL), 1)
    kept = jnp.where(row == ((column >> 3) & 7), wide, 0.0)
    return jnp.sum(kept, axis=0, keepdims=True).astype(I32)


def pairs_by_rank(pairs):
    source = lax.broadcasted_iota(I32, (128, 128), 0)
    col = lax.broadcasted_iota(I32, (128, 128), 1)
    pick = jnp.where(source == (col & (PEERS - 1)) * 2 + (col >> 6), 1.0, 0.0).astype(BF16)
    wide = jnp.broadcast_to(pairs + 1, (8, 128))
    upper = jnp.dot((wide >> 5).astype(F32).astype(BF16), pick, preferred_element_type=F32)
    lower = jnp.dot((wide & 31).astype(F32).astype(BF16), pick, preferred_element_type=F32)
    return (upper * 32.0 + lower)[0:1].astype(I32) - 1


def covariance(log_scale, quat):
    norm = jnp.sqrt(quat[0] * quat[0] + quat[1] * quat[1] + quat[2] * quat[2] + quat[3] * quat[3])
    quat_w, quat_x, quat_y, quat_z = [q / norm for q in quat]
    orient = [
        [
            1.0 - 2.0 * (quat_y * quat_y + quat_z * quat_z),
            2.0 * (quat_x * quat_y - quat_w * quat_z),
            2.0 * (quat_x * quat_z + quat_w * quat_y),
        ],
        [
            2.0 * (quat_x * quat_y + quat_w * quat_z),
            1.0 - 2.0 * (quat_x * quat_x + quat_z * quat_z),
            2.0 * (quat_y * quat_z - quat_w * quat_x),
        ],
        [
            2.0 * (quat_x * quat_z - quat_w * quat_y),
            2.0 * (quat_y * quat_z + quat_w * quat_x),
            1.0 - 2.0 * (quat_x * quat_x + quat_y * quat_y),
        ],
    ]
    scales = [jnp.exp(s) for s in log_scale]
    factor = [[orient[i][j] * scales[j] for j in range(3)] for i in range(3)]

    def entry(i, j):
        return (
            factor[i][0] * factor[j][0] + factor[i][1] * factor[j][1] + factor[i][2] * factor[j][2]
        )

    return [entry(0, 0), entry(0, 1), entry(0, 2), entry(1, 1), entry(1, 2), entry(2, 2)]


def harmonics(dir_x, dir_y, dir_z):
    sq_x, sq_y, sq_z = (dir_x * dir_x, dir_y * dir_y, dir_z * dir_z)
    return [
        -SH_ONE * dir_y,
        SH_ONE * dir_z,
        -SH_ONE * dir_x,
        SH_TWO[0] * dir_x * dir_y,
        SH_TWO[1] * dir_y * dir_z,
        SH_TWO[2] * (2.0 * sq_z - sq_x - sq_y),
        SH_TWO[3] * dir_x * dir_z,
        SH_TWO[4] * (sq_x - sq_y),
        SH_THREE[0] * dir_y * (3.0 * sq_x - sq_y),
        SH_THREE[1] * dir_x * dir_y * dir_z,
        SH_THREE[2] * dir_y * (4.0 * sq_z - sq_x - sq_y),
        SH_THREE[3] * dir_z * (2.0 * sq_z - 3.0 * sq_x - 3.0 * sq_y),
        SH_THREE[4] * dir_x * (4.0 * sq_z - sq_x - sq_y),
        SH_THREE[5] * dir_z * (sq_x - sq_y),
        SH_THREE[6] * dir_x * (sq_x - 3.0 * sq_y),
    ]


def view_rows(position, sigma, coeffs, cam):
    rot = [cam[0:3], cam[3:6], cam[6:9]]
    offset = cam[9:12]
    focal_x, focal_y, centre_x, centre_y = cam[12:16]
    cam_x, cam_y, cam_z = [
        rot[i][0] * position[0] + rot[i][1] * position[1] + rot[i][2] * position[2] + offset[i]
        for i in range(3)
    ]
    inverse_z = 1.0 / cam_z
    mean_u = focal_x * cam_x * inverse_z + centre_x
    mean_w = focal_y * cam_y * inverse_z + centre_y
    jac_a0 = focal_x * inverse_z
    jac_a2 = -focal_x * cam_x * inverse_z * inverse_z
    jac_b1 = focal_y * inverse_z
    jac_b2 = -focal_y * cam_y * inverse_z * inverse_z
    row_a = [jac_a0 * rot[0][i] + jac_a2 * rot[2][i] for i in range(3)]
    row_b = [jac_b1 * rot[1][i] + jac_b2 * rot[2][i] for i in range(3)]
    full = [
        [sigma[0], sigma[1], sigma[2]],
        [sigma[1], sigma[3], sigma[4]],
        [sigma[2], sigma[4], sigma[5]],
    ]

    def through(row):
        return [full[i][0] * row[0] + full[i][1] * row[1] + full[i][2] * row[2] for i in range(3)]

    def dot3(left, right):
        return left[0] * right[0] + left[1] * right[1] + left[2] * right[2]

    sigma_a = through(row_a)
    sigma_b = through(row_b)
    cov_aa = dot3(row_a, sigma_a) + 0.3
    cov_ab = dot3(row_a, sigma_b)
    cov_bb = dot3(row_b, sigma_b) + 0.3
    determinant = cov_aa * cov_bb - cov_ab * cov_ab
    inverse_det = 1.0 / determinant
    ray = [
        position[i] + (rot[0][i] * offset[0] + rot[1][i] * offset[1] + rot[2][i] * offset[2])
        for i in range(3)
    ]
    inverse_norm = 1.0 / jnp.sqrt(dot3(ray, ray))
    basis = harmonics(*[r * inverse_norm for r in ray])
    colours = []
    for channel in range(3):
        total = SH_ZERO * coeffs[channel]
        for index in range(15):
            total = total + basis[index] * coeffs[3 + 3 * index + channel]
        colours.append(jnp.maximum(total + 0.5, 0.0))
    return [
        mean_u,
        mean_w,
        cov_bb * inverse_det,
        -cov_ab * inverse_det,
        cov_aa * inverse_det,
    ] + colours


def send_kernel(
    params_hbm,
    first_hbm,
    second_hbm,
    slots_hbm,
    sources_hbm,
    targets_hbm,
    camera_hbm,
    lists_hbm,
    tiles_hbm,
    wanted_hbm,
    out_ref,
    order_ref,
    entries_ref,
    corner_ref,
    wanted_ref,
    counts_ref,
    landing_ref,
    shown_ref,
    params_ref,
    first_ref,
    second_ref,
    slots_ref,
    sources_ref,
    targets_ref,
    camera_ref,
    lists_ref,
    tiles_ref,
    sems,
):
    pairs = (
        (slots_hbm, slots_ref),
        (params_hbm, params_ref),
        (camera_hbm, camera_ref),
        (sources_hbm, sources_ref),
        (targets_hbm, targets_ref),
        (lists_hbm, lists_ref),
        (tiles_hbm, tiles_ref),
        (wanted_hbm, wanted_ref),
        (first_hbm, first_ref),
        (second_hbm, second_ref),
    )
    copies = [pltpu.make_async_copy(a, b, sems.at[i]) for i, (a, b) in enumerate(pairs)]
    for copy in copies:
        copy.start()
    for at in (0, 3, 4):
        copies[at].wait()
    order = slots_by_rank(slots_ref[...])
    order_ref[...] = order
    hot = low_onehot(order)
    sources = pairs_by_rank(sources_ref[...])
    source_hot = low_onehot(sources)
    counts = add_columns(jnp.ones((8, 128), F32), sources, source_hot, 1)[0:1]
    counts_ref[...] = counts
    out_ref[pl.ds(2, PEERS, stride=3), :] = jnp.broadcast_to(sources.astype(F32), (PEERS, 128))
    landing_ref[...] = pairs_by_rank(targets_ref[...])
    for at in (1, 2, 5, 6, 7, 8, 9):
        copies[at].wait()
    dense = params_ref[...].reshape(59, 8, 128)
    rows = [dense[i] for i in range(59)]
    cam = [camera_ref[0, i] for i in range(16)]
    sigma = covariance(rows[3:6], rows[6:10])
    seen = view_rows(rows[0:3], sigma, rows[11:59], cam)
    opacity = 1.0 / (1.0 + jnp.exp(-rows[10]))
    listed = seen[0:5] + [opacity] + seen[5:8]
    blank = jnp.zeros((8, 128), F32)
    table = jnp.stack(listed + [blank] * (ROWS - 9)).reshape(ROWS, LOCAL)
    taken = take_columns(table, order, hot)
    out_ref[pl.ds(0, PEERS, stride=3), :] = pack_peers(taken[0:8])
    plane = jnp.full((16, LOCAL), lax.axis_index("view"), I32)
    share = []
    for ref in (params_ref, first_ref, second_ref):
        final = jnp.concatenate([ref[48:59, :], jnp.broadcast_to(counts, (5, LOCAL))], axis=0)
        low = jnp.where(plane == 0, ref[0:16, :], ref[16:32, :])
        share.append(jnp.where(plane < 2, low, jnp.where(plane == 2, ref[32:48, :], final)))
    moved = take_columns(jnp.concatenate(share, axis=0), sources, source_hot)
    moved = jnp.concatenate([moved[:, 0:PEERS], moved[:, PEERS:]], axis=0)
    flat = jnp.concatenate([halves(taken[8:9]), halves(order.astype(F32)), moved], axis=0)
    out_ref[pl.ds(1, PEERS, stride=3), :] = flat.T
    entries_ref[...] = jnp.concatenate([lists_ref[0, i : i + 1] for i in range(TILES)], axis=1)
    for tile in range(TILES):
        number = tiles_ref[0, tile]
        corner_ref[tile : tile + 1, :] = jnp.full(
            (1, 256), ((number & (ACROSS - 1)) * 16).astype(F32)
        )
        corner_ref[TILES + tile : TILES + tile + 1, :] = jnp.full(
            (1, 256), ((number >> 4) * 16).astype(F32)
        )
    lane = lax.broadcasted_iota(I32, (1, 128), 1)
    shown = jnp.zeros((1, 128), F32)
    for i in range(16):
        shown = jnp.where(lane == i, cam[i], shown)
    shown_ref[...] = shown


def odd_core(shape):
    return jnp.full(shape, lax.axis_index("gauss") & 1, I32) > 0


def write_sums(out_ref, four, ninth, numbers, wanted, give, left):
    odd = odd_core((8, 128))
    right = lax.broadcasted_iota(I32, (8, 128), 1) >= PEERS
    stack = jnp.concatenate([four, ninth, numbers], axis=0)
    rows = [[] for _ in range(6)]
    for k in range(CAP):
        lines = stack[:, k * PEERS : (k + 1) * PEERS]
        lines = jnp.concatenate([lines, lines], axis=1)
        for row in range(6):
            rows[row].append(jnp.broadcast_to(lines[row : row + 1], (8, 128)))
    for group in range(PEERS // 8):
        span = slice(group * 8, (group + 1) * 8)
        totals = [None] * 5
        for k in range(CAP):
            same = wanted[span] == rows[5][k]
            for row in range(5):
                term = jnp.where(same, rows[row][k], 0.0)
                totals[row] = term if k == 0 else totals[row] + term
        start = group * 8 * BLOCKS
        turn = pltpu.roll(totals[4], PEERS, axis=1)
        half = jnp.where(odd, turn, totals[4]) if give else jnp.where(odd, totals[4], turn)
        out_ref[pl.ds(start + 1, 8, stride=BLOCKS), :] = jnp.where(right, half, left[span])
        for row in range(4):
            out_ref[pl.ds(start + 2 + row, 8, stride=BLOCKS), :] = totals[row]


def render_kernel(
    recv_ref,
    entries_ref,
    corner_ref,
    target_ref,
    give_ref,
    share_ref,
    given_ref,
    rest_ref,
    index_ref,
    numbers_ref,
    wanted_ref,
    alpha_ref,
    grad_ref,
):
    lead = recv_ref[pl.ds(0, PEERS, stride=3), :]
    tail = recv_ref[pl.ds(1, PEERS, stride=3), :]
    sources = recv_ref[pl.ds(2, PEERS, stride=3), :]
    flat = tail.T
    share_ref[...] = jnp.concatenate([flat[32 : 32 + SHARE], flat[32 + SHARE :]], axis=1)
    numbers = joined(flat[16:32])
    table = jnp.concatenate(
        [unpack_peers(lead), joined(flat[0:16]), jnp.zeros((ROWS - 9, LOCAL), F32)], axis=0
    )
    entries = entries_ref[...]
    idx = jnp.where(entries < 0, -1, (entries & 15) * PEERS + (entries >> 4))
    hot = low_onehot(idx)
    listed = take_columns(table, idx, hot)
    iota_r = lax.broadcasted_iota(I32, (256, 256), 0)
    iota_c = lax.broadcasted_iota(I32, (256, 256), 1)
    before_mask = jnp.where(iota_r < iota_c, 1.0, 0.0).astype(BF16)
    before_mask = jnp.concatenate([before_mask, before_mask], axis=0)
    after_mask = jnp.where(iota_r > iota_c, 1.0, 0.0).astype(BF16)
    after_mask = jnp.concatenate([after_mask, after_mask], axis=0)
    steps = lax.broadcasted_iota(I32, (16, 256), 0).astype(F32)
    nt = (((1,), (1,)), ((), ()))
    tiles = range(TILES)
    heres, offs_u, offs_w = [], [], []
    for tile in tiles:
        here = listed[:, tile * 256 : (tile + 1) * 256]
        left = corner_ref[tile : tile + 1]
        top = corner_ref[TILES + tile : TILES + tile + 1]
        con_a, con_b, con_c, opacity = here[2:3], here[3:4], here[4:5], here[5:6]
        off_u = (steps + left + 0.5) - here[0:1]
        off_w = (steps + top + 0.5) - here[1:2]
        quad_u = LOG2E * (jnp.log(opacity) - 0.5 * con_a * off_u * off_u)
        cross = -LOG2E * con_b * off_u
        quad_w = (-0.5 * LOG2E) * con_c * off_w * off_w
        for j in range(16):
            exponent = quad_u + quad_w[j : j + 1] + cross * off_w[j : j + 1]
            alpha_ref[tile, j * 16 : (j + 1) * 16, :] = jnp.exp2(exponent)
        heres.append(here)
        offs_u.append(off_u)
        offs_w.append(off_w)
    log_keeps, befores = [], []
    for t in tiles:
        log_keeps.append(jnp.log(1.0 - alpha_ref[t]))
        logs = jnp.concatenate(split(log_keeps[t], 2), axis=1)
        befores.append(jnp.dot(logs, before_mask, preferred_element_type=F32))
    weights = [jnp.exp(befores[t]) * alpha_ref[t] for t in tiles]
    weight_parts = [split(x, 2) for x in weights]
    colour_parts = [split(here[6:9], 3) for here in heres]
    residual_parts = []
    for tile in tiles:
        stacked = jnp.concatenate(
            [p.astype(F32) for p in colour_parts[tile]] + [jnp.zeros((7, 256), F32)], axis=0
        ).astype(BF16)
        summed = lax.dot_general(
            jnp.concatenate([stacked, stacked], axis=1),
            jnp.concatenate(weight_parts[tile], axis=1),
            nt,
            preferred_element_type=F32,
        )
        residual = summed[0:3] + summed[3:6] + summed[6:9] - target_ref[:, tile]
        residual_parts.append([p.astype(F32) for p in split(residual, 3)])
    pairs = ((0, 0), (0, 1), (1, 0), (1, 1), (0, 2), (2, 0))
    blank = jnp.zeros((14, 256), F32)
    pulls = []
    for tile in tiles:
        left_side = jnp.concatenate([residual_parts[tile][a] for a, _ in pairs] + [blank], axis=0)
        right_side = jnp.concatenate(
            [colour_parts[tile][b].astype(F32) for _, b in pairs] + [blank], axis=0
        )
        pulls.append(
            lax.dot_general(
                left_side.astype(BF16),
                right_side.astype(BF16),
                (((0,), (0,)), ((), ())),
                preferred_element_type=F32,
            )
        )
    weighteds, afters = [], []
    for t in tiles:
        weighteds.append(pulls[t] * weights[t])
        flow = jnp.concatenate(split(weighteds[t], 2), axis=1)
        afters.append(jnp.dot(flow, after_mask, preferred_element_type=F32))
    for t in tiles:
        grad_ref[t] = weighteds[t] - afters[t] * (alpha_ref[t] * jnp.exp(-log_keeps[t]))
    results = []
    for tile in tiles:
        here, off_u, off_w = heres[tile], offs_u[tile], offs_w[tile]
        con_a, con_b, con_c = here[2:3], here[3:4], here[4:5]
        stacked_res = jnp.concatenate(
            residual_parts[tile] + [jnp.zeros((7, 256), F32)], axis=0
        ).astype(BF16)
        colour_sum = jnp.dot(
            jnp.concatenate([stacked_res, stacked_res], axis=1),
            jnp.concatenate(weight_parts[tile], axis=0),
            preferred_element_type=F32,
        )
        colour_grad = colour_sum[0:3] + colour_sum[3:6] + colour_sum[6:9]
        zeroth = first = second = grad_ref[tile, 240:256, :]
        for j in range(14, -1, -1):
            zeroth = zeroth + grad_ref[tile, j * 16 : (j + 1) * 16, :]
            first = first + zeroth
            second = second + first
        start = off_w[0:1]
        by_step = first - zeroth
        by_square = 2.0 * second - 3.0 * by_step - 2.0 * zeroth
        first = start * zeroth + by_step
        second = start * (first + by_step) + by_square

        def over(values):
            return jnp.sum(values, axis=0, keepdims=True)

        along = zeroth * off_u
        m_00, m_10, m_20 = over(zeroth), over(along), over(along * off_u)
        m_01, m_11, m_02 = over(first), over(first * off_u), over(second)
        results.append(
            jnp.concatenate(
                [
                    con_a * m_10 + con_b * m_01,
                    con_c * m_01 + con_b * m_10,
                    -0.5 * m_20,
                    -m_11,
                    -0.5 * m_02,
                    m_00,
                    colour_grad,
                    jnp.zeros((ROWS - 9, 256), F32),
                ],
                axis=0,
            )
        )
    grads = jnp.concatenate(results, axis=1)
    odd = odd_core((4, LOCAL))
    first = jnp.where(odd, grads[0:4], grads[4:8])
    first = jnp.concatenate([first, grads[8:9], jnp.zeros((3, LOCAL), F32)], axis=0)
    given = add_columns(first, idx, hot, 2)
    given_ref[...] = given
    rest_ref[...] = jnp.concatenate(
        [jnp.where(odd, grads[4:8], grads[0:4]), jnp.zeros((4, LOCAL), F32)], axis=0
    )
    index_ref[...] = idx
    turned = sources.T
    wanted = jnp.concatenate([turned[0:PEERS], turned[PEERS:]], axis=1)
    numbers_ref[...] = numbers
    wanted_ref[...] = wanted
    blank = jnp.zeros((PEERS, 128), F32)
    give_ref[pl.ds(0, PEERS, stride=BLOCKS), :] = blank
    write_sums(give_ref, given[0:4], given[4:5], numbers, wanted, True, blank)


def keep_kernel(given_ref, rest_ref, index_ref, numbers_ref, wanted_ref, out_ref):
    idx = index_ref[...]
    given = given_ref[...]
    kept = add_columns(rest_ref[...], idx, low_onehot(idx), 2)[0:4]
    odd = odd_core((4, LOCAL))
    halves_in_order = [jnp.where(odd, given[0:4], kept), jnp.where(odd, kept, given[0:4])]
    out_ref[pl.ds(0, PEERS, stride=BLOCKS), :] = pack_peers(
        jnp.concatenate(halves_in_order, axis=0)
    )
    flat = jnp.concatenate([halves(given[4:5]), jnp.zeros((112, PEERS), F32)], axis=0)
    write_sums(out_ref, kept, given[4:5], numbers_ref[...], wanted_ref[...], False, flat.T)


def owner_kernel(recv_ref, order_ref, shown_ref, share_ref, out_ref):
    lead = unpack_peers(recv_ref[pl.ds(0, PEERS, stride=BLOCKS), :])
    last = joined(recv_ref[pl.ds(1, PEERS, stride=BLOCKS), :].T[0:16])
    values = jnp.concatenate([lead, last, jnp.zeros((ROWS - 9, LOCAL), F32)], axis=0)
    order = order_ref[...]
    owned = add_columns(values, order, low_onehot(order), 2)
    out_ref[0:AT_MOVED, :] = owned[0:9].reshape(9, 8, 128).reshape(AT_MOVED, 128)
    odd = (lax.broadcasted_iota(I32, (PEERS, 128), 0) & 1) > 0

    def sums(block):
        values = recv_ref[pl.ds(block, PEERS, stride=BLOCKS), :]
        return [
            jnp.sum(jnp.where(odd, 0.0, values), axis=0, keepdims=True),
            jnp.sum(jnp.where(odd, values, 0.0), axis=0, keepdims=True),
        ]

    for row in range(4):
        even_sum, odd_sum = sums(2 + row)
        out_ref[AT_MOVED + row : AT_MOVED + row + 1, :] = even_sum
        out_ref[AT_MOVED + 4 + row : AT_MOVED + 5 + row, :] = odd_sum
    even_sum, odd_sum = sums(1)
    out_ref[AT_MOVED + 8 : AT_MOVED + 9, :] = jnp.concatenate(
        [even_sum[:, PEERS:], odd_sum[:, PEERS:]], axis=1
    )
    out_ref[AT_CAMERA : AT_CAMERA + 1, :] = shown_ref[...]
    out_ref[AT_CAMERA + 1 : AT_SHARE, :] = jnp.zeros((AT_SHARE - AT_CAMERA - 1, 128), F32)
    out_ref[AT_SHARE:SENT, :] = share_ref[...]


def log_one_plus(t):
    s = t / (2.0 + t)
    square = s * s
    total = jnp.full_like(s, 1.0 / 17.0)
    for odd in (15, 13, 11, 9, 7, 5, 3, 1):
        total = total * square + 1.0 / odd
    return 2.0 * s * total


def one_minus_exp(x):
    small = jnp.ones_like(x)
    for n in range(10, 1, -1):
        small = 1.0 + small * x * (1.0 / n)
    return jnp.where(x > -0.5, -x * small, 1.0 - jnp.exp(x))


def rates_column():
    row = lax.broadcasted_iota(I32, (59, 1), 0)
    rate = jnp.where(row < 14, 0.0025, 0.000125)
    rate = jnp.where(row < 11, 0.05, rate)
    rate = jnp.where(row < 10, 0.001, rate)
    rate = jnp.where(row < 6, 0.005, rate)
    return jnp.where(row < 3, 0.00016, rate)


def tree_sum(values):
    return (values[0] + values[1]) + (values[2] + values[3])


def adam(params, first_old, second_old, gradient):
    first = 0.9 * first_old + 0.1 * gradient
    second = 0.999 * second_old + 0.001 * gradient * gradient
    scale = rates_column() * (1.0 / BIAS_ONE)
    stepped = params - scale * first / (jnp.sqrt(second * (1.0 / BIAS_TWO)) + 1e-15)
    return stepped, first, second


def spread_logit(logit, counts):
    soft = jnp.maximum(logit, 0.0) + log_one_plus(jnp.exp(-jnp.abs(logit)))
    share = -soft / (counts + 1.0)
    return jnp.log(one_minus_exp(share)) - share


def sigmoid_rest(logit):
    return 1.0 - 1.0 / (1.0 + jnp.exp(-logit))


def incoming_columns(parts):
    def stacked(row):
        return jnp.concatenate([ref[row : row + 1, :] for ref in parts], axis=0)

    def folded(x):
        return (x[0:1] + x[1:2]) + (x[2:3] + x[3:4])

    def wide(x):
        return jnp.broadcast_to(x, (VIEWS, 128))

    plane = jnp.full((SHARE, 128), lax.axis_index("view"), I32)
    shares = [ref[AT_SHARE:SENT, :] for ref in parts]
    for bit in (1, 2):
        flip = (plane & bit) > 0
        shares = [jnp.where(flip, shares[i ^ bit], shares[i]) for i in range(VIEWS)]
    params, first_old, second_old = [
        jnp.concatenate([part[i : i + 16] for part in shares], axis=0) for i in (0, 16, 32)
    ]
    rows = [params[i : i + 1] for i in range(59)]
    shown = stacked(AT_CAMERA)
    cam = [wide(shown[:, i : i + 1]) for i in range(16)]
    sigma, pull_sigma = jax.vjp(covariance, rows[3:6], rows[6:10])
    _, pull = jax.vjp(
        lambda p, s, c: view_rows(p, s, c, cam),
        [wide(x) for x in rows[0:3]],
        [wide(x) for x in sigma],
        [wide(x) for x in rows[11:59]],
    )
    got = [stacked(AT_MOVED + i) for i in range(9)]
    d_pos, d_sigma, d_coeff = pull([got[i] for i in (0, 1, 2, 3, 4, 6, 7, 8)])
    d_scale, d_quat = pull_sigma([folded(x) for x in d_sigma])
    d_logit = folded(got[5]) * sigmoid_rest(rows[10])
    gradient = jnp.concatenate(
        [folded(x) for x in d_pos]
        + list(d_scale)
        + list(d_quat)
        + [d_logit]
        + [folded(x) for x in d_coeff],
        axis=0,
    )
    stepped, _, _ = adam(params[0:59], first_old[0:59], second_old[0:59], gradient)
    logit = spread_logit(stepped[10:11], params[59:60])
    row = lax.broadcasted_iota(I32, (59, 128), 0)
    return jnp.concatenate(
        [jnp.where(row == 10, logit, stepped), jnp.ones((5, 128), F32)], axis=0
    )


def pull_view(ref, position, sigma, coeffs):
    got = [ref[8 * i : 8 * i + 8, :] for i in range(9)]
    shown = jnp.broadcast_to(ref[AT_CAMERA : AT_CAMERA + 1, :], (8, 128))
    cam = [jnp.broadcast_to(shown[:, i : i + 1], (8, 128)) for i in range(16)]
    _, pull = jax.vjp(lambda p, s, c: view_rows(p, s, c, cam), position, sigma, coeffs)
    d_pos, d_sigma, d_coeff = pull([got[i] for i in (0, 1, 2, 3, 4, 6, 7, 8)])
    return list(d_pos) + list(d_sigma) + list(d_coeff)


def early_kernel(params_ref, own_ref, last_ref, dense_ref, own_part_ref, last_part_ref):
    dense = params_ref[...].reshape(59, 8, 128)
    dense_ref[...] = dense.reshape(59 * 8, 128)
    rows = [dense[i] for i in range(59)]
    sigma = covariance(rows[3:6], rows[6:10])
    for ref, part_ref in ((own_ref, own_part_ref), (last_ref, last_part_ref)):
        for i, piece in enumerate(pull_view(ref, rows[0:3], sigma, rows[11:59])):
            part_ref[8 * i : 8 * i + 8, :] = piece


def step_kernel(
    dense_ref,
    own_part_ref,
    last_part_ref,
    params_ref,
    first_ref,
    second_ref,
    own_ref,
    near_ref,
    far_ref,
    last_ref,
    counts_ref,
    targets_ref,
    new_params_ref,
    new_first_ref,
    new_second_ref,
    gradient_ref,
):
    parts = (own_ref, near_ref, far_ref, last_ref)
    targets = targets_ref[...]
    placed = add_columns(incoming_columns(parts), targets, low_onehot(targets))
    rows = [dense_ref[8 * i : 8 * i + 8, :] for i in range(59)]
    sigma, pull_sigma = jax.vjp(covariance, rows[3:6], rows[6:10])
    near, far = [pull_view(ref, rows[0:3], sigma, rows[11:59]) for ref in (near_ref, far_ref)]
    total = []
    for i in range(57):
        own, last = [ref[8 * i : 8 * i + 8, :] for ref in (own_part_ref, last_part_ref)]
        total.append((own + near[i]) + (far[i] + last))
    d_pos, d_sigma, d_coeff = total[0:3], total[3:9], total[9:57]
    opacity_parts = [ref[40:48, :] for ref in parts]
    d_scale, d_quat = pull_sigma(d_sigma)
    d_logit = tree_sum(opacity_parts) * sigmoid_rest(rows[10])
    gradient = jnp.stack(d_pos + list(d_scale) + list(d_quat) + [d_logit] + d_coeff).reshape(
        59, LOCAL
    )
    gradient_ref[...] = gradient
    stepped, first, second = adam(params_ref[...], first_ref[...], second_ref[...], gradient)
    counts = counts_ref[...]
    landed = placed[59:60] > 0.5
    cleared = (counts + placed[59:60]) > 0.5
    row = lax.broadcasted_iota(I32, (59, LOCAL), 0)
    spread = jnp.where(
        (row == 10) & (counts > 0.5), spread_logit(stepped[10:11], counts), stepped
    )
    new_params_ref[...] = jnp.where(landed, placed[0:59], spread)
    new_first_ref[...] = jnp.where(cleared, 0.0, first)
    new_second_ref[...] = jnp.where(cleared, 0.0, second)


def call(kernel, shapes, ins, scratch=()):
    spec = {
        "v": pl.BlockSpec(memory_space=pltpu.VMEM),
        "s": pl.BlockSpec(memory_space=pltpu.SMEM),
        "h": pl.BlockSpec(memory_space=pltpu.HBM),
    }
    out_shape = [jax.ShapeDtypeStruct(shape, dtype) for shape, dtype in shapes]
    return pl.pallas_call(
        kernel,
        out_shape=out_shape,
        in_specs=[spec[kind] for kind in ins],
        out_specs=[spec["v"]] * len(out_shape),
        scratch_shapes=list(scratch),
        compiler_params=pltpu.CompilerParams(vmem_limit_bytes=VMEM_LIMIT),
    )


def in_hbm(array):
    return pltpu.with_memory_space_constraint(array, pltpu.HBM)


def exchange(block):
    parts = block.reshape(PEERS, 1, -1)
    got = lax.all_to_all(parts, "gauss", split_axis=0, concat_axis=0, tiled=True)
    return got.reshape(block.shape)


def shards(
    params,
    first_moment,
    second_moment,
    cameras,
    target,
    tile_index,
    tile_lists,
    send_slots,
    reloc_send,
    reloc_recv,
):
    columns = ((1, LOCAL), I32)
    whole = ((59, LOCAL), F32)
    outgoing, order, entries, corners, wanted, counts, landing, shown = call(
        send_kernel,
        [
            ((3 * PEERS, 128), F32),
            columns,
            columns,
            ((2 * TILES, 256), F32),
            ((3, TILES, 256), F32),
            ((1, LOCAL), F32),
            ((1, 128), I32),
            ((1, 128), F32),
        ],
        "hhhhhhhhhh",
        [
            pltpu.VMEM((59, LOCAL), F32),
            pltpu.VMEM((59, LOCAL), F32),
            pltpu.VMEM((59, LOCAL), F32),
            pltpu.VMEM((8, 128), I32),
            pltpu.VMEM((1, 128), I32),
            pltpu.VMEM((1, 128), I32),
            pltpu.SMEM((1, 16), F32),
            pltpu.VMEM((1, TILES, 256), I32),
            pltpu.SMEM((1, TILES), I32),
            pltpu.SemaphoreType.DMA((10,)),
        ],
    )(
        in_hbm(params),
        in_hbm(first_moment),
        in_hbm(second_moment),
        in_hbm(send_slots.reshape(8, 128)),
        in_hbm(reloc_send),
        in_hbm(reloc_recv),
        in_hbm(cameras),
        in_hbm(tile_lists),
        in_hbm(tile_index),
        in_hbm(jnp.transpose(target[0], (1, 0, 2))),
    )
    received = exchange(outgoing)
    back = ((BLOCKS * PEERS, 128), F32)
    eight = ((8, LOCAL), F32)
    give, share, given, rest, index, numbers, asked = call(
        render_kernel,
        [
            back,
            ((SHARE, 128), F32),
            eight,
            eight,
            columns,
            ((1, LOCAL), F32),
            ((PEERS, 128), F32),
        ],
        "vvvv",
        [pltpu.VMEM((TILES, 256, 256), F32), pltpu.VMEM((TILES, 256, 256), F32)],
    )(received, entries, corners, wanted)
    sibling = lax.ppermute(give, "gauss", [(i, i ^ 1) for i in range(PEERS)])
    (kept,) = call(keep_kernel, [back], "vvvvv")(given, rest, index, numbers, asked)
    returned = exchange(kept + sibling)
    (own,) = call(owner_kernel, [((SENT, 128), F32)], "vvvv")(returned, order, shown, share)
    others = [
        lax.ppermute(own, "view", [(i, i ^ flip) for i in range(VIEWS)]) for flip in (1, 2, 3)
    ]
    tiles = ((57 * 8, 128), F32)
    dense, own_part, last_part = call(early_kernel, [((59 * 8, 128), F32), tiles, tiles], "vvv")(
        params, own, others[2]
    )
    return call(step_kernel, [whole, whole, whole, whole], "vvvvvvvvvvvv")(
        dense, own_part, last_part, params, first_moment, second_moment, own, *others, counts, landing
    )


def solution(mesh):
    in_specs = (
        P(None, "gauss"),
        P(None, "gauss"),
        P(None, "gauss"),
        P("view", None),
        P("view", "gauss", None, None),
        P("view", "gauss"),
        P("view", "gauss", None),
        P("view", "gauss", None),
        P("gauss", None),
        P("gauss", None),
    )
    out_specs = (P(None, "gauss"), P(None, "gauss"), P(None, "gauss"), P(None, "gauss"))
    return jax.shard_map(shards, mesh=mesh, in_specs=in_specs, out_specs=out_specs, check_vma=False)
```
